256 devices in a mesh: row: 4 (over x), col: 64 (over y, z, core).
Axes of the slice: x: 4, y: 4, z: 8, core: 2. Of those that a mesh axis runs over, the one named last changes fastest.
Arguments:
- source: bfloat16 [32768, 128], P(('row', 'col')), may hold values from -6 to 6
- target: bfloat16 [32768, 128], P('col'), may hold values from -6 to 6
- potential: float32 [32768], P('col'), may hold values from -0.3 to 0.3
Outputs:
- source_potential: float32 [32768], P(('row', 'col'))
- target_potential: float32 [32768], P('col')
- mapped: bfloat16 [32768, 128], P(('row', 'col'))
The draws below stay inside these ranges and needn't reach their ends.
All inputs are finite; a program needn't handle non-finite values.
Results may differ from the reference program's by a relative error of at most 0.008.
Values may be sent and summed in bfloat16 or wider, within the bound.
A program may use at most 64 MiB of HBM per device.

```python
import math
import jax
import jax.numpy as jnp
from jax import lax

D = 128
NS = 32768
NT = 32768


def anchor_rows(key, count, lowest, highest):
    key = jax.random.fold_in(key, 7)
    subkeys = jax.random.split(key, 3)
    strength = jax.random.uniform(subkeys[0], (count, 1), jnp.float32, lowest, highest)
    sign_table = jnp.where(jax.random.bernoulli(subkeys[1], 0.5, (count, D)), 1.0, -1.0)
    spread = jax.random.uniform(subkeys[2], (count, D), jnp.float32, 0.5, 1.0)
    return strength * sign_table * spread


def draw_source(key, part):
    pair_count = NT // 64
    anchors = anchor_rows(key, pair_count, 2.3, 5.5)
    key = jax.random.fold_in(key, 11)
    subkeys = jax.random.split(key, 9)
    values = jax.random.normal(subkeys[1], (NS, D), jnp.float32)
    far_lowest = 1.5
    far_highest = 3.6
    offset_top = 3.2
    values = jnp.clip(values, -6.0, 6.0)
    half_rows = NS // 2
    pair_span = half_rows // pair_count
    pair_starts = jnp.arange(pair_count, dtype=jnp.int32) * half_rows // pair_count
    aligned_rows = 2 * (pair_starts + jax.random.randint(subkeys[2], (pair_count,), 0, pair_span))
    far_count = max(1, NS // 128)
    far_span = half_rows // far_count
    far_starts = jnp.arange(far_count, dtype=jnp.int32) * half_rows // far_count
    far_rows = 2 * (far_starts + jax.random.randint(subkeys[3], (far_count,), 0, far_span)) + 1
    far_strength = jax.random.uniform(subkeys[4], (far_count, 1), jnp.float32, far_lowest, far_highest)
    far_signs = jnp.where(jax.random.bernoulli(subkeys[5], 0.5, (far_count, D)), 1.0, -1.0)
    far_spread = jax.random.uniform(subkeys[6], (far_count, D), jnp.float32, 0.8, 1.0)
    values = values.at[far_rows].set(far_strength * far_signs * far_spread)
    offset_pick = jax.random.uniform(subkeys[7], (pair_count, 1), jnp.float32, 0.0, 1.0)
    offset_scale = jnp.where(offset_pick < 0.3, 0.0, 0.3 + (offset_top - 0.3) * (offset_pick - 0.3) / 0.7)
    offset_noise = jax.random.normal(subkeys[8], (pair_count, D), jnp.float32)
    aligned_values = jnp.clip(anchors + offset_scale * offset_noise, -6.0, 6.0)
    values = values.at[aligned_rows].set(aligned_values)
    return values.astype(jnp.bfloat16)


def draw_target(key, part):
    pair_count = NT // 64
    anchors = anchor_rows(key, pair_count, 2.3, 5.5)
    far_lowest = 2.3
    far_highest = 5.5
    key = jax.random.fold_in(key, 13)
    subkeys = jax.random.split(key, 7)
    values = jax.random.normal(subkeys[1], (NT, D), jnp.float32)
    values = jnp.clip(values, -6.0, 6.0)
    slot_offset = jax.random.randint(subkeys[2], (pair_count,), 0, 32)
    block_base = jnp.arange(pair_count, dtype=jnp.int32) * 64
    slot_rows = block_base + slot_offset
    far_rows = block_base + (slot_offset + 16) % 32
    partner = jnp.clip(anchors + 0.28 * jax.random.normal(subkeys[3], (pair_count, D), jnp.float32), -6.0, 6.0)
    far_strength = jax.random.uniform(subkeys[4], (pair_count, 1), jnp.float32, far_lowest, far_highest)
    far_signs = jnp.where(jax.random.bernoulli(subkeys[5], 0.5, (pair_count, D)), 1.0, -1.0)
    far_spread = jax.random.uniform(subkeys[6], (pair_count, D), jnp.float32, 0.5, 1.0)
    values = values.at[far_rows].set(far_strength * far_signs * far_spread)
    values = values.at[slot_rows].set(anchors)
    values = values.at[slot_rows + 32].set(partner)
    return values.astype(jnp.bfloat16)


def level_of(rng, dims, cuts, smallest, high):
    factor_of = 1.0
    for axis_at, shards_of in cuts:
        heights = jax.random.uniform(jax.random.fold_in(jax.random.fold_in(rng, 6), axis_at), (shards_of,), jnp.float32, smallest / len(cuts), high / len(cuts))
        factor_of = factor_of * jnp.repeat(jnp.exp(heights), dims[axis_at] // shards_of).reshape((-1,) + (1,) * (len(dims) - 1 - axis_at))
    return factor_of


def scatter_about(own_key, extent, scale, limit, cuts=(), held_as=jnp.bfloat16):
    entries = jax.random.normal(own_key, extent, jnp.float32) * scale
    if len(cuts) > 0:
        entries = level_of(own_key, extent, cuts, -0.22, 0.18) * entries
    return jnp.clip(entries, min=-limit, max=limit).astype(held_as)


def setup_inputs(seed: int = 0) -> dict:
    keys = jax.random.split(jax.random.key(seed), 4)
    return {
        "source": draw_source(jax.random.fold_in(keys[3], 71), 0),
        "target": draw_target(jax.random.fold_in(keys[3], 71), 0),
        "potential": scatter_about(keys[2], (NT,), 0.05, 0.3, ((0, 64),), jnp.float32),
    }


epsilon = 0.02


def cost_tile(block_rows, target, target_sq):
    row_sq = jnp.sum(jnp.square(block_rows.astype(jnp.float32)), axis=1)
    inner = jnp.dot(block_rows, target.T, preferred_element_type=jnp.float32)
    return (row_sq[:, None] + target_sq[None, :] - 2.0 * inner) / (2.0 * D)


def reference(source, target, potential):
    block_size = math.gcd(NS, 2048)
    target_sq = jnp.sum(jnp.square(target.astype(jnp.float32)), axis=1)
    blocks = source.reshape(NS // block_size, block_size, D)

    def row_pass(block_rows):
        scores = (potential[None, :] - cost_tile(block_rows, target, target_sq)) / epsilon
        peak = jnp.max(scores, axis=1)
        total = jnp.sum(jnp.exp(scores - peak[:, None]), axis=1)
        return -epsilon * (peak + jnp.log(total)) - epsilon * math.log(NS)

    source_potential = lax.map(row_pass, blocks).reshape(NS)
    f_blocks = source_potential.reshape(NS // block_size, block_size)

    def column_step(carry, items):
        peak, total = carry
        block_rows, f_block = items
        scores = (f_block[:, None] - cost_tile(block_rows, target, target_sq)) / epsilon
        new_peak = jnp.maximum(peak, jnp.max(scores, axis=0))
        total = total * jnp.exp(peak - new_peak) + jnp.sum(jnp.exp(scores - new_peak[None, :]), axis=0)
        return (new_peak, total), None

    start = (jnp.full((NT,), -jnp.inf, jnp.float32), jnp.zeros((NT,), jnp.float32))
    (peak, total), unused = lax.scan(column_step, start, (blocks, f_blocks))
    target_potential = -epsilon * (peak + jnp.log(total)) - epsilon * math.log(NT)

    def bary_pass(items):
        block_rows, f_block = items
        plan = jnp.exp((f_block[:, None] + target_potential[None, :] - cost_tile(block_rows, target, target_sq)) / epsilon)
        denominator = jnp.sum(plan, axis=1)
        numerator = jnp.dot(plan.astype(jnp.bfloat16), target, preferred_element_type=jnp.float32)
        return (numerator / denominator[:, None]).astype(jnp.bfloat16)

    mapped = lax.map(bary_pass, (blocks, f_blocks)).reshape(NS, D)
    return source_potential, target_potential, mapped
```

```python
import functools
import math

import jax
import jax.numpy as jnp
from jax import lax
from jax.experimental import pallas as pl
from jax.experimental.pallas import tpu as pltpu
from jax.sharding import PartitionSpec as P

MESH = pl.DeviceIdType.MESH
EPS = 0.02
LOG2E = 1.0 / math.log(2.0)
F32 = jnp.float32
BF16 = jnp.bfloat16

Y, Z, C = 4, 8, 2
LOW = -1e30
VMEM = 63495680
W, EXTRA = 128, 16


def split2(x):
    hi = x.astype(BF16)
    return hi, (x - hi.astype(F32)).astype(BF16)


def split3(x):
    hi = x.astype(BF16).astype(F32)
    mid = (x - hi).astype(BF16).astype(F32)
    return hi, mid, x - hi - mid


def squares(rows):
    both = jnp.concatenate(split2(jnp.square(rows.astype(F32))), axis=1)
    ones = jnp.ones((8, both.shape[1]), BF16)
    return lax.dot_general(ones, both, (((1,), (1,)), ((), ())), preferred_element_type=F32)[0:1, :]


def kernel(dims, src, tgt, pot, f_out, g_out, map_out, tbuf, abuf, sbuf, pbuf, lhs, rhs, ta, buf_a, buf_b, col_a, col_b, macc, sacc, lrow, lfin,
           mstage, sstage, mcol, lcol, xbuf, zsend, zbuf, wrep, e2, acc, nsend, nrecv, i_sem, a_send, a_recv, t_send, t_recv, s_send, s_recv,
           r_send, r_recv, x_send, x_recv, z_send, z_recv, n_send, n_recv):
    X, Y, Z, C, ns, nt, D, all_s, all_t = dims
    G = Y * C
    Q = nt // W
    CH = Z * W
    SCALE = LOG2E / (D * EPS)
    x = lax.axis_index("row")
    col = lax.axis_index("col")
    y = col // (Z * C)
    z = (col // C) % Z
    c = col % C

    def dev(xx, yy, zz, cc):
        return {"row": xx, "col": (yy * Z + zz) * C + cc}

    def remote(a, b, send, recv, to):
        cp = pltpu.make_async_remote_copy(
            src_ref=a, dst_ref=b, send_sem=send, recv_sem=recv, device_id=to, device_id_type=MESH)
        cp.start()
        return cp

    def lse(items):
        top = functools.reduce(jnp.maximum, items)
        total = functools.reduce(jnp.add, [jnp.exp2((i - top) * SCALE) for i in items])
        return top + jnp.log2(total) * (1.0 / SCALE)

    group = [(dy, dc) for dy in range(Y) for dc in range(C) if (dy, dc) != (0, 0)]

    def group_dev(dy, dc):
        return dev(x, (y + dy) % Y, z, (c + dc) % C)

    place = y * C + c

    barrier = pltpu.get_barrier_semaphore()
    peers = [group_dev(*g) for g in group]
    peers += [dev((x + d) % X, y, z, c) for d in range(1, X)]
    peers += [dev(x, y, (z + d) % Z, c) for d in range(1, Z)]
    for peer in peers:
        pl.semaphore_signal(barrier, inc=1, device_id=peer, device_id_type=MESH)
    fetch = [pltpu.make_async_copy(tgt.at[pl.ds(q * W, W), :], tbuf.at[0, q], i_sem.at[q]) for q in range(Q)]
    fetch.append(pltpu.make_async_copy(pot, pbuf, i_sem.at[Q]))
    fetch.append(pltpu.make_async_copy(src, sbuf.at[place], i_sem.at[Q + 1]))
    for cp in fetch:
        cp.start()
    pl.semaphore_wait(barrier, len(peers))

    s_copies = [remote(src, sbuf.at[place], s_send.at[i], s_recv.at[i], group_dev(*g)) for i, g in enumerate(group)]

    H = Z // 2
    t_copies = {}
    right = dev(x, y, (z + 1) % Z, c)
    left = dev(x, y, (z + Z - 1) % Z, c)

    def to_z(r, j):
        q = (x + j) % Q
        k = r * Q + j
        t_copies[r, j] = remote(
            tgt.at[pl.ds(pl.multiple_of(q * W, W), W), :], tbuf.at[r, q], t_send.at[k], t_recv.at[k],
            dev(x, y, (z + Z - r) % Z, c))

    for d in range(2, H):
        to_z(d, 0)
        to_z(Z - d, 0)
    for j in range(Q):
        to_z(1, j)
        to_z(Z - 1, j)

    def half_way():
        have = jnp.where(c == 0, H + 1, H - 1)
        to = jnp.where(c == 0, (z + 1) % Z, (z + Z - 1) % Z)
        k = H * Q
        t_copies[H, 0] = remote(tbuf.at[have, x], tbuf.at[H, x], t_send.at[k], t_recv.at[k], dev(x, y, to, c))

    def spread(r):
        t_copies[r, 0].wait_recv()
        for d in range(1, X):
            k = r * Q + d
            t_copies[r, d] = remote(tbuf.at[r, x], tbuf.at[r, x], t_send.at[k], t_recv.at[k], dev((x + d) % X, y, z, c))

    for cp in fetch:
        cp.wait()
    own_sq = [squares(tbuf[0, q]) for q in range(Q)]
    offset = jnp.concatenate([pbuf[0:1, q * W:(q + 1) * W] * float(D) - 0.5 * own_sq[q] for q in range(Q)], axis=0)
    abuf[0] = jnp.concatenate(list(split3(offset)) + [jnp.zeros((EXTRA - 3 * Q, W), F32)], axis=0).astype(BF16)
    a_copies = [
        remote(abuf.at[0], abuf.at[r], a_send.at[r - 1], a_recv.at[r - 1], dev(x, y, (z + Z - r) % Z, c)) for r in range(1, Z)]

    rhs[D + EXTRA:2 * D, :] = jnp.zeros((D - EXTRA, Z * nt), BF16)
    macc[...] = jnp.full(macc.shape, LOW, F32)
    sacc[...] = jnp.zeros(sacc.shape, F32)
    lanes = lax.broadcasted_iota(jnp.int32, (ns, D), 1)
    for cp in s_copies:
        cp.wait_recv()
    for p in range(G):
        lhs[p * ns:(p + 1) * ns, 0:D] = sbuf[p]
        lhs[p * ns:(p + 1) * ns, D:2 * D] = jnp.where(lanes < 3, 1.0, 0.0).astype(BF16)

    def take(slot):
        offsets = abuf[slot].astype(F32)
        for q in range(Q):
            at = q * CH + slot * W
            piece = tbuf[slot, q]
            rhs[0:D, at:at + W] = piece.T
            rhs[D:D + EXTRA, at:at + W] = jnp.concatenate(
                [offsets[q + i * Q:q + i * Q + 1, :] for i in range(3)]
                + [jnp.ones((3, W), F32), jnp.zeros((EXTRA - 6, W), F32)], axis=0).astype(BF16)
            ta[at:at + W, 0:D] = piece
            ta[at:at + W, D:2 * D] = jnp.ones((W, D), BF16)

    step = 2 * ns

    def fold(buf, start):
        for i in range(step // 64):
            rows = pl.ds(start + i * 64, 64)
            pieces = [buf[i * 64:(i + 1) * 64, q * W:(q + 1) * W] for q in range(Q)]
            old = macc[rows, :]
            top = functools.reduce(jnp.maximum, pieces, old)
            total = sacc[rows, :] * jnp.exp2((old - top) * SCALE)
            for piece in pieces:
                total = total + jnp.exp2((piece - top) * SCALE)
            macc[rows, :] = top
            sacc[rows, :] = total

    def row_pass(slot):
        @pl.loop(0, G // 4)
        def _(p):
            right_side = jnp.concatenate([rhs[:, q * CH + slot * W:q * CH + (slot + 1) * W] for q in range(Q)], axis=1)
            first = pl.multiple_of(p * 2 * step, 2 * step)
            second = pl.multiple_of(p * 2 * step + step, step)
            buf_a[...] = jnp.dot(lhs[pl.ds(first, step), :], right_side, preferred_element_type=F32)
            buf_b[...] = jnp.dot(lhs[pl.ds(second, step), :], right_side, preferred_element_type=F32)
            fold(buf_a, first)
            fold(buf_b, second)

    def arrive(slot):
        a_copies[slot - 1].wait_recv()
        for j in range(Q):
            if j > 0 or slot in (1, Z - 1):
                t_copies[slot, j].wait_recv()
        take(slot)
        row_pass(slot)

    take(0)
    row_pass(0)
    for d in range(2, H):
        spread(d)
        spread(Z - d)
    half_way()
    arrive(1)
    spread(H)
    arrive(Z - 1)
    for d in range(2, H):
        arrive(d)
        arrive(Z - d)
    arrive(H)

    for p in range(G):
        m = macc[p * ns:(p + 1) * ns, :].T
        s = sacc[p * ns:(p + 1) * ns, :].T
        top = jnp.max(m, axis=0, keepdims=True)
        total = jnp.sum(s * jnp.exp2((m - top) * SCALE), axis=0, keepdims=True)
        lrow[0, p:p + 1, :] = top + jnp.log2(total) * (1.0 / SCALE)
    r_copies = [
        remote(lrow.at[0], lrow.at[i + 1], r_send.at[i], r_recv.at[i], group_dev(*g)) for i, g in enumerate(group)]
    src_sq = squares(sbuf[place])
    for cp in r_copies:
        cp.wait_recv()
    l1 = lse([lrow[i] for i in range(G)])
    lfin[0:G, :] = l1
    for p in range(G):
        parts = [jnp.zeros((3, ns), F32)] + list(split3(-l1[p:p + 1, :])) + [jnp.zeros((D - 6, ns), F32)]
        lhs[p * ns:(p + 1) * ns, D:2 * D] = jnp.concatenate(parts, axis=0).T.astype(BF16)
    f_out[...] = (0.5 * src_sq - lfin[pl.ds(place, 1), :]) * (1.0 / D) - EPS * math.log(all_s)

    def scores(buf, at):
        buf[...] = jnp.dot(lhs[...], rhs[:, pl.ds(pl.multiple_of(at, 2 * W), 2 * W)], preferred_element_type=F32)

    def column(buf, slot, at):
        for i in range(2):
            wide = slice(i * W, (i + 1) * W)
            top = buf[0:64, wide]
            for j in range(1, G * ns // 64):
                top = jnp.maximum(top, buf[j * 64:(j + 1) * 64, wide])
            top = jnp.max(top, axis=0, keepdims=True)
            total = jnp.zeros((64, W), F32)
            for j in range(G * ns // 64):
                e = jnp.exp2((buf[j * 64:(j + 1) * 64, wide] - top) * SCALE)
                total = total + e
                e2[j * 64:(j + 1) * 64, pl.ds(pl.multiple_of(at + i * W, W), W)] = e.astype(BF16)
            total = jnp.sum(total, axis=0, keepdims=True)
            mstage[slot + i] = jnp.broadcast_to(top, (8, W))
            sstage[slot + i] = jnp.broadcast_to(total, (8, W))

    x_copies, z_copies = {}, {}

    def column_chunk(q):
        scores(col_a, q * CH)

        @pl.loop(0, Z // 4)
        def _(t):
            slot = t * 4
            at = q * CH + slot * W
            scores(col_b, at + 2 * W)
            column(col_a, slot, at)
            scores(col_a, jnp.minimum(at + 4 * W, (q + 1) * CH - 2 * W))
            column(col_b, slot + 2, at + 2 * W)

        mcol[q] = jnp.concatenate([mstage[r, 0:1, :] for r in range(Z)], axis=0)
        total = jnp.concatenate([sstage[r, 0:1, :] for r in range(Z)], axis=0)
        lcol[q] = mcol[q] + jnp.log2(total) * (1.0 / SCALE)
        for d in range(1, X):
            k = q * (X - 1) + d - 1
            x_copies[q, d] = remote(lcol.at[q], xbuf.at[k], x_send.at[k], x_recv.at[k], dev((x + d) % X, y, z, c))

    def across_z(q):
        for d in range(1, X):
            x_copies[q, d].wait_recv()
        zsend[q] = lse([lcol[q]] + [xbuf[q * (X - 1) + d - 1] for d in range(1, X)])
        for d in range(1, Z):
            k = q * (Z - 1) + d - 1
            z_copies[q, d] = remote(zsend.at[q], zbuf.at[k], z_send.at[k], z_recv.at[k], dev(x, y, (z + d) % Z, c))

    def weights(q):
        terms = [zsend[q]]
        for d in range(1, Z):
            z_copies[q, d].wait_recv()
            got = zbuf[q * (Z - 1) + d - 1]
            terms.append(jnp.concatenate([got[d:Z, :], got[0:d, :]], axis=0))
        l2 = lse(terms)
        g_out[0:1, q * W:(q + 1) * W] = (0.5 * own_sq[q] - l2[0:1, :]) * (1.0 / D) + EPS * (math.log(all_s) - math.log(all_t))
        w = jnp.exp2((mcol[q] - l2) * SCALE)
        for r in range(Z):
            wrep[q, :, r * W:(r + 1) * W] = jnp.broadcast_to(w[r:r + 1, :], (16, W)).astype(BF16)

    pair = C * ns

    def weighted(q, start):
        plan = e2[pl.ds(start, pair), q * CH:(q + 1) * CH]
        plan = (plan.reshape(pair // 16, 16, CH) * wrep[q][None]).reshape(pair, CH)
        return jnp.dot(plan, ta[q * CH:(q + 1) * CH, :], preferred_element_type=F32)

    def add_chunk(q):
        weights(q)

        @pl.loop(0, Y)
        def _(t):
            start = pl.multiple_of(t * pair, pair)
            got = weighted(q, start)
            acc[pl.ds(start, pair), :] = got if q == 0 else acc[pl.ds(start, pair), :] + got

    for q in range(Q):
        column_chunk(q)
        if q > 0:
            across_z(q - 1)
    add_chunk(0)
    across_z(Q - 1)
    for q in range(1, Q - 1):
        add_chunk(q)
    weights(Q - 1)

    eye = lax.broadcasted_iota(jnp.int32, (ns, W), 0) == lax.broadcasted_iota(jnp.int32, (ns, W), 1)
    n_copies = {}
    own = None
    for dy in sorted(range(1, Y), key=lambda d: -min(d, Y - d)) + [0]:
        start = pl.multiple_of(((y + dy) % Y) * pair, pair)
        acc[pl.ds(start, pair), :] = acc[pl.ds(start, pair), :] + weighted(Q - 1, start)
        for dc in reversed(range(C)):
            rows = pl.ds(pl.multiple_of(start + ((c + dc) % C) * ns, ns), ns)
            num, den = acc[rows, 0:D], acc[rows, D:2 * D]
            den = jnp.sum(jnp.where(eye, den, 0.0), axis=0, keepdims=True)
            if (dy, dc) == (0, 0):
                own = (num, den)
                continue
            i = group.index((dy, dc))
            hi, lo = split2(den)
            nsend[i, 0:ns, :] = num.astype(BF16)
            nsend[i, ns:ns + 16, :] = jnp.concatenate(
                [hi.astype(F32), lo.astype(F32), jnp.zeros((14, W), F32)], axis=0).astype(BF16)
            n_copies[i] = remote(nsend.at[i], nrecv.at[i], n_send.at[i], n_recv.at[i], group_dev(dy, dc))
    for cps in (s_copies, a_copies, t_copies.values(), r_copies, x_copies.values(), z_copies.values()):
        for cp in cps:
            cp.wait_send()
    num, den = own
    for i in n_copies:
        n_copies[i].wait_recv()
        got = nrecv[i].astype(F32)
        num = num + got[0:ns, :]
        den = den + got[ns:ns + 1, :] + got[ns + 1:ns + 2, :]
    den = jnp.broadcast_to(den, (ns, W)).T
    map_out[...] = (num / den).astype(BF16)
    for cp in n_copies.values():
        cp.wait_send()


def local(dims, source, target, potential):
    X, Y, Z, C, ns, nt, D, all_s, all_t = dims
    G = Y * C
    Q = nt // W
    vm = pltpu.VMEM
    dma = pltpu.SemaphoreType.DMA
    f, g, mapped = pl.pallas_call(
        functools.partial(kernel, dims),
        out_shape=(
            jax.ShapeDtypeStruct((1, ns), F32),
            jax.ShapeDtypeStruct((1, nt), F32),
            jax.ShapeDtypeStruct((ns, D), BF16),
        ),
        in_specs=[pl.BlockSpec(memory_space=pl.ANY)] * 3,
        out_specs=(pl.BlockSpec(memory_space=pltpu.VMEM),) * 3,
        scratch_shapes=[
            vm((Z, Q, W, D), BF16),
            vm((Z, EXTRA, W), BF16),
            vm((G, ns, D), BF16),
            vm((1, nt), F32),
            vm((G * ns, 2 * D), BF16),
            vm((2 * D, Z * nt), BF16),
            vm((Z * nt, 2 * D), BF16),
            vm((2 * ns, nt), F32),
            vm((2 * ns, nt), F32),
            vm((G * ns, 2 * W), F32),
            vm((G * ns, 2 * W), F32),
            vm((G * ns, 128), F32),
            vm((G * ns, 128), F32),
            vm((G, G, ns), F32),
            vm((8, ns), F32),
            vm((Z, 8, W), F32),
            vm((Z, 8, W), F32),
            vm((Q, Z, W), F32),
            vm((Q, Z, W), F32),
            vm((Q * (X - 1), Z, W), F32),
            vm((Q, Z, W), F32),
            vm((Q * (Z - 1), Z, W), F32),
            vm((Q, 16, Z * W), BF16),
            vm((G * ns, Z * nt), BF16),
            vm((G * ns, 2 * D), F32),
            vm((G - 1, ns + 16, D), BF16),
            vm((G - 1, ns + 16, D), BF16),
            dma((Q + 2,)),
            dma((Z - 1,)), dma((Z - 1,)),
            dma((Z * Q,)), dma((Z * Q,)),
            dma((G - 1,)), dma((G - 1,)),
            dma((G - 1,)), dma((G - 1,)),
            dma((Q * (X - 1),)), dma((Q * (X - 1),)),
            dma((Q * (Z - 1),)), dma((Q * (Z - 1),)),
            dma((G - 1,)), dma((G - 1,)),
        ],
        compiler_params=pltpu.CompilerParams(
            collective_id=0, has_side_effects=True, vmem_limit_bytes=VMEM),
        cost_estimate=pl.CostEstimate(flops=6 * 10**9, bytes_accessed=10**6, transcendentals=10**7),
    )(source, target, potential.reshape(1, nt))
    return f.reshape(ns), g.reshape(nt), mapped


def solution(mesh, shape=(Y, Z, C)):
    placed = (P(("row", "col"), None), P("col", None), P("col"))

    def whole(source, target, potential):
        rows, cols = mesh.shape["row"], mesh.shape["col"]
        dims = (rows, *shape, source.shape[0] // (rows * cols), target.shape[0] // cols, source.shape[1],
                source.shape[0], target.shape[0])
        return jax.shard_map(
            functools.partial(local, dims),
            mesh=mesh,
            in_specs=placed,
            out_specs=(P(("row", "col")), P("col"), P(("row", "col"), None)),
            check_vma=False,
        )(source, target, potential)

    return whole
```

```python
import functools
import math

import jax
import jax.numpy as jnp
from jax import lax
from jax.experimental import pallas as pl
from jax.experimental.pallas import tpu as pltpu
from jax.sharding import PartitionSpec as P

MESH = pl.DeviceIdType.MESH
EPS = 0.02
LOG2E = 1.0 / math.log(2.0)
F32 = jnp.float32
BF16 = jnp.bfloat16

Y, Z, C = 4, 8, 2
LOW = -1e30
VMEM = 63532032
W, EXTRA = 128, 16


def split2(x):
    hi = x.astype(BF16)
    return hi, (x - hi.astype(F32)).astype(BF16)


def split3(x):
    hi = x.astype(BF16).astype(F32)
    mid = (x - hi).astype(BF16).astype(F32)
    return hi, mid, x - hi - mid


def squares(rows):
    both = jnp.concatenate(split2(jnp.square(rows.astype(F32))), axis=1)
    ones = jnp.ones((8, both.shape[1]), BF16)
    return lax.dot_general(ones, both, (((1,), (1,)), ((), ())), preferred_element_type=F32)[0:1, :]


def kernel(dims, src, tgt, pot, f_out, g_out, map_out, tbuf, abuf, sbuf, pbuf, lhs, rhs, ta, buf_a, buf_b, col_a, col_b, top_a, top_b, macc, sacc, lrow, lfin,
           mstage, sstage, mcol, lcol, xbuf, zsend, zbuf, wrep, e2, acc, nsend, nrecv, i_sem, a_send, a_recv, t_send, t_recv, s_send, s_recv,
           r_send, r_recv, x_send, x_recv, z_send, z_recv, n_send, n_recv):
    X, Y, Z, C, ns, nt, D, all_s, all_t = dims
    G = Y * C
    Q = nt // W
    CH = Z * W
    SCALE = LOG2E / (D * EPS)
    x = lax.axis_index("row")
    col = lax.axis_index("col")
    y = col // (Z * C)
    z = (col // C) % Z
    c = col % C

    def dev(xx, yy, zz, cc):
        return {"row": xx, "col": (yy * Z + zz) * C + cc}

    def remote(a, b, send, recv, to):
        cp = pltpu.make_async_remote_copy(
            src_ref=a, dst_ref=b, send_sem=send, recv_sem=recv, device_id=to, device_id_type=MESH)
        cp.start()
        return cp

    def lse(items):
        top = functools.reduce(jnp.maximum, items)
        total = functools.reduce(jnp.add, [jnp.exp2((i - top) * SCALE) for i in items])
        return top + jnp.log2(total) * (1.0 / SCALE)

    group = [(dy, dc) for dy in range(Y) for dc in range(C) if (dy, dc) != (0, 0)]

    def group_dev(dy, dc):
        return dev(x, (y + dy) % Y, z, (c + dc) % C)

    place = y * C + c

    barrier = pltpu.get_barrier_semaphore()
    peers = [group_dev(*g) for g in group]
    peers += [dev((x + d) % X, y, z, c) for d in range(1, X)]
    peers += [dev(x, y, (z + d) % Z, c) for d in range(1, Z)]
    for peer in peers:
        pl.semaphore_signal(barrier, inc=1, device_id=peer, device_id_type=MESH)
    fetch = [pltpu.make_async_copy(tgt.at[pl.ds(q * W, W), :], tbuf.at[0, pl.ds(q * W, W), :], i_sem.at[q]) for q in range(Q)]
    fetch.append(pltpu.make_async_copy(pot, pbuf, i_sem.at[Q]))
    fetch.append(pltpu.make_async_copy(src, sbuf.at[place], i_sem.at[Q + 1]))
    for cp in fetch:
        cp.start()
    rhs[D + EXTRA:2 * D, :] = jnp.zeros((D - EXTRA, Z * nt), BF16)
    macc[...] = jnp.full(macc.shape, LOW, F32)
    sacc[...] = jnp.zeros(sacc.shape, F32)
    ta[:, D:2 * D] = jnp.ones((Z * nt, D), BF16)
    lanes = lax.broadcasted_iota(jnp.int32, (ns, D), 1)
    for p in range(G):
        lhs[p * ns:(p + 1) * ns, D:2 * D] = jnp.where(lanes < 3, 1.0, 0.0).astype(BF16)
    pl.semaphore_wait(barrier, len(peers))

    H = Z // 2
    half = nt // 2
    t_copies = {}

    def side(d):
        return dev(x, y, (z + d) % Z, c)

    own_piece = pl.ds(pl.multiple_of(x * W, W), W)

    def to_z(r, k, a, b):
        t_copies[r, k] = remote(a, b, t_send.at[r * Q + k], t_recv.at[r * Q + k], side(Z - r))

    for r in (3, Z - 3):
        to_z(r, 0, tgt.at[own_piece, :], tbuf.at[r, own_piece, :])
    for h in range(2):
        rows = pl.ds(h * half, half)
        for r in (1, Z - 1):
            to_z(r, h, tgt.at[rows, :], tbuf.at[r, rows, :])

    def pass_on(r, h):
        t_copies[r, h].wait_recv()
        rows = pl.ds(h * half, half)
        there = 2 if r == 1 else Z - 2
        t_copies[there, h] = remote(
            tbuf.at[r, rows, :], tbuf.at[there, rows, :], t_send.at[there * Q + h], t_recv.at[there * Q + h],
            side(Z - 1 if r == 1 else 1))

    def half_way():
        have = jnp.where(c == 0, Z - 3, 3)
        to = jnp.where(c == 0, (z + 1) % Z, (z + Z - 1) % Z)
        t_copies[H, 0] = remote(
            tbuf.at[have, own_piece, :], tbuf.at[H, own_piece, :], t_send.at[H * Q], t_recv.at[H * Q], dev(x, y, to, c))

    def spread(r):
        t_copies[r, 0].wait_recv()
        for d in range(1, X):
            k = r * Q + d
            t_copies[r, d] = remote(
                tbuf.at[r, own_piece, :], tbuf.at[r, own_piece, :], t_send.at[k], t_recv.at[k], dev((x + d) % X, y, z, c))

    s_copies = [remote(src, sbuf.at[place], s_send.at[i], s_recv.at[i], group_dev(*g)) for i, g in enumerate(group)]

    for cp in fetch:
        cp.wait()
    own_sq = [squares(tbuf[0, q * W:(q + 1) * W, :]) for q in range(Q)]
    offset = jnp.concatenate([pbuf[0:1, q * W:(q + 1) * W] * float(D) - 0.5 * own_sq[q] for q in range(Q)], axis=0)
    abuf[0] = jnp.concatenate(list(split3(offset)) + [jnp.zeros((EXTRA - 3 * Q, W), F32)], axis=0).astype(BF16)
    a_copies = [
        remote(abuf.at[0], abuf.at[r], a_send.at[r - 1], a_recv.at[r - 1], dev(x, y, (z + Z - r) % Z, c)) for r in range(1, Z)]

    spread(3)
    spread(Z - 3)
    half_way()

    for cp in s_copies:
        cp.wait_recv()
    for p in range(G):
        lhs[p * ns:(p + 1) * ns, 0:D] = sbuf[p]

    def take(slot):
        offsets = abuf[slot].astype(F32)
        for q in range(Q):
            at = q * CH + slot * W
            piece = tbuf[slot, q * W:(q + 1) * W, :]
            rhs[0:D, at:at + W] = piece.T
            rhs[D:D + EXTRA, at:at + W] = jnp.concatenate(
                [offsets[q + i * Q:q + i * Q + 1, :] for i in range(3)]
                + [jnp.ones((3, W), F32), jnp.zeros((EXTRA - 6, W), F32)], axis=0).astype(BF16)
            ta[at:at + W, 0:D] = piece

    RC = 64
    per = G * ns // 2 // RC

    def fold(buf, start):
        rows = pl.ds(start, RC)
        pieces = [buf[:, q * W:(q + 1) * W] for q in range(Q)]
        old = macc[rows, :]
        top = functools.reduce(jnp.maximum, pieces, old)
        total = sacc[rows, :] * jnp.exp2((old - top) * SCALE)
        for piece in pieces:
            total = total + jnp.exp2((piece - top) * SCALE)
        macc[rows, :] = top
        sacc[rows, :] = total

    def row_pass(slot):
        @pl.loop(0, 2)
        def _(p):
            right_side = jnp.concatenate([rhs[:, q * CH + slot * W:q * CH + (slot + 1) * W] for q in range(Q)], axis=1)
            start = pl.multiple_of(p * per * RC, per * RC)
            bufs = (buf_a, buf_b)
            for i in range(per + 1):
                if i < per:
                    bufs[i % 2][...] = jnp.dot(lhs[pl.ds(start + i * RC, RC), :], right_side, preferred_element_type=F32)
                if i > 0:
                    fold(bufs[(i - 1) % 2], start + (i - 1) * RC)

    waited = {(1, 0), (1, 1), (Z - 1, 0), (Z - 1, 1), (3, 0), (Z - 3, 0), (H, 0)}

    def arrive(slot):
        a_copies[slot - 1].wait_recv()
        for (r, k), cp in t_copies.items():
            if r == slot and (r, k) not in waited:
                cp.wait_recv()
        take(slot)
        row_pass(slot)

    take(0)
    pass_on(1, 0)
    pass_on(Z - 1, 0)
    row_pass(0)
    spread(H)
    pass_on(1, 1)
    pass_on(Z - 1, 1)
    for slot in (1, Z - 1, 3, Z - 3, 2, Z - 2, H):
        arrive(slot)

    for p in range(G):
        m = macc[p * ns:(p + 1) * ns, :].T
        s = sacc[p * ns:(p + 1) * ns, :].T
        top = jnp.max(m, axis=0, keepdims=True)
        total = jnp.sum(s * jnp.exp2((m - top) * SCALE), axis=0, keepdims=True)
        lrow[0, p:p + 1, :] = top + jnp.log2(total) * (1.0 / SCALE)
    r_copies = [
        remote(lrow.at[0], lrow.at[i + 1], r_send.at[i], r_recv.at[i], group_dev(*g)) for i, g in enumerate(group)]
    src_sq = squares(sbuf[place])
    for cp in r_copies:
        cp.wait_recv()
    l1 = lse([lrow[i] for i in range(G)])
    lfin[0:G, :] = l1
    for p in range(G):
        parts = [jnp.zeros((3, ns), F32)] + list(split3(-l1[p:p + 1, :])) + [jnp.zeros((D - 6, ns), F32)]
        lhs[p * ns:(p + 1) * ns, D:2 * D] = jnp.concatenate(parts, axis=0).T.astype(BF16)
    f_out[...] = (0.5 * src_sq - lfin[pl.ds(place, 1), :]) * (1.0 / D) - EPS * math.log(all_s)

    MC = 128
    chunks = G * ns // MC

    def scores(buf, tops, at):
        right_side = rhs[:, pl.ds(pl.multiple_of(at, 2 * W), 2 * W)]
        top = None
        for i in range(chunks):
            u = jnp.dot(lhs[i * MC:(i + 1) * MC, :], right_side, preferred_element_type=F32)
            buf[i * MC:(i + 1) * MC, :] = u
            part = jnp.max(u.reshape(MC // 8, 8, 2 * W), axis=0)
            top = part if top is None else jnp.maximum(top, part)
            yield
        tops[...] = jnp.broadcast_to(jnp.max(top, axis=0, keepdims=True), (8, 2 * W))
        yield

    def column(buf, tops, slot, at):
        top = tops[...]
        total = jnp.zeros((8, 2 * W), F32)
        for i in range(chunks):
            for j in range(0, MC, 32):
                rows = slice(i * MC + j, i * MC + j + 32)
                e = jnp.exp2((buf[rows, :].reshape(4, 8, 2 * W) - top[None]) * SCALE)
                total = total + jnp.sum(e, axis=0)
                e2[rows, pl.ds(pl.multiple_of(at, 2 * W), 2 * W)] = e.reshape(32, 2 * W).astype(BF16)
            yield
        total = jnp.broadcast_to(jnp.sum(total, axis=0, keepdims=True), (8, 2 * W))
        for i in range(2):
            mstage[slot + i] = top[:, i * W:(i + 1) * W]
            sstage[slot + i] = total[:, i * W:(i + 1) * W]
        yield

    def together(*steps):
        for _ in zip(*steps):
            pass

    x_copies, z_copies = {}, {}

    def column_chunk(q):
        @pl.loop(0, Z // 4)
        def _(t):
            slot = t * 4
            at = q * CH + slot * W
            together(scores(col_b, top_b, at + 2 * W), column(col_a, top_a, slot, at))
            after = at + 4 * W if q < Q - 1 else jnp.minimum(at + 4 * W, Z * nt - 2 * W)
            together(scores(col_a, top_a, after), column(col_b, top_b, slot + 2, at + 2 * W))

        mcol[q] = jnp.concatenate([mstage[r, 0:1, :] for r in range(Z)], axis=0)
        total = jnp.concatenate([sstage[r, 0:1, :] for r in range(Z)], axis=0)
        lcol[q] = mcol[q] + jnp.log2(total) * (1.0 / SCALE)
        for d in range(1, X):
            k = q * (X - 1) + d - 1
            x_copies[q, d] = remote(lcol.at[q], xbuf.at[k], x_send.at[k], x_recv.at[k], dev((x + d) % X, y, z, c))

    def across_z(q):
        for d in range(1, X):
            x_copies[q, d].wait_recv()
        zsend[q] = lse([lcol[q]] + [xbuf[q * (X - 1) + d - 1] for d in range(1, X)])
        for d in range(1, Z):
            k = q * (Z - 1) + d - 1
            z_copies[q, d] = remote(zsend.at[q], zbuf.at[k], z_send.at[k], z_recv.at[k], dev(x, y, (z + d) % Z, c))

    def weights(q):
        terms = [zsend[q]]
        for d in range(1, Z):
            z_copies[q, d].wait_recv()
            got = zbuf[q * (Z - 1) + d - 1]
            terms.append(jnp.concatenate([got[d:Z, :], got[0:d, :]], axis=0))
        l2 = lse(terms)
        g_out[0:1, q * W:(q + 1) * W] = (0.5 * own_sq[q] - l2[0:1, :]) * (1.0 / D) + EPS * (math.log(all_s) - math.log(all_t))
        w = jnp.exp2((mcol[q] - l2) * SCALE)
        for r in range(Z):
            wrep[q, :, r * W:(r + 1) * W] = jnp.broadcast_to(w[r:r + 1, :], (16, W)).astype(BF16)

    pair = C * ns

    KC = CH // 2

    def weighted(q, start, first):
        for i in range(0, pair, MC):
            rows = pl.ds(start + i, MC)
            total = None if first else acc[rows, :]
            for k in range(0, CH, KC):
                plan = e2[rows, q * CH + k:q * CH + k + KC].reshape(MC // 16, 16, KC) * wrep[q, :, k:k + KC][None]
                got = jnp.dot(plan.reshape(MC, KC), ta[q * CH + k:q * CH + k + KC, :], preferred_element_type=F32)
                total = got if total is None else total + got
            acc[rows, :] = total

    def add_chunk(q):
        weights(q)

        @pl.loop(0, Y)
        def _(t):
            weighted(q, pl.multiple_of(t * pair, pair), q == 0)

    together(scores(col_a, top_a, 0))
    for q in range(Q):
        column_chunk(q)
        if q > 0:
            across_z(q - 1)
    add_chunk(0)
    across_z(Q - 1)
    for q in range(1, Q - 1):
        add_chunk(q)
    weights(Q - 1)

    eye = lax.broadcasted_iota(jnp.int32, (ns, W), 0) == lax.broadcasted_iota(jnp.int32, (ns, W), 1)
    n_copies = {}
    own = None
    for dy in sorted(range(1, Y), key=lambda d: -min(d, Y - d)) + [0]:
        start = pl.multiple_of(((y + dy) % Y) * pair, pair)
        weighted(Q - 1, start, False)
        for dc in reversed(range(C)):
            rows = pl.ds(pl.multiple_of(start + ((c + dc) % C) * ns, ns), ns)
            num, den = acc[rows, 0:D], acc[rows, D:2 * D]
            den = jnp.sum(jnp.where(eye, den, 0.0), axis=0, keepdims=True)
            if (dy, dc) == (0, 0):
                own = (num, den)
                continue
            i = group.index((dy, dc))
            hi, lo = split2(den)
            nsend[i, 0:ns, :] = num.astype(BF16)
            nsend[i, ns:ns + 16, :] = jnp.concatenate(
                [hi.astype(F32), lo.astype(F32), jnp.zeros((14, W), F32)], axis=0).astype(BF16)
            n_copies[i] = remote(nsend.at[i], nrecv.at[i], n_send.at[i], n_recv.at[i], group_dev(dy, dc))
    for cps in (s_copies, a_copies, t_copies.values(), r_copies, x_copies.values(), z_copies.values()):
        for cp in cps:
            cp.wait_send()
    num, den = own
    for i in n_copies:
        n_copies[i].wait_recv()
        got = nrecv[i].astype(F32)
        num = num + got[0:ns, :]
        den = den + got[ns:ns + 1, :] + got[ns + 1:ns + 2, :]
    den = jnp.broadcast_to(den, (ns, W)).T
    map_out[...] = (num / den).astype(BF16)
    for cp in n_copies.values():
        cp.wait_send()


def write_out(f, g, mapped, f_out, g_out, map_out, sem):
    copies = [
        pltpu.make_async_copy(a, b, sem.at[i]) for i, (a, b) in enumerate(((f, f_out), (g, g_out), (mapped, map_out)))]
    for cp in copies:
        cp.start()
    for cp in copies:
        cp.wait()


def local(dims, source, target, potential):
    X, Y, Z, C, ns, nt, D, all_s, all_t = dims
    G = Y * C
    Q = nt // W
    vm = pltpu.VMEM
    dma = pltpu.SemaphoreType.DMA
    f, g, mapped = pl.pallas_call(
        functools.partial(kernel, dims),
        out_shape=(
            jax.ShapeDtypeStruct((1, ns), F32),
            jax.ShapeDtypeStruct((1, nt), F32),
            jax.ShapeDtypeStruct((ns, D), BF16),
        ),
        in_specs=[pl.BlockSpec(memory_space=pl.ANY)] * 3,
        out_specs=(pl.BlockSpec(memory_space=pltpu.VMEM),) * 3,
        scratch_shapes=[
            vm((Z, nt, D), BF16),
            vm((Z, EXTRA, W), BF16),
            vm((G, ns, D), BF16),
            vm((1, nt), F32),
            vm((G * ns, 2 * D), BF16),
            vm((2 * D, Z * nt), BF16),
            vm((Z * nt, 2 * D), BF16),
            vm((64, nt), F32),
            vm((64, nt), F32),
            vm((G * ns, 2 * W), F32),
            vm((G * ns, 2 * W), F32),
            vm((8, 2 * W), F32),
            vm((8, 2 * W), F32),
            vm((G * ns, 128), F32),
            vm((G * ns, 128), F32),
            vm((G, G, ns), F32),
            vm((8, ns), F32),
            vm((Z, 8, W), F32),
            vm((Z, 8, W), F32),
            vm((Q, Z, W), F32),
            vm((Q, Z, W), F32),
            vm((Q * (X - 1), Z, W), F32),
            vm((Q, Z, W), F32),
            vm((Q * (Z - 1), Z, W), F32),
            vm((Q, 16, Z * W), BF16),
            vm((G * ns, Z * nt), BF16),
            vm((G * ns, 2 * D), F32),
            vm((G - 1, ns + 16, D), BF16),
            vm((G - 1, ns + 16, D), BF16),
            dma((Q + 2,)),
            dma((Z - 1,)), dma((Z - 1,)),
            dma((Z * Q,)), dma((Z * Q,)),
            dma((G - 1,)), dma((G - 1,)),
            dma((G - 1,)), dma((G - 1,)),
            dma((Q * (X - 1),)), dma((Q * (X - 1),)),
            dma((Q * (Z - 1),)), dma((Q * (Z - 1),)),
            dma((G - 1,)), dma((G - 1,)),
        ],
        compiler_params=pltpu.CompilerParams(
            collective_id=0, has_side_effects=True, vmem_limit_bytes=VMEM),
        cost_estimate=pl.CostEstimate(flops=6 * 10**9, bytes_accessed=10**6, transcendentals=10**7),
    )(source, target, potential.reshape(1, nt))
    f, g, mapped = pl.pallas_call(
        write_out,
        out_shape=(
            jax.ShapeDtypeStruct((1, ns), F32),
            jax.ShapeDtypeStruct((1, nt), F32),
            jax.ShapeDtypeStruct((ns, D), BF16),
        ),
        in_specs=[pl.BlockSpec(memory_space=pl.ANY)] * 3,
        out_specs=(pl.BlockSpec(memory_space=pl.ANY),) * 3,
        scratch_shapes=[dma((3,))],
        compiler_params=pltpu.CompilerParams(vmem_limit_bytes=VMEM),
    )(f, g, mapped)
    return f.reshape(ns), g.reshape(nt), mapped


def solution(mesh, shape=(Y, Z, C)):
    placed = (P(("row", "col"), None), P("col", None), P("col"))

    def whole(source, target, potential):
        rows, cols = mesh.shape["row"], mesh.shape["col"]
        dims = (rows, *shape, source.shape[0] // (rows * cols), target.shape[0] // cols, source.shape[1],
                source.shape[0], target.shape[0])
        return jax.shard_map(
            functools.partial(local, dims),
            mesh=mesh,
            in_specs=placed,
            out_specs=(P(("row", "col")), P("col"), P(("row", "col"), None)),
            check_vma=False,
        )(source, target, potential)

    return whole
```

```python
import functools
import math

import jax
import jax.numpy as jnp
from jax import lax
from jax.experimental import pallas as pl
from jax.experimental.pallas import tpu as pltpu
from jax.sharding import PartitionSpec as P

MESH = pl.DeviceIdType.MESH
EPS = 0.02
LOG2E = 1.0 / math.log(2.0)
F32 = jnp.float32
BF16 = jnp.bfloat16

Y, Z, C = 4, 8, 2
LOW = -1e30
VMEM = 63532032
W, EXTRA = 128, 16


def split2(x):
    hi = x.astype(BF16)
    return hi, (x - hi.astype(F32)).astype(BF16)


def split3(x):
    hi = x.astype(BF16).astype(F32)
    mid = (x - hi).astype(BF16).astype(F32)
    return hi, mid, x - hi - mid


def squares(rows):
    both = jnp.concatenate(split2(jnp.square(rows.astype(F32))), axis=1)
    ones = jnp.ones((8, both.shape[1]), BF16)
    return lax.dot_general(ones, both, (((1,), (1,)), ((), ())), preferred_element_type=F32)[0:1, :]


def kernel(dims, src, tgt, pot, f_out, g_out, map_out, tbuf, abuf, sbuf, pbuf, lhs, rhs, ta, uall, lbc, col_a, col_b, top_a, top_b, macc, sacc, lrow, lfin,
           mstage, sstage, mcol, lcol, xbuf, zsend, zbuf, wrep, e2, acc, nsend, nrecv, i_sem, a_send, a_recv, t_send, t_recv, s_send, s_recv,
           r_send, r_recv, x_send, x_recv, z_send, z_recv, n_send, n_recv):
    X, Y, Z, C, ns, nt, D, all_s, all_t = dims
    G = Y * C
    Q = nt // W
    CH = Z * W
    SCALE = LOG2E / (D * EPS)
    x = lax.axis_index("row")
    col = lax.axis_index("col")
    y = col // (Z * C)
    z = (col // C) % Z
    c = col % C

    def dev(xx, yy, zz, cc):
        return {"row": xx, "col": (yy * Z + zz) * C + cc}

    def remote(a, b, send, recv, to):
        cp = pltpu.make_async_remote_copy(
            src_ref=a, dst_ref=b, send_sem=send, recv_sem=recv, device_id=to, device_id_type=MESH)
        cp.start()
        return cp

    def lse(items):
        top = functools.reduce(jnp.maximum, items)
        total = functools.reduce(jnp.add, [jnp.exp2((i - top) * SCALE) for i in items])
        return top + jnp.log2(total) * (1.0 / SCALE)

    group = [(dy, dc) for dy in range(Y) for dc in range(C) if (dy, dc) != (0, 0)]

    def group_dev(dy, dc):
        return dev(x, (y + dy) % Y, z, (c + dc) % C)

    place = y * C + c

    barrier = pltpu.get_barrier_semaphore()
    peers = [group_dev(*g) for g in group]
    peers += [dev((x + d) % X, y, z, c) for d in range(1, X)]
    peers += [dev(x, y, (z + d) % Z, c) for d in range(1, Z)]
    for peer in peers:
        pl.semaphore_signal(barrier, inc=1, device_id=peer, device_id_type=MESH)
    fetch = [pltpu.make_async_copy(tgt.at[pl.ds(q * W, W), :], tbuf.at[0, pl.ds(q * W, W), :], i_sem.at[q]) for q in range(Q)]
    fetch.append(pltpu.make_async_copy(pot, pbuf, i_sem.at[Q]))
    fetch.append(pltpu.make_async_copy(src, sbuf.at[place], i_sem.at[Q + 1]))
    for cp in fetch:
        cp.start()
    rhs[D + EXTRA:2 * D, :] = jnp.zeros((D - EXTRA, Z * nt), BF16)
    macc[...] = jnp.full(macc.shape, LOW, F32)
    sacc[...] = jnp.zeros(sacc.shape, F32)
    ta[:, D:2 * D] = jnp.ones((Z * nt, D), BF16)
    lanes = lax.broadcasted_iota(jnp.int32, (ns, D), 1)
    for p in range(G):
        lhs[p * ns:(p + 1) * ns, D:2 * D] = jnp.where(lanes < 3, 1.0, 0.0).astype(BF16)
    pl.semaphore_wait(barrier, len(peers))

    H = Z // 2
    half = nt // 2
    t_copies = {}

    def side(d):
        return dev(x, y, (z + d) % Z, c)

    own_piece = pl.ds(pl.multiple_of(x * W, W), W)

    def to_z(r, k, a, b):
        t_copies[r, k] = remote(a, b, t_send.at[r * Q + k], t_recv.at[r * Q + k], side(Z - r))

    for r in (3, Z - 3):
        to_z(r, 0, tgt.at[own_piece, :], tbuf.at[r, own_piece, :])
    for h in range(2):
        rows = pl.ds(h * half, half)
        for r in (1, Z - 1):
            to_z(r, h, tgt.at[rows, :], tbuf.at[r, rows, :])

    def pass_on(r, h):
        t_copies[r, h].wait_recv()
        rows = pl.ds(h * half, half)
        there = 2 if r == 1 else Z - 2
        t_copies[there, h] = remote(
            tbuf.at[r, rows, :], tbuf.at[there, rows, :], t_send.at[there * Q + h], t_recv.at[there * Q + h],
            side(Z - 1 if r == 1 else 1))

    def half_way():
        have = jnp.where(c == 0, Z - 3, 3)
        to = jnp.where(c == 0, (z + 1) % Z, (z + Z - 1) % Z)
        t_copies[H, 0] = remote(
            tbuf.at[have, own_piece, :], tbuf.at[H, own_piece, :], t_send.at[H * Q], t_recv.at[H * Q], dev(x, y, to, c))

    def spread(r):
        t_copies[r, 0].wait_recv()
        for d in range(1, X):
            k = r * Q + d
            t_copies[r, d] = remote(
                tbuf.at[r, own_piece, :], tbuf.at[r, own_piece, :], t_send.at[k], t_recv.at[k], dev((x + d) % X, y, z, c))

    s_copies = [remote(src, sbuf.at[place], s_send.at[i], s_recv.at[i], group_dev(*g)) for i, g in enumerate(group)]

    for cp in fetch:
        cp.wait()
    own_sq = [squares(tbuf[0, q * W:(q + 1) * W, :]) for q in range(Q)]
    offset = jnp.concatenate([pbuf[0:1, q * W:(q + 1) * W] * float(D) - 0.5 * own_sq[q] for q in range(Q)], axis=0)
    abuf[0] = jnp.concatenate(list(split3(offset)) + [jnp.zeros((EXTRA - 3 * Q, W), F32)], axis=0).astype(BF16)
    a_copies = [
        remote(abuf.at[0], abuf.at[r], a_send.at[r - 1], a_recv.at[r - 1], dev(x, y, (z + Z - r) % Z, c)) for r in range(1, Z)]

    spread(3)
    spread(Z - 3)
    half_way()

    for cp in s_copies:
        cp.wait_recv()
    for p in range(G):
        lhs[p * ns:(p + 1) * ns, 0:D] = sbuf[p]

    def take(slot):
        offsets = abuf[slot].astype(F32)
        for q in range(Q):
            at = q * CH + slot * W
            cols = slice(slot * nt + q * W, slot * nt + (q + 1) * W)
            piece = tbuf[slot, q * W:(q + 1) * W, :]
            rhs[0:D, cols] = piece.T
            rhs[D:D + EXTRA, cols] = jnp.concatenate(
                [offsets[q + i * Q:q + i * Q + 1, :] for i in range(3)] + [jnp.zeros((EXTRA - 3, W), F32)],
                axis=0).astype(BF16)
            ta[at:at + W, 0:D] = piece

    RC = 64
    per = G * ns // 2 // RC

    def fold(u, rows):
        pieces = [u[:, q * W:(q + 1) * W] for q in range(Q)]
        old = macc[rows, :]
        top = functools.reduce(jnp.maximum, pieces, old)
        total = sacc[rows, :] * jnp.exp2((old - top) * SCALE)
        for piece in pieces:
            total = total + jnp.exp2((piece - top) * SCALE)
        macc[rows, :] = top
        sacc[rows, :] = total

    def row_pass(slot):
        @pl.loop(0, 2)
        def _(p):
            cols = slice(slot * nt, (slot + 1) * nt)
            start = pl.multiple_of(p * per * RC, per * RC)
            for i in range(per):
                rows = pl.ds(start + i * RC, RC)
                u = jnp.dot(lhs[rows, :], rhs[:, cols], preferred_element_type=F32)
                uall[rows, cols] = u
                fold(u, rows)

    waited = {(1, 0), (1, 1), (Z - 1, 0), (Z - 1, 1), (3, 0), (Z - 3, 0), (H, 0)}

    def arrive(slot):
        a_copies[slot - 1].wait_recv()
        for (r, k), cp in t_copies.items():
            if r == slot and (r, k) not in waited:
                cp.wait_recv()
        take(slot)
        row_pass(slot)

    take(0)
    pass_on(1, 0)
    pass_on(Z - 1, 0)
    row_pass(0)
    spread(H)
    pass_on(1, 1)
    pass_on(Z - 1, 1)
    for slot in (1, Z - 1, 3, Z - 3, 2, Z - 2, H):
        arrive(slot)

    for p in range(G):
        m = macc[p * ns:(p + 1) * ns, :].T
        s = sacc[p * ns:(p + 1) * ns, :].T
        top = jnp.max(m, axis=0, keepdims=True)
        total = jnp.sum(s * jnp.exp2((m - top) * SCALE), axis=0, keepdims=True)
        lrow[0, p:p + 1, :] = top + jnp.log2(total) * (1.0 / SCALE)
    r_copies = [
        remote(lrow.at[0], lrow.at[i + 1], r_send.at[i], r_recv.at[i], group_dev(*g)) for i, g in enumerate(group)]
    src_sq = squares(sbuf[place])
    for cp in r_copies:
        cp.wait_recv()
    l1 = lse([lrow[i] for i in range(G)])
    lfin[0:G, :] = l1
    for p in range(G):
        lbc[p * ns:(p + 1) * ns, :] = jnp.broadcast_to(l1[p:p + 1, :], (ns, W)).T
    f_out[...] = (0.5 * src_sq - lfin[pl.ds(place, 1), :]) * (1.0 / D) - EPS * math.log(all_s)

    MC = 128
    chunks = G * ns // MC

    def scores(buf, tops, q, slot):
        cols = [pl.ds(pl.multiple_of((slot + i) * nt + q * W, W), W) for i in range(2)]
        top = None
        for i in range(chunks):
            for j in range(0, MC, 32):
                rows = slice(i * MC + j, i * MC + j + 32)
                less = lbc[rows, :]
                u = jnp.concatenate([uall[rows, col] - less for col in cols], axis=1)
                buf[rows, :] = u
                part = jnp.max(u.reshape(4, 8, 2 * W), axis=0)
                top = part if top is None else jnp.maximum(top, part)
            yield
        tops[...] = jnp.broadcast_to(jnp.max(top, axis=0, keepdims=True), (8, 2 * W))
        yield

    def column(buf, tops, slot, at):
        top = tops[...]
        total = jnp.zeros((8, 2 * W), F32)
        for i in range(chunks):
            for j in range(0, MC, 32):
                rows = slice(i * MC + j, i * MC + j + 32)
                e = jnp.exp2((buf[rows, :].reshape(4, 8, 2 * W) - top[None]) * SCALE)
                total = total + jnp.sum(e, axis=0)
                e2[rows, pl.ds(pl.multiple_of(at, 2 * W), 2 * W)] = e.reshape(32, 2 * W).astype(BF16)
            yield
        total = jnp.broadcast_to(jnp.sum(total, axis=0, keepdims=True), (8, 2 * W))
        for i in range(2):
            mstage[slot + i] = top[:, i * W:(i + 1) * W]
            sstage[slot + i] = total[:, i * W:(i + 1) * W]
        yield

    def together(*steps):
        for _ in zip(*steps):
            pass

    x_copies, z_copies = {}, {}

    def column_chunk(q):
        @pl.loop(0, Z // 4)
        def _(t):
            slot = t * 4
            at = q * CH + slot * W
            together(scores(col_b, top_b, q, slot + 2), column(col_a, top_a, slot, at))
            ahead = jnp.where(t < Z // 4 - 1, slot + 4, 0)
            together(scores(col_a, top_a, jnp.minimum(q + (t + 1) // (Z // 4), Q - 1), ahead),
                     column(col_b, top_b, slot + 2, at + 2 * W))

        mcol[q] = jnp.concatenate([mstage[r, 0:1, :] for r in range(Z)], axis=0)
        total = jnp.concatenate([sstage[r, 0:1, :] for r in range(Z)], axis=0)
        lcol[q] = mcol[q] + jnp.log2(total) * (1.0 / SCALE)
        for d in range(1, X):
            k = q * (X - 1) + d - 1
            x_copies[q, d] = remote(lcol.at[q], xbuf.at[k], x_send.at[k], x_recv.at[k], dev((x + d) % X, y, z, c))

    def across_z(q):
        for d in range(1, X):
            x_copies[q, d].wait_recv()
        zsend[q] = lse([lcol[q]] + [xbuf[q * (X - 1) + d - 1] for d in range(1, X)])
        for d in range(1, Z):
            k = q * (Z - 1) + d - 1
            z_copies[q, d] = remote(zsend.at[q], zbuf.at[k], z_send.at[k], z_recv.at[k], dev(x, y, (z + d) % Z, c))

    def weights(q):
        terms = [zsend[q]]
        for d in range(1, Z):
            z_copies[q, d].wait_recv()
            got = zbuf[q * (Z - 1) + d - 1]
            terms.append(jnp.concatenate([got[d:Z, :], got[0:d, :]], axis=0))
        l2 = lse(terms)
        g_out[0:1, q * W:(q + 1) * W] = pbuf[0:1, q * W:(q + 1) * W] - l2[0:1, :] * (1.0 / D) + EPS * (
            math.log(all_s) - math.log(all_t))
        w = jnp.exp2((mcol[q] - l2) * SCALE)
        for r in range(Z):
            wrep[q, :, r * W:(r + 1) * W] = jnp.broadcast_to(w[r:r + 1, :], (16, W)).astype(BF16)

    pair = C * ns

    KC = CH // 2

    def weighted(q, start, first):
        for i in range(0, pair, MC):
            rows = pl.ds(start + i, MC)
            total = None if first else acc[rows, :]
            for k in range(0, CH, KC):
                plan = e2[rows, q * CH + k:q * CH + k + KC].reshape(MC // 16, 16, KC) * wrep[q, :, k:k + KC][None]
                got = jnp.dot(plan.reshape(MC, KC), ta[q * CH + k:q * CH + k + KC, :], preferred_element_type=F32)
                total = got if total is None else total + got
            acc[rows, :] = total

    def add_chunk(q):
        weights(q)

        @pl.loop(0, Y)
        def _(t):
            weighted(q, pl.multiple_of(t * pair, pair), q == 0)

    together(scores(col_a, top_a, 0, 0))
    for q in range(Q):
        column_chunk(q)
        if q > 0:
            across_z(q - 1)
    add_chunk(0)
    across_z(Q - 1)
    for q in range(1, Q - 1):
        add_chunk(q)
    weights(Q - 1)

    eye = lax.broadcasted_iota(jnp.int32, (ns, W), 0) == lax.broadcasted_iota(jnp.int32, (ns, W), 1)
    n_copies = {}
    own = None
    for dy in sorted(range(1, Y), key=lambda d: -min(d, Y - d)) + [0]:
        start = pl.multiple_of(((y + dy) % Y) * pair, pair)
        weighted(Q - 1, start, False)
        for dc in reversed(range(C)):
            rows = pl.ds(pl.multiple_of(start + ((c + dc) % C) * ns, ns), ns)
            num, den = acc[rows, 0:D], acc[rows, D:2 * D]
            den = jnp.sum(jnp.where(eye, den, 0.0), axis=0, keepdims=True)
            if (dy, dc) == (0, 0):
                own = (num, den)
                continue
            i = group.index((dy, dc))
            hi, lo = split2(den)
            nsend[i, 0:ns, :] = num.astype(BF16)
            nsend[i, ns:ns + 16, :] = jnp.concatenate(
                [hi.astype(F32), lo.astype(F32), jnp.zeros((14, W), F32)], axis=0).astype(BF16)
            n_copies[i] = remote(nsend.at[i], nrecv.at[i], n_send.at[i], n_recv.at[i], group_dev(dy, dc))
    for cps in (s_copies, a_copies, t_copies.values(), r_copies, x_copies.values(), z_copies.values()):
        for cp in cps:
            cp.wait_send()
    num, den = own
    for i in n_copies:
        n_copies[i].wait_recv()
        got = nrecv[i].astype(F32)
        num = num + got[0:ns, :]
        den = den + got[ns:ns + 1, :] + got[ns + 1:ns + 2, :]
    den = jnp.broadcast_to(den, (ns, W)).T
    map_out[...] = (num / den).astype(BF16)
    for cp in n_copies.values():
        cp.wait_send()


def write_out(f, g, mapped, f_out, g_out, map_out, sem):
    copies = [
        pltpu.make_async_copy(a, b, sem.at[i]) for i, (a, b) in enumerate(((f, f_out), (g, g_out), (mapped, map_out)))]
    for cp in copies:
        cp.start()
    for cp in copies:
        cp.wait()


def local(dims, source, target, potential):
    X, Y, Z, C, ns, nt, D, all_s, all_t = dims
    G = Y * C
    Q = nt // W
    vm = pltpu.VMEM
    dma = pltpu.SemaphoreType.DMA
    f, g, mapped = pl.pallas_call(
        functools.partial(kernel, dims),
        out_shape=(
            jax.ShapeDtypeStruct((1, ns), F32),
            jax.ShapeDtypeStruct((1, nt), F32),
            jax.ShapeDtypeStruct((ns, D), BF16),
        ),
        in_specs=[pl.BlockSpec(memory_space=pl.ANY)] * 3,
        out_specs=(pl.BlockSpec(memory_space=pltpu.VMEM),) * 3,
        scratch_shapes=[
            vm((Z, nt, D), BF16),
            vm((Z, EXTRA, W), BF16),
            vm((G, ns, D), BF16),
            vm((1, nt), F32),
            vm((G * ns, 2 * D), BF16),
            vm((2 * D, Z * nt), BF16),
            vm((Z * nt, 2 * D), BF16),
            vm((G * ns, Z * nt), F32),
            vm((G * ns, W), F32),
            vm((G * ns, 2 * W), F32),
            vm((G * ns, 2 * W), F32),
            vm((8, 2 * W), F32),
            vm((8, 2 * W), F32),
            vm((G * ns, 128), F32),
            vm((G * ns, 128), F32),
            vm((G, G, ns), F32),
            vm((8, ns), F32),
            vm((Z, 8, W), F32),
            vm((Z, 8, W), F32),
            vm((Q, Z, W), F32),
            vm((Q, Z, W), F32),
            vm((Q * (X - 1), Z, W), F32),
            vm((Q, Z, W), F32),
            vm((Q * (Z - 1), Z, W), F32),
            vm((Q, 16, Z * W), BF16),
            vm((G * ns, Z * nt), BF16),
            vm((G * ns, 2 * D), F32),
            vm((G - 1, ns + 16, D), BF16),
            vm((G - 1, ns + 16, D), BF16),
            dma((Q + 2,)),
            dma((Z - 1,)), dma((Z - 1,)),
            dma((Z * Q,)), dma((Z * Q,)),
            dma((G - 1,)), dma((G - 1,)),
            dma((G - 1,)), dma((G - 1,)),
            dma((Q * (X - 1),)), dma((Q * (X - 1),)),
            dma((Q * (Z - 1),)), dma((Q * (Z - 1),)),
            dma((G - 1,)), dma((G - 1,)),
        ],
        compiler_params=pltpu.CompilerParams(
            collective_id=0, has_side_effects=True, vmem_limit_bytes=VMEM),
        cost_estimate=pl.CostEstimate(flops=6 * 10**9, bytes_accessed=10**6, transcendentals=10**7),
    )(source, target, potential.reshape(1, nt))
    f, g, mapped = pl.pallas_call(
        write_out,
        out_shape=(
            jax.ShapeDtypeStruct((1, ns), F32),
            jax.ShapeDtypeStruct((1, nt), F32),
            jax.ShapeDtypeStruct((ns, D), BF16),
        ),
        in_specs=[pl.BlockSpec(memory_space=pl.ANY)] * 3,
        out_specs=(pl.BlockSpec(memory_space=pl.ANY),) * 3,
        scratch_shapes=[dma((3,))],
        compiler_params=pltpu.CompilerParams(vmem_limit_bytes=VMEM),
    )(f, g, mapped)
    return f.reshape(ns), g.reshape(nt), mapped


def solution(mesh, shape=(Y, Z, C)):
    placed = (P(("row", "col"), None), P("col", None), P("col"))

    def whole(source, target, potential):
        rows, cols = mesh.shape["row"], mesh.shape["col"]
        dims = (rows, *shape, source.shape[0] // (rows * cols), target.shape[0] // cols, source.shape[1],
                source.shape[0], target.shape[0])
        return jax.shard_map(
            functools.partial(local, dims),
            mesh=mesh,
            in_specs=placed,
            out_specs=(P(("row", "col")), P("col"), P(("row", "col"), None)),
            check_vma=False,
        )(source, target, potential)

    return whole
```

```python
import functools
import math

import jax
import jax.numpy as jnp
from jax import lax
from jax.experimental import pallas as pl
from jax.experimental.pallas import tpu as pltpu
from jax.sharding import PartitionSpec as P

MESH = pl.DeviceIdType.MESH
EPS = 0.02
LOG2E = 1.0 / math.log(2.0)
F32 = jnp.float32
BF16 = jnp.bfloat16

Y, Z, C = 4, 8, 2
LOW = -1e30
VMEM = 63532032
W, EXTRA = 128, 16


def split2(x):
    hi = x.astype(BF16)
    return hi, (x - hi.astype(F32)).astype(BF16)


def split3(x):
    hi = x.astype(BF16).astype(F32)
    mid = (x - hi).astype(BF16).astype(F32)
    return hi, mid, x - hi - mid


def squares(rows):
    both = jnp.concatenate(split2(jnp.square(rows.astype(F32))), axis=1)
    ones = jnp.ones((8, both.shape[1]), BF16)
    return lax.dot_general(ones, both, (((1,), (1,)), ((), ())), preferred_element_type=F32)[0:1, :]


def kernel(dims, src, tgt, pot, f_out, g_out, map_out, tbuf, abuf, sbuf, pbuf, lhs, rhs, ta, uall, lbc, col_a, col_b, top_a, top_b, macc, sacc, lrow, lfin,
           mstage, sstage, mcol, lcol, xbuf, zsend, zbuf, wrep, e2, acc, plan, nsend, nrecv, i_sem, a_send, a_recv, t_send, t_recv, s_send, s_recv,
           r_send, r_recv, x_send, x_recv, z_send, z_recv, n_send, n_recv):
    X, Y, Z, C, ns, nt, D, all_s, all_t = dims
    G = Y * C
    Q = nt // W
    CH = Z * W
    SCALE = LOG2E / (D * EPS)
    x = lax.axis_index("row")
    col = lax.axis_index("col")
    y = col // (Z * C)
    z = (col // C) % Z
    c = col % C

    def dev(xx, yy, zz, cc):
        return {"row": xx, "col": (yy * Z + zz) * C + cc}

    def remote(a, b, send, recv, to):
        cp = pltpu.make_async_remote_copy(
            src_ref=a, dst_ref=b, send_sem=send, recv_sem=recv, device_id=to, device_id_type=MESH)
        cp.start()
        return cp

    def lse(items):
        top = functools.reduce(jnp.maximum, items)
        total = functools.reduce(jnp.add, [jnp.exp2((i - top) * SCALE) for i in items])
        return top + jnp.log2(total) * (1.0 / SCALE)

    group = [(dy, dc) for dy in range(Y) for dc in range(C) if (dy, dc) != (0, 0)]

    def group_dev(dy, dc):
        return dev(x, (y + dy) % Y, z, (c + dc) % C)

    place = y * C + c

    barrier = pltpu.get_barrier_semaphore()
    peers = [group_dev(*g) for g in group]
    peers += [dev((x + d) % X, y, z, c) for d in range(1, X)]
    peers += [dev(x, y, (z + d) % Z, c) for d in range(1, Z)]
    for peer in peers:
        pl.semaphore_signal(barrier, inc=1, device_id=peer, device_id_type=MESH)
    fetch = [pltpu.make_async_copy(tgt.at[pl.ds(q * W, W), :], tbuf.at[0, pl.ds(q * W, W), :], i_sem.at[q]) for q in range(Q)]
    fetch.append(pltpu.make_async_copy(pot, pbuf, i_sem.at[Q]))
    fetch.append(pltpu.make_async_copy(src, sbuf.at[place], i_sem.at[Q + 1]))
    for cp in fetch:
        cp.start()
    rhs[D + EXTRA:2 * D, :] = jnp.zeros((D - EXTRA, Z * nt), BF16)
    macc[...] = jnp.full(macc.shape, LOW, F32)
    sacc[...] = jnp.zeros(sacc.shape, F32)
    ta[:, D:2 * D] = jnp.ones((Z * nt, D), BF16)
    lanes = lax.broadcasted_iota(jnp.int32, (ns, D), 1)
    for p in range(G):
        lhs[p * ns:(p + 1) * ns, D:2 * D] = jnp.where(lanes < 3, 1.0, 0.0).astype(BF16)
    pl.semaphore_wait(barrier, len(peers))

    H = Z // 2
    half = nt // 2
    t_copies = {}

    def side(d):
        return dev(x, y, (z + d) % Z, c)

    own_piece = pl.ds(pl.multiple_of(x * W, W), W)

    def to_z(r, k, a, b):
        t_copies[r, k] = remote(a, b, t_send.at[r * Q + k], t_recv.at[r * Q + k], side(Z - r))

    for r in (3, Z - 3):
        to_z(r, 0, tgt.at[own_piece, :], tbuf.at[r, own_piece, :])
    for h in range(2):
        rows = pl.ds(h * half, half)
        for r in (1, Z - 1):
            to_z(r, h, tgt.at[rows, :], tbuf.at[r, rows, :])

    def pass_on(r, h):
        t_copies[r, h].wait_recv()
        rows = pl.ds(h * half, half)
        there = 2 if r == 1 else Z - 2
        t_copies[there, h] = remote(
            tbuf.at[r, rows, :], tbuf.at[there, rows, :], t_send.at[there * Q + h], t_recv.at[there * Q + h],
            side(Z - 1 if r == 1 else 1))

    def half_way():
        have = jnp.where(c == 0, Z - 3, 3)
        to = jnp.where(c == 0, (z + 1) % Z, (z + Z - 1) % Z)
        t_copies[H, 0] = remote(
            tbuf.at[have, own_piece, :], tbuf.at[H, own_piece, :], t_send.at[H * Q], t_recv.at[H * Q], dev(x, y, to, c))

    def spread(r):
        t_copies[r, 0].wait_recv()
        for d in range(1, X):
            k = r * Q + d
            t_copies[r, d] = remote(
                tbuf.at[r, own_piece, :], tbuf.at[r, own_piece, :], t_send.at[k], t_recv.at[k], dev((x + d) % X, y, z, c))

    s_copies = [remote(src, sbuf.at[place], s_send.at[i], s_recv.at[i], group_dev(*g)) for i, g in enumerate(group)]

    for cp in fetch:
        cp.wait()
    own_sq = [squares(tbuf[0, q * W:(q + 1) * W, :]) for q in range(Q)]
    offset = jnp.concatenate([pbuf[0:1, q * W:(q + 1) * W] * float(D) - 0.5 * own_sq[q] for q in range(Q)], axis=0)
    abuf[0] = jnp.concatenate(list(split3(offset)) + [jnp.zeros((EXTRA - 3 * Q, W), F32)], axis=0).astype(BF16)
    a_copies = [
        remote(abuf.at[0], abuf.at[r], a_send.at[r - 1], a_recv.at[r - 1], dev(x, y, (z + Z - r) % Z, c)) for r in range(1, Z)]

    spread(3)
    spread(Z - 3)
    half_way()

    for cp in s_copies:
        cp.wait_recv()
    for p in range(G):
        lhs[p * ns:(p + 1) * ns, 0:D] = sbuf[p]

    def take(slot):
        offsets = abuf[slot].astype(F32)
        for q in range(Q):
            at = q * CH + slot * W
            cols = slice(slot * nt + q * W, slot * nt + (q + 1) * W)
            piece = tbuf[slot, q * W:(q + 1) * W, :]
            rhs[0:D, cols] = piece.T
            rhs[D:D + EXTRA, cols] = jnp.concatenate(
                [offsets[q + i * Q:q + i * Q + 1, :] for i in range(3)] + [jnp.zeros((EXTRA - 3, W), F32)],
                axis=0).astype(BF16)
            ta[at:at + W, 0:D] = piece

    RC = 64
    RM = 2 * ns

    def fold(rows, cols):
        pieces = [uall[rows, cols + q * W:cols + (q + 1) * W] for q in range(Q)]
        old = macc[rows, :]
        top = functools.reduce(jnp.maximum, pieces, old)
        total = sacc[rows, :] * jnp.exp2((old - top) * SCALE)
        for piece in pieces:
            total = total + jnp.exp2((piece - top) * SCALE)
        macc[rows, :] = top
        sacc[rows, :] = total

    def row_pass(slot):
        at = slot * nt
        for i in range(0, G * ns + RM, RM):
            if i < G * ns:
                uall[i:i + RM, at:at + nt] = jnp.dot(lhs[i:i + RM, :], rhs[:, at:at + nt], preferred_element_type=F32)
            if i > 0:
                for j in range(i - RM, i, RC):
                    fold(slice(j, j + RC), at)

    waited = {(1, 0), (1, 1), (Z - 1, 0), (Z - 1, 1), (3, 0), (Z - 3, 0), (H, 0)}

    def arrive(slot):
        a_copies[slot - 1].wait_recv()
        for (r, k), cp in t_copies.items():
            if r == slot and (r, k) not in waited:
                cp.wait_recv()
        take(slot)
        row_pass(slot)

    take(0)
    pass_on(1, 0)
    pass_on(Z - 1, 0)
    row_pass(0)
    spread(H)
    pass_on(1, 1)
    pass_on(Z - 1, 1)
    for slot in (1, Z - 1, 3, Z - 3, 2, Z - 2, H):
        arrive(slot)

    for p in range(G):
        m = macc[p * ns:(p + 1) * ns, :].T
        s = sacc[p * ns:(p + 1) * ns, :].T
        top = jnp.max(m, axis=0, keepdims=True)
        total = jnp.sum(s * jnp.exp2((m - top) * SCALE), axis=0, keepdims=True)
        lrow[0, p:p + 1, :] = top + jnp.log2(total) * (1.0 / SCALE)
    r_copies = [
        remote(lrow.at[0], lrow.at[i + 1], r_send.at[i], r_recv.at[i], group_dev(*g)) for i, g in enumerate(group)]
    src_sq = squares(sbuf[place])
    for cp in r_copies:
        cp.wait_recv()
    l1 = lse([lrow[i] for i in range(G)])
    lfin[0:G, :] = l1
    for p in range(G):
        lbc[p * ns:(p + 1) * ns, :] = jnp.broadcast_to(l1[p:p + 1, :], (ns, W)).T
    f_out[...] = (0.5 * src_sq - lfin[pl.ds(place, 1), :]) * (1.0 / D) - EPS * math.log(all_s)

    MC = 128
    chunks = G * ns // MC

    def scores(buf, tops, q, slot):
        cols = [pl.ds(pl.multiple_of((slot + i) * nt + q * W, W), W) for i in range(2)]
        top = None
        for i in range(chunks):
            for j in range(0, MC, 32):
                rows = slice(i * MC + j, i * MC + j + 32)
                less = lbc[rows, :]
                u = jnp.concatenate([uall[rows, col] - less for col in cols], axis=1)
                buf[rows, :] = u
                part = jnp.max(u.reshape(4, 8, 2 * W), axis=0)
                top = part if top is None else jnp.maximum(top, part)
            yield
        tops[...] = jnp.broadcast_to(jnp.max(top, axis=0, keepdims=True), (8, 2 * W))
        yield

    def column(buf, tops, slot, at):
        top = tops[...]
        total = jnp.zeros((8, 2 * W), F32)
        for i in range(chunks):
            for j in range(0, MC, 32):
                rows = slice(i * MC + j, i * MC + j + 32)
                e = jnp.exp2((buf[rows, :].reshape(4, 8, 2 * W) - top[None]) * SCALE)
                total = total + jnp.sum(e, axis=0)
                e2[rows, pl.ds(pl.multiple_of(at, 2 * W), 2 * W)] = e.reshape(32, 2 * W).astype(BF16)
            yield
        total = jnp.broadcast_to(jnp.sum(total, axis=0, keepdims=True), (8, 2 * W))
        for i in range(2):
            mstage[slot + i] = top[:, i * W:(i + 1) * W]
            sstage[slot + i] = total[:, i * W:(i + 1) * W]
        yield

    def together(*steps):
        for _ in zip(*steps):
            pass

    x_copies, z_copies = {}, {}

    def column_chunk(q):
        @pl.loop(0, Z // 4)
        def _(t):
            slot = t * 4
            at = q * CH + slot * W
            together(scores(col_b, top_b, q, slot + 2), column(col_a, top_a, slot, at))
            ahead = jnp.where(t < Z // 4 - 1, slot + 4, 0)
            together(scores(col_a, top_a, jnp.minimum(q + (t + 1) // (Z // 4), Q - 1), ahead),
                     column(col_b, top_b, slot + 2, at + 2 * W))

        mcol[q] = jnp.concatenate([mstage[r, 0:1, :] for r in range(Z)], axis=0)
        total = jnp.concatenate([sstage[r, 0:1, :] for r in range(Z)], axis=0)
        lcol[q] = mcol[q] + jnp.log2(total) * (1.0 / SCALE)
        for d in range(1, X):
            k = q * (X - 1) + d - 1
            x_copies[q, d] = remote(lcol.at[q], xbuf.at[k], x_send.at[k], x_recv.at[k], dev((x + d) % X, y, z, c))

    def across_z(q):
        for d in range(1, X):
            x_copies[q, d].wait_recv()
        zsend[q] = lse([lcol[q]] + [xbuf[q * (X - 1) + d - 1] for d in range(1, X)])
        for d in range(1, Z):
            k = q * (Z - 1) + d - 1
            z_copies[q, d] = remote(zsend.at[q], zbuf.at[k], z_send.at[k], z_recv.at[k], dev(x, y, (z + d) % Z, c))

    def weights(q):
        terms = [zsend[q]]
        for d in range(1, Z):
            z_copies[q, d].wait_recv()
            got = zbuf[q * (Z - 1) + d - 1]
            terms.append(jnp.concatenate([got[d:Z, :], got[0:d, :]], axis=0))
        l2 = lse(terms)
        g_out[0:1, q * W:(q + 1) * W] = pbuf[0:1, q * W:(q + 1) * W] - l2[0:1, :] * (1.0 / D) + EPS * (
            math.log(all_s) - math.log(all_t))
        w = jnp.exp2((mcol[q] - l2) * SCALE)
        for r in range(Z):
            wrep[q, :, r * W:(r + 1) * W] = jnp.broadcast_to(w[r:r + 1, :], (16, W)).astype(BF16)

    pair = C * ns

    def weigh(q, rows):
        for i in range(0, rows.size, 64):
            part = pl.ds(rows.start + i, 64)
            plan[part, :] = (e2[part, q * CH:(q + 1) * CH].reshape(4, 16, CH) * wrep[q][None]).reshape(64, CH)

    def weighted(q, rows):
        got = jnp.dot(plan[rows, :], ta[q * CH:(q + 1) * CH, :], preferred_element_type=F32)
        acc[rows, :] = got if q == 0 else acc[rows, :] + got

    def add_chunk(q):
        weights(q)
        weigh(q, pl.ds(0, G * ns))
        for i in range(2):
            weighted(q, pl.ds(i * (G * ns // 2), G * ns // 2))

    together(scores(col_a, top_a, 0, 0))
    for q in range(Q):
        column_chunk(q)
        if q > 0:
            across_z(q - 1)
    add_chunk(0)
    across_z(Q - 1)
    for q in range(1, Q - 1):
        add_chunk(q)
    weights(Q - 1)

    eye = lax.broadcasted_iota(jnp.int32, (ns, W), 0) == lax.broadcasted_iota(jnp.int32, (ns, W), 1)
    n_copies = {}
    own = None
    for dy in sorted(range(1, Y), key=lambda d: -min(d, Y - d)) + [0]:
        start = pl.multiple_of(((y + dy) % Y) * pair, pair)
        rows = pl.ds(start, pair)
        weigh(Q - 1, rows)
        weighted(Q - 1, rows)
        for dc in reversed(range(C)):
            rows = pl.ds(pl.multiple_of(start + ((c + dc) % C) * ns, ns), ns)
            num, den = acc[rows, 0:D], acc[rows, D:2 * D]
            den = jnp.sum(jnp.where(eye, den, 0.0), axis=0, keepdims=True)
            if (dy, dc) == (0, 0):
                own = (num, den)
                continue
            i = group.index((dy, dc))
            hi, lo = split2(den)
            nsend[i, 0:ns, :] = num.astype(BF16)
            nsend[i, ns:ns + 16, :] = jnp.concatenate(
                [hi.astype(F32), lo.astype(F32), jnp.zeros((14, W), F32)], axis=0).astype(BF16)
            n_copies[i] = remote(nsend.at[i], nrecv.at[i], n_send.at[i], n_recv.at[i], group_dev(dy, dc))
    for cps in (s_copies, a_copies, t_copies.values(), r_copies, x_copies.values(), z_copies.values()):
        for cp in cps:
            cp.wait_send()
    num, den = own
    for i in n_copies:
        n_copies[i].wait_recv()
        got = nrecv[i].astype(F32)
        num = num + got[0:ns, :]
        den = den + got[ns:ns + 1, :] + got[ns + 1:ns + 2, :]
    den = jnp.broadcast_to(den, (ns, W)).T
    map_out[...] = (num / den).astype(BF16)
    for cp in n_copies.values():
        cp.wait_send()


def write_out(f, g, mapped, f_out, g_out, map_out, sem):
    copies = [
        pltpu.make_async_copy(a, b, sem.at[i]) for i, (a, b) in enumerate(((f, f_out), (g, g_out), (mapped, map_out)))]
    for cp in copies:
        cp.start()
    for cp in copies:
        cp.wait()


def local(dims, source, target, potential):
    X, Y, Z, C, ns, nt, D, all_s, all_t = dims
    G = Y * C
    Q = nt // W
    vm = pltpu.VMEM
    dma = pltpu.SemaphoreType.DMA
    f, g, mapped = pl.pallas_call(
        functools.partial(kernel, dims),
        out_shape=(
            jax.ShapeDtypeStruct((1, ns), F32),
            jax.ShapeDtypeStruct((1, nt), F32),
            jax.ShapeDtypeStruct((ns, D), BF16),
        ),
        in_specs=[pl.BlockSpec(memory_space=pl.ANY)] * 3,
        out_specs=(pl.BlockSpec(memory_space=pltpu.VMEM),) * 3,
        scratch_shapes=[
            vm((Z, nt, D), BF16),
            vm((Z, EXTRA, W), BF16),
            vm((G, ns, D), BF16),
            vm((1, nt), F32),
            vm((G * ns, 2 * D), BF16),
            vm((2 * D, Z * nt), BF16),
            vm((Z * nt, 2 * D), BF16),
            vm((G * ns, Z * nt), F32),
            vm((G * ns, W), F32),
            vm((G * ns, 2 * W), F32),
            vm((G * ns, 2 * W), F32),
            vm((8, 2 * W), F32),
            vm((8, 2 * W), F32),
            vm((G * ns, 128), F32),
            vm((G * ns, 128), F32),
            vm((G, G, ns), F32),
            vm((8, ns), F32),
            vm((Z, 8, W), F32),
            vm((Z, 8, W), F32),
            vm((Q, Z, W), F32),
            vm((Q, Z, W), F32),
            vm((Q * (X - 1), Z, W), F32),
            vm((Q, Z, W), F32),
            vm((Q * (Z - 1), Z, W), F32),
            vm((Q, 16, Z * W), BF16),
            vm((G * ns, Z * nt), BF16),
            vm((G * ns, 2 * D), F32),
            vm((G * ns, Z * W), BF16),
            vm((G - 1, ns + 16, D), BF16),
            vm((G - 1, ns + 16, D), BF16),
            dma((Q + 2,)),
            dma((Z - 1,)), dma((Z - 1,)),
            dma((Z * Q,)), dma((Z * Q,)),
            dma((G - 1,)), dma((G - 1,)),
            dma((G - 1,)), dma((G - 1,)),
            dma((Q * (X - 1),)), dma((Q * (X - 1),)),
            dma((Q * (Z - 1),)), dma((Q * (Z - 1),)),
            dma((G - 1,)), dma((G - 1,)),
        ],
        compiler_params=pltpu.CompilerParams(
            collective_id=0, has_side_effects=True, vmem_limit_bytes=VMEM),
        cost_estimate=pl.CostEstimate(flops=6 * 10**9, bytes_accessed=10**6, transcendentals=10**7),
    )(source, target, potential.reshape(1, nt))
    f, g, mapped = pl.pallas_call(
        write_out,
        out_shape=(
            jax.ShapeDtypeStruct((1, ns), F32),
            jax.ShapeDtypeStruct((1, nt), F32),
            jax.ShapeDtypeStruct((ns, D), BF16),
        ),
        in_specs=[pl.BlockSpec(memory_space=pl.ANY)] * 3,
        out_specs=(pl.BlockSpec(memory_space=pl.ANY),) * 3,
        scratch_shapes=[dma((3,))],
        compiler_params=pltpu.CompilerParams(vmem_limit_bytes=VMEM),
    )(f, g, mapped)
    return f.reshape(ns), g.reshape(nt), mapped


def solution(mesh, shape=(Y, Z, C)):
    placed = (P(("row", "col"), None), P("col", None), P("col"))

    def whole(source, target, potential):
        rows, cols = mesh.shape["row"], mesh.shape["col"]
        dims = (rows, *shape, source.shape[0] // (rows * cols), target.shape[0] // cols, source.shape[1],
                source.shape[0], target.shape[0])
        return jax.shard_map(
            functools.partial(local, dims),
            mesh=mesh,
            in_specs=placed,
            out_specs=(P(("row", "col")), P("col"), P(("row", "col"), None)),
            check_vma=False,
        )(source, target, potential)

    return whole
```

```python
import functools
import math

import jax
import jax.numpy as jnp
from jax import lax
from jax.experimental import pallas as pl
from jax.experimental.pallas import tpu as pltpu
from jax.sharding import PartitionSpec as P

MESH = pl.DeviceIdType.MESH
EPS = 0.02
LOG2E = 1.0 / math.log(2.0)
F32 = jnp.float32
BF16 = jnp.bfloat16

Y, Z, C = 4, 8, 2
LOW = -1e30
VMEM = 63532032
W, EXTRA = 128, 16


def split2(x):
    hi = x.astype(BF16)
    return hi, (x - hi.astype(F32)).astype(BF16)


def split3(x):
    hi = x.astype(BF16).astype(F32)
    mid = (x - hi).astype(BF16).astype(F32)
    return hi, mid, x - hi - mid


def squares(rows):
    both = jnp.concatenate(split2(jnp.square(rows.astype(F32))), axis=1)
    ones = jnp.ones((8, both.shape[1]), BF16)
    return lax.dot_general(ones, both, (((1,), (1,)), ((), ())), preferred_element_type=F32)[0:1, :]


def kernel(dims, src, tgt, pot, f_out, g_out, map_out, tbuf, abuf, sbuf, pbuf, lhs, rhs, ta, uall, lbc, col_a, col_b, top_a, top_b, macc, sacc, lrow, lfin,
           mstage, sstage, mcol, lcol, xbuf, zsend, zbuf, wrep, e2, acc, plan, nsend, nrecv, i_sem, a_send, a_recv, t_send, t_recv, s_send, s_recv,
           r_send, r_recv, x_send, x_recv, z_send, z_recv, n_send, n_recv):
    X, Y, Z, C, ns, nt, D, all_s, all_t = dims
    G = Y * C
    Q = nt // W
    CH = Z * W
    SCALE = LOG2E / (D * EPS)
    x = lax.axis_index("row")
    col = lax.axis_index("col")
    y = col // (Z * C)
    z = (col // C) % Z
    c = col % C

    def dev(xx, yy, zz, cc):
        return {"row": xx, "col": (yy * Z + zz) * C + cc}

    def remote(a, b, send, recv, to):
        cp = pltpu.make_async_remote_copy(
            src_ref=a, dst_ref=b, send_sem=send, recv_sem=recv, device_id=to, device_id_type=MESH)
        cp.start()
        return cp

    def lse(items):
        top = functools.reduce(jnp.maximum, items)
        total = functools.reduce(jnp.add, [jnp.exp2((i - top) * SCALE) for i in items])
        return top + jnp.log2(total) * (1.0 / SCALE)

    group = [(dy, dc) for dy in range(Y) for dc in range(C) if (dy, dc) != (0, 0)]

    def group_dev(dy, dc):
        return dev(x, (y + dy) % Y, z, (c + dc) % C)

    place = y * C + c

    barrier = pltpu.get_barrier_semaphore()
    peers = [group_dev(*g) for g in group]
    peers += [dev((x + d) % X, y, z, c) for d in range(1, X)]
    peers += [dev(x, y, (z + d) % Z, c) for d in range(1, Z)]
    for peer in peers:
        pl.semaphore_signal(barrier, inc=1, device_id=peer, device_id_type=MESH)
    fetch = [pltpu.make_async_copy(tgt.at[pl.ds(q * W, W), :], tbuf.at[0, pl.ds(q * W, W), :], i_sem.at[q]) for q in range(Q)]
    fetch.append(pltpu.make_async_copy(pot, pbuf, i_sem.at[Q]))
    fetch.append(pltpu.make_async_copy(src, sbuf.at[place], i_sem.at[Q + 1]))
    for cp in fetch:
        cp.start()
    rhs[D + EXTRA:2 * D, :] = jnp.zeros((D - EXTRA, Z * nt), BF16)
    macc[...] = jnp.full(macc.shape, LOW, F32)
    sacc[...] = jnp.zeros(sacc.shape, F32)
    ta[:, D:2 * D] = jnp.ones((Z * nt, D), BF16)
    lanes = lax.broadcasted_iota(jnp.int32, (ns, D), 1)
    for p in range(G):
        lhs[p * ns:(p + 1) * ns, D:2 * D] = jnp.where(lanes < 3, 1.0, 0.0).astype(BF16)
    pl.semaphore_wait(barrier, len(peers))

    H = Z // 2
    half = nt // 2
    t_copies = {}

    def side(d):
        return dev(x, y, (z + d) % Z, c)

    own_piece = pl.ds(pl.multiple_of(x * W, W), W)

    def to_z(r, k, a, b):
        t_copies[r, k] = remote(a, b, t_send.at[r * Q + k], t_recv.at[r * Q + k], side(Z - r))

    for r in (3, Z - 3):
        to_z(r, 0, tgt.at[own_piece, :], tbuf.at[r, own_piece, :])
    for h in range(2):
        rows = pl.ds(h * half, half)
        for r in (1, Z - 1):
            to_z(r, h, tgt.at[rows, :], tbuf.at[r, rows, :])

    def pass_on(r, h):
        t_copies[r, h].wait_recv()
        rows = pl.ds(h * half, half)
        there = 2 if r == 1 else Z - 2
        t_copies[there, h] = remote(
            tbuf.at[r, rows, :], tbuf.at[there, rows, :], t_send.at[there * Q + h], t_recv.at[there * Q + h],
            side(Z - 1 if r == 1 else 1))

    def half_way():
        have = jnp.where(c == 0, Z - 3, 3)
        to = jnp.where(c == 0, (z + 1) % Z, (z + Z - 1) % Z)
        t_copies[H, 0] = remote(
            tbuf.at[have, own_piece, :], tbuf.at[H, own_piece, :], t_send.at[H * Q], t_recv.at[H * Q], dev(x, y, to, c))

    def spread(r):
        t_copies[r, 0].wait_recv()
        for d in range(1, X):
            k = r * Q + d
            t_copies[r, d] = remote(
                tbuf.at[r, own_piece, :], tbuf.at[r, own_piece, :], t_send.at[k], t_recv.at[k], dev((x + d) % X, y, z, c))

    s_copies = [remote(src, sbuf.at[place], s_send.at[i], s_recv.at[i], group_dev(*g)) for i, g in enumerate(group)]

    for cp in fetch:
        cp.wait()
    own_sq = [squares(tbuf[0, q * W:(q + 1) * W, :]) for q in range(Q)]
    offset = jnp.concatenate([pbuf[0:1, q * W:(q + 1) * W] * float(D) - 0.5 * own_sq[q] for q in range(Q)], axis=0)
    abuf[0] = jnp.concatenate(list(split3(offset)) + [jnp.zeros((EXTRA - 3 * Q, W), F32)], axis=0).astype(BF16)
    a_copies = [
        remote(abuf.at[0], abuf.at[r], a_send.at[r - 1], a_recv.at[r - 1], dev(x, y, (z + Z - r) % Z, c)) for r in range(1, Z)]

    spread(3)
    spread(Z - 3)
    half_way()

    for cp in s_copies:
        cp.wait_recv()
    for p in range(G):
        lhs[p * ns:(p + 1) * ns, 0:D] = sbuf[p]

    def take(slot):
        offsets = abuf[slot].astype(F32)
        for q in range(Q):
            at = q * CH + slot * W
            cols = slice(slot * nt + q * W, slot * nt + (q + 1) * W)
            piece = tbuf[slot, q * W:(q + 1) * W, :]
            rhs[0:D, cols] = piece.T
            rhs[D:D + EXTRA, cols] = jnp.concatenate(
                [offsets[q + i * Q:q + i * Q + 1, :] for i in range(3)] + [jnp.zeros((EXTRA - 3, W), F32)],
                axis=0).astype(BF16)
            ta[at:at + W, 0:D] = piece

    RC = 64
    RM = 2 * ns

    def fold(rows, cols):
        pieces = [uall[rows, cols + q * W:cols + (q + 1) * W] for q in range(Q)]
        old = macc[rows, :]
        top = functools.reduce(jnp.maximum, pieces, old)
        total = sacc[rows, :] * jnp.exp2((old - top) * SCALE)
        for piece in pieces:
            total = total + jnp.exp2((piece - top) * SCALE)
        macc[rows, :] = top
        sacc[rows, :] = total

    def row_pass(slot):
        at = slot * nt
        for i in range(0, G * ns + RM, RM):
            if i < G * ns:
                uall[i:i + RM, at:at + nt] = jnp.dot(lhs[i:i + RM, :], rhs[:, at:at + nt], preferred_element_type=F32)
            if i > 0:
                for j in range(i - RM, i, RC):
                    fold(slice(j, j + RC), at)

    waited = {(1, 0), (1, 1), (Z - 1, 0), (Z - 1, 1), (3, 0), (Z - 3, 0), (H, 0)}

    def arrive(slot):
        a_copies[slot - 1].wait_recv()
        for (r, k), cp in t_copies.items():
            if r == slot and (r, k) not in waited:
                cp.wait_recv()
        take(slot)
        row_pass(slot)

    take(0)
    pass_on(1, 0)
    pass_on(Z - 1, 0)
    row_pass(0)
    spread(H)
    pass_on(1, 1)
    pass_on(Z - 1, 1)
    for slot in (1, Z - 1, 3, Z - 3, 2, Z - 2, H):
        arrive(slot)

    for p in range(G):
        m = macc[p * ns:(p + 1) * ns, :].T
        s = sacc[p * ns:(p + 1) * ns, :].T
        top = jnp.max(m, axis=0, keepdims=True)
        total = jnp.sum(s * jnp.exp2((m - top) * SCALE), axis=0, keepdims=True)
        lrow[0, p:p + 1, :] = top + jnp.log2(total) * (1.0 / SCALE)
    r_copies = [
        remote(lrow.at[0], lrow.at[i + 1], r_send.at[i], r_recv.at[i], group_dev(*g)) for i, g in enumerate(group)]
    src_sq = squares(sbuf[place])
    for cp in r_copies:
        cp.wait_recv()
    l1 = lse([lrow[i] for i in range(G)])
    lfin[0:G, :] = l1
    for p in range(G):
        lbc[p * ns:(p + 1) * ns, :] = jnp.broadcast_to(l1[p:p + 1, :], (ns, W)).T
    f_out[...] = (0.5 * src_sq - lfin[pl.ds(place, 1), :]) * (1.0 / D) - EPS * math.log(all_s)

    MC = 128
    chunks = G * ns // MC

    def scores(buf, tops, q, slot):
        cols = [slice((slot + i) * nt + q * W, (slot + i) * nt + (q + 1) * W) for i in range(2)]
        top = None
        for i in range(chunks):
            for j in range(0, MC, 32):
                rows = slice(i * MC + j, i * MC + j + 32)
                less = lbc[rows, :]
                u = jnp.concatenate([uall[rows, col] - less for col in cols], axis=1)
                buf[rows, :] = u
                part = jnp.max(u.reshape(4, 8, 2 * W), axis=0)
                top = part if top is None else jnp.maximum(top, part)
            yield
        tops[...] = jnp.broadcast_to(jnp.max(top, axis=0, keepdims=True), (8, 2 * W))
        yield

    def column(buf, tops, slot, at):
        top = tops[...]
        total = jnp.zeros((8, 2 * W), F32)
        for i in range(chunks):
            for j in range(0, MC, 32):
                rows = slice(i * MC + j, i * MC + j + 32)
                e = jnp.exp2((buf[rows, :].reshape(4, 8, 2 * W) - top[None]) * SCALE)
                total = total + jnp.sum(e, axis=0)
                e2[rows, at:at + 2 * W] = e.reshape(32, 2 * W).astype(BF16)
            yield
        total = jnp.broadcast_to(jnp.sum(total, axis=0, keepdims=True), (8, 2 * W))
        for i in range(2):
            mstage[slot + i] = top[:, i * W:(i + 1) * W]
            sstage[slot + i] = total[:, i * W:(i + 1) * W]
        yield

    def together(*steps):
        for _ in zip(*steps):
            pass

    x_copies, z_copies = {}, {}

    tiles = [(q, slot) for q in range(Q) for slot in range(0, Z, 2)]

    def column_chunk(q):
        for n, (tile_q, slot) in enumerate(tiles):
            if tile_q == q:
                here, there = ((col_a, top_a), (col_b, top_b)) if n % 2 == 0 else ((col_b, top_b), (col_a, top_a))
                steps = [column(*here, slot, q * CH + slot * W)]
                if n + 1 < len(tiles):
                    steps.insert(0, scores(*there, *tiles[n + 1]))
                together(*steps)

        mcol[q] = jnp.concatenate([mstage[r, 0:1, :] for r in range(Z)], axis=0)
        total = jnp.concatenate([sstage[r, 0:1, :] for r in range(Z)], axis=0)
        lcol[q] = mcol[q] + jnp.log2(total) * (1.0 / SCALE)
        for d in range(1, X):
            k = q * (X - 1) + d - 1
            x_copies[q, d] = remote(lcol.at[q], xbuf.at[k], x_send.at[k], x_recv.at[k], dev((x + d) % X, y, z, c))

    def across_z(q):
        for d in range(1, X):
            x_copies[q, d].wait_recv()
        zsend[q] = lse([lcol[q]] + [xbuf[q * (X - 1) + d - 1] for d in range(1, X)])
        for d in range(1, Z):
            k = q * (Z - 1) + d - 1
            z_copies[q, d] = remote(zsend.at[q], zbuf.at[k], z_send.at[k], z_recv.at[k], dev(x, y, (z + d) % Z, c))

    def weights(q):
        terms = [zsend[q]]
        for d in range(1, Z):
            z_copies[q, d].wait_recv()
            got = zbuf[q * (Z - 1) + d - 1]
            terms.append(jnp.concatenate([got[d:Z, :], got[0:d, :]], axis=0))
        l2 = lse(terms)
        g_out[0:1, q * W:(q + 1) * W] = pbuf[0:1, q * W:(q + 1) * W] - l2[0:1, :] * (1.0 / D) + EPS * (
            math.log(all_s) - math.log(all_t))
        w = jnp.exp2((mcol[q] - l2) * SCALE)
        for r in range(Z):
            wrep[q, :, r * W:(r + 1) * W] = jnp.broadcast_to(w[r:r + 1, :], (16, W)).astype(BF16)

    pair = C * ns

    def weigh(q, rows):
        for i in range(0, rows.size, 64):
            part = pl.ds(rows.start + i, 64)
            plan[part, :] = (e2[part, q * CH:(q + 1) * CH].reshape(4, 16, CH) * wrep[q][None]).reshape(64, CH)

    def weighted(q, rows):
        got = jnp.dot(plan[rows, :], ta[q * CH:(q + 1) * CH, :], preferred_element_type=F32)
        acc[rows, :] = got if q == 0 else acc[rows, :] + got

    def add_chunk(q):
        weights(q)
        weigh(q, pl.ds(0, G * ns))
        for i in range(2):
            weighted(q, pl.ds(i * (G * ns // 2), G * ns // 2))

    together(scores(col_a, top_a, 0, 0))
    for q in range(Q):
        column_chunk(q)
    for q in range(Q):
        across_z(q)
    for q in range(Q - 1):
        add_chunk(q)
    weights(Q - 1)

    eye = lax.broadcasted_iota(jnp.int32, (ns, W), 0) == lax.broadcasted_iota(jnp.int32, (ns, W), 1)
    n_copies = {}
    own = None
    for dy in sorted(range(1, Y), key=lambda d: -min(d, Y - d)) + [0]:
        start = pl.multiple_of(((y + dy) % Y) * pair, pair)
        rows = pl.ds(start, pair)
        weigh(Q - 1, rows)
        weighted(Q - 1, rows)
        for dc in reversed(range(C)):
            rows = pl.ds(pl.multiple_of(start + ((c + dc) % C) * ns, ns), ns)
            num, den = acc[rows, 0:D], acc[rows, D:2 * D]
            den = jnp.sum(jnp.where(eye, den, 0.0), axis=0, keepdims=True)
            if (dy, dc) == (0, 0):
                own = (num, den)
                continue
            i = group.index((dy, dc))
            hi, lo = split2(den)
            nsend[i, 0:ns, :] = num.astype(BF16)
            nsend[i, ns:ns + 16, :] = jnp.concatenate(
                [hi.astype(F32), lo.astype(F32), jnp.zeros((14, W), F32)], axis=0).astype(BF16)
            n_copies[i] = remote(nsend.at[i], nrecv.at[i], n_send.at[i], n_recv.at[i], group_dev(dy, dc))
    for cps in (s_copies, a_copies, t_copies.values(), r_copies, x_copies.values(), z_copies.values()):
        for cp in cps:
            cp.wait_send()
    num, den = own
    for i in n_copies:
        n_copies[i].wait_recv()
        got = nrecv[i].astype(F32)
        num = num + got[0:ns, :]
        den = den + got[ns:ns + 1, :] + got[ns + 1:ns + 2, :]
    den = jnp.broadcast_to(den, (ns, W)).T
    map_out[...] = (num / den).astype(BF16)
    for cp in n_copies.values():
        cp.wait_send()


def write_out(f, g, mapped, f_out, g_out, map_out, sem):
    copies = [
        pltpu.make_async_copy(a, b, sem.at[i]) for i, (a, b) in enumerate(((f, f_out), (g, g_out), (mapped, map_out)))]
    for cp in copies:
        cp.start()
    for cp in copies:
        cp.wait()


def local(dims, source, target, potential):
    X, Y, Z, C, ns, nt, D, all_s, all_t = dims
    G = Y * C
    Q = nt // W
    vm = pltpu.VMEM
    dma = pltpu.SemaphoreType.DMA
    f, g, mapped = pl.pallas_call(
        functools.partial(kernel, dims),
        out_shape=(
            jax.ShapeDtypeStruct((1, ns), F32),
            jax.ShapeDtypeStruct((1, nt), F32),
            jax.ShapeDtypeStruct((ns, D), BF16),
        ),
        in_specs=[pl.BlockSpec(memory_space=pl.ANY)] * 3,
        out_specs=(pl.BlockSpec(memory_space=pltpu.VMEM),) * 3,
        scratch_shapes=[
            vm((Z, nt, D), BF16),
            vm((Z, EXTRA, W), BF16),
            vm((G, ns, D), BF16),
            vm((1, nt), F32),
            vm((G * ns, 2 * D), BF16),
            vm((2 * D, Z * nt), BF16),
            vm((Z * nt, 2 * D), BF16),
            vm((G * ns, Z * nt), F32),
            vm((G * ns, W), F32),
            vm((G * ns, 2 * W), F32),
            vm((G * ns, 2 * W), F32),
            vm((8, 2 * W), F32),
            vm((8, 2 * W), F32),
            vm((G * ns, 128), F32),
            vm((G * ns, 128), F32),
            vm((G, G, ns), F32),
            vm((8, ns), F32),
            vm((Z, 8, W), F32),
            vm((Z, 8, W), F32),
            vm((Q, Z, W), F32),
            vm((Q, Z, W), F32),
            vm((Q * (X - 1), Z, W), F32),
            vm((Q, Z, W), F32),
            vm((Q * (Z - 1), Z, W), F32),
            vm((Q, 16, Z * W), BF16),
            vm((G * ns, Z * nt), BF16),
            vm((G * ns, 2 * D), F32),
            vm((G * ns, Z * W), BF16),
            vm((G - 1, ns + 16, D), BF16),
            vm((G - 1, ns + 16, D), BF16),
            dma((Q + 2,)),
            dma((Z - 1,)), dma((Z - 1,)),
            dma((Z * Q,)), dma((Z * Q,)),
            dma((G - 1,)), dma((G - 1,)),
            dma((G - 1,)), dma((G - 1,)),
            dma((Q * (X - 1),)), dma((Q * (X - 1),)),
            dma((Q * (Z - 1),)), dma((Q * (Z - 1),)),
            dma((G - 1,)), dma((G - 1,)),
        ],
        compiler_params=pltpu.CompilerParams(
            collective_id=0, has_side_effects=True, vmem_limit_bytes=VMEM),
        cost_estimate=pl.CostEstimate(flops=6 * 10**9, bytes_accessed=10**6, transcendentals=10**7),
    )(source, target, potential.reshape(1, nt))
    f, g, mapped = pl.pallas_call(
        write_out,
        out_shape=(
            jax.ShapeDtypeStruct((1, ns), F32),
            jax.ShapeDtypeStruct((1, nt), F32),
            jax.ShapeDtypeStruct((ns, D), BF16),
        ),
        in_specs=[pl.BlockSpec(memory_space=pl.ANY)] * 3,
        out_specs=(pl.BlockSpec(memory_space=pl.ANY),) * 3,
        scratch_shapes=[dma((3,))],
        compiler_params=pltpu.CompilerParams(vmem_limit_bytes=VMEM),
    )(f, g, mapped)
    return f.reshape(ns), g.reshape(nt), mapped


def solution(mesh, shape=(Y, Z, C)):
    placed = (P(("row", "col"), None), P("col", None), P("col"))

    def whole(source, target, potential):
        rows, cols = mesh.shape["row"], mesh.shape["col"]
        dims = (rows, *shape, source.shape[0] // (rows * cols), target.shape[0] // cols, source.shape[1],
                source.shape[0], target.shape[0])
        return jax.shard_map(
            functools.partial(local, dims),
            mesh=mesh,
            in_specs=placed,
            out_specs=(P(("row", "col")), P("col"), P(("row", "col"), None)),
            check_vma=False,
        )(source, target, potential)

    return whole
```

```python
import functools
import math

import jax
import jax.numpy as jnp
from jax import lax
from jax.experimental import pallas as pl
from jax.experimental.pallas import tpu as pltpu
from jax.sharding import PartitionSpec as P

MESH = pl.DeviceIdType.MESH
EPS = 0.02
LOG2E = 1.0 / math.log(2.0)
F32 = jnp.float32
BF16 = jnp.bfloat16

Y, Z, C = 4, 8, 2
LOW = -1e30
VMEM = 63532032
W, EXTRA = 128, 16


def split2(x):
    hi = x.astype(BF16)
    return hi, (x - hi.astype(F32)).astype(BF16)


def split3(x):
    hi = x.astype(BF16).astype(F32)
    mid = (x - hi).astype(BF16).astype(F32)
    return hi, mid, x - hi - mid


def squares(rows):
    both = jnp.concatenate(split2(jnp.square(rows.astype(F32))), axis=1)
    ones = jnp.ones((8, both.shape[1]), BF16)
    return lax.dot_general(ones, both, (((1,), (1,)), ((), ())), preferred_element_type=F32)[0:1, :]


def kernel(dims, src, tgt, pot, f_out, g_out, map_out, tbuf, abuf, sbuf, pbuf, lhs, rhs, ta, uall, lbc, col_a, col_b, top_a, top_b, macc, sacc, lrow, lfin,
           mstage, sstage, mcol, lcol, xbuf, zsend, zbuf, wrep, e2, acc, plan, nsend, nrecv, i_sem, a_send, a_recv, t_send, t_recv, s_send, s_recv,
           r_send, r_recv, x_send, x_recv, z_send, z_recv, n_send, n_recv):
    X, Y, Z, C, ns, nt, D, all_s, all_t = dims
    G = Y * C
    Q = nt // W
    CH = Z * W
    SCALE = LOG2E / (D * EPS)
    x = lax.axis_index("row")
    col = lax.axis_index("col")
    y = col // (Z * C)
    z = (col // C) % Z
    c = col % C

    def dev(xx, yy, zz, cc):
        return {"row": xx, "col": (yy * Z + zz) * C + cc}

    def remote(a, b, send, recv, to):
        cp = pltpu.make_async_remote_copy(
            src_ref=a, dst_ref=b, send_sem=send, recv_sem=recv, device_id=to, device_id_type=MESH)
        cp.start()
        return cp

    def lse(items):
        top = functools.reduce(jnp.maximum, items)
        total = functools.reduce(jnp.add, [jnp.exp2((i - top) * SCALE) for i in items])
        return top + jnp.log2(total) * (1.0 / SCALE)

    group = [(dy, dc) for dy in range(Y) for dc in range(C) if (dy, dc) != (0, 0)]

    def group_dev(dy, dc):
        return dev(x, (y + dy) % Y, z, (c + dc) % C)

    place = y * C + c

    barrier = pltpu.get_barrier_semaphore()
    peers = [group_dev(*g) for g in group]
    peers += [dev((x + d) % X, y, z, c) for d in range(1, X)]
    peers += [dev(x, y, (z + d) % Z, c) for d in range(1, Z)]
    for peer in peers:
        pl.semaphore_signal(barrier, inc=1, device_id=peer, device_id_type=MESH)
    fetch = [pltpu.make_async_copy(tgt.at[pl.ds(q * W, W), :], tbuf.at[0, pl.ds(q * W, W), :], i_sem.at[q]) for q in range(Q)]
    fetch.append(pltpu.make_async_copy(pot, pbuf, i_sem.at[Q]))
    fetch.append(pltpu.make_async_copy(src, sbuf.at[place], i_sem.at[Q + 1]))
    for cp in fetch:
        cp.start()
    rhs[D + EXTRA:2 * D, :] = jnp.zeros((D - EXTRA, Z * nt), BF16)
    macc[...] = jnp.full(macc.shape, LOW, F32)
    sacc[...] = jnp.zeros(sacc.shape, F32)
    ta[:, D:2 * D] = jnp.ones((Z * nt, D), BF16)
    lanes = lax.broadcasted_iota(jnp.int32, (ns, D), 1)
    for p in range(G):
        lhs[p * ns:(p + 1) * ns, D:2 * D] = jnp.where(lanes < 3, 1.0, 0.0).astype(BF16)
    pl.semaphore_wait(barrier, len(peers))

    s_copies = [remote(src, sbuf.at[place], s_send.at[i], s_recv.at[i], group_dev(*g)) for i, g in enumerate(group)]

    H = Z // 2
    half = nt // 2
    t_copies = {}

    def side(d):
        return dev(x, y, (z + d) % Z, c)

    own_piece = pl.ds(pl.multiple_of(x * W, W), W)

    def to_z(r, k, a, b):
        t_copies[r, k] = remote(a, b, t_send.at[r * Q + k], t_recv.at[r * Q + k], side(Z - r))

    for r in (3, Z - 3):
        to_z(r, 0, tgt.at[own_piece, :], tbuf.at[r, own_piece, :])
    for h in range(2):
        rows = pl.ds(h * half, half)
        for r in (1, Z - 1):
            to_z(r, h, tgt.at[rows, :], tbuf.at[r, rows, :])

    def pass_on(r, h):
        t_copies[r, h].wait_recv()
        rows = pl.ds(h * half, half)
        there = 2 if r == 1 else Z - 2
        t_copies[there, h] = remote(
            tbuf.at[r, rows, :], tbuf.at[there, rows, :], t_send.at[there * Q + h], t_recv.at[there * Q + h],
            side(Z - 1 if r == 1 else 1))

    def half_way():
        have = jnp.where(c == 0, Z - 3, 3)
        to = jnp.where(c == 0, (z + 1) % Z, (z + Z - 1) % Z)
        t_copies[H, 0] = remote(
            tbuf.at[have, own_piece, :], tbuf.at[H, own_piece, :], t_send.at[H * Q], t_recv.at[H * Q], dev(x, y, to, c))

    def spread(r):
        t_copies[r, 0].wait_recv()
        for d in range(1, X):
            k = r * Q + d
            t_copies[r, d] = remote(
                tbuf.at[r, own_piece, :], tbuf.at[r, own_piece, :], t_send.at[k], t_recv.at[k], dev((x + d) % X, y, z, c))

    for cp in fetch:
        cp.wait()
    own_sq = [squares(tbuf[0, q * W:(q + 1) * W, :]) for q in range(Q)]
    offset = jnp.concatenate([pbuf[0:1, q * W:(q + 1) * W] * float(D) - 0.5 * own_sq[q] for q in range(Q)], axis=0)
    abuf[0] = jnp.concatenate(list(split3(offset)) + [jnp.zeros((EXTRA - 3 * Q, W), F32)], axis=0).astype(BF16)
    a_copies = [
        remote(abuf.at[0], abuf.at[r], a_send.at[r - 1], a_recv.at[r - 1], dev(x, y, (z + Z - r) % Z, c)) for r in range(1, Z)]

    spread(3)
    spread(Z - 3)
    half_way()

    for cp in s_copies:
        cp.wait_recv()
    for p in range(G):
        lhs[p * ns:(p + 1) * ns, 0:D] = sbuf[p]

    def take(slot):
        offsets = abuf[slot].astype(F32)
        for q in range(Q):
            at = q * CH + slot * W
            cols = slice(slot * nt + q * W, slot * nt + (q + 1) * W)
            piece = tbuf[slot, q * W:(q + 1) * W, :]
            rhs[0:D, cols] = piece.T
            rhs[D:D + EXTRA, cols] = jnp.concatenate(
                [offsets[q + i * Q:q + i * Q + 1, :] for i in range(3)] + [jnp.zeros((EXTRA - 3, W), F32)],
                axis=0).astype(BF16)
            ta[at:at + W, 0:D] = piece

    RC = 64
    RM = 4 * ns

    def fold(rows, cols):
        pieces = [uall[rows, cols + q * W:cols + (q + 1) * W] for q in range(Q)]
        old = macc[rows, :]
        top = functools.reduce(jnp.maximum, pieces, old)
        total = sacc[rows, :] * jnp.exp2((old - top) * SCALE)
        for piece in pieces:
            total = total + jnp.exp2((piece - top) * SCALE)
        macc[rows, :] = top
        sacc[rows, :] = total

    def row_pass(slot):
        at = slot * nt
        for i in range(0, G * ns + RM, RM):
            if i < G * ns:
                uall[i:i + RM, at:at + nt] = jnp.dot(lhs[i:i + RM, :], rhs[:, at:at + nt], preferred_element_type=F32)
            if i > 0:
                for j in range(i - RM, i, RC):
                    fold(slice(j, j + RC), at)

    waited = {(1, 0), (1, 1), (Z - 1, 0), (Z - 1, 1), (3, 0), (Z - 3, 0), (H, 0)}

    def arrive(*slots):
        for slot in slots:
            a_copies[slot - 1].wait_recv()
            for (r, k), cp in t_copies.items():
                if r == slot and (r, k) not in waited:
                    cp.wait_recv()
        for slot in slots:
            take(slot)
        for slot in slots:
            row_pass(slot)

    take(0)
    pass_on(1, 0)
    pass_on(Z - 1, 0)
    row_pass(0)
    spread(H)
    pass_on(1, 1)
    pass_on(Z - 1, 1)
    arrive(1, Z - 1)
    arrive(3, Z - 3)
    arrive(2, Z - 2)
    arrive(H)

    for p in range(G):
        rows = slice(p * ns, (p + 1) * ns)
        part = (macc[rows, :] + jnp.log2(sacc[rows, :]) * (1.0 / SCALE)).T
        top = jnp.max(part, axis=0, keepdims=True)
        total = jnp.sum(jnp.exp2((part - top) * SCALE), axis=0, keepdims=True)
        lrow[0, p:p + 1, :] = top + jnp.log2(total) * (1.0 / SCALE)
    r_copies = [
        remote(lrow.at[0], lrow.at[i + 1], r_send.at[i], r_recv.at[i], group_dev(*g)) for i, g in enumerate(group)]
    src_sq = squares(sbuf[place])
    for cp in r_copies:
        cp.wait_recv()
    l1 = lse([lrow[i] for i in range(G)])
    lfin[0:G, :] = l1
    for p in range(G):
        lbc[p * ns:(p + 1) * ns, :] = jnp.broadcast_to(l1[p:p + 1, :], (ns, W)).T
    f_out[...] = (0.5 * src_sq - lfin[pl.ds(place, 1), :]) * (1.0 / D) - EPS * math.log(all_s)

    MC = 128
    chunks = G * ns // MC

    def scores(buf, tops, q, slot):
        cols = [slice((slot + i) * nt + q * W, (slot + i) * nt + (q + 1) * W) for i in range(2)]
        top = None
        for i in range(chunks):
            for j in range(0, MC, 32):
                rows = slice(i * MC + j, i * MC + j + 32)
                less = lbc[rows, :]
                u = jnp.concatenate([uall[rows, col] - less for col in cols], axis=1)
                buf[rows, :] = u
                part = jnp.max(u.reshape(4, 8, 2 * W), axis=0)
                top = part if top is None else jnp.maximum(top, part)
            yield
        tops[...] = jnp.broadcast_to(jnp.max(top, axis=0, keepdims=True), (8, 2 * W))
        yield

    def column(buf, tops, slot, at):
        top = tops[...]
        total = jnp.zeros((8, 2 * W), F32)
        for i in range(chunks):
            for j in range(0, MC, 32):
                rows = slice(i * MC + j, i * MC + j + 32)
                e = jnp.exp2((buf[rows, :].reshape(4, 8, 2 * W) - top[None]) * SCALE)
                total = total + jnp.sum(e, axis=0)
                e2[rows, at:at + 2 * W] = e.reshape(32, 2 * W).astype(BF16)
            yield
        total = jnp.broadcast_to(jnp.sum(total, axis=0, keepdims=True), (8, 2 * W))
        for i in range(2):
            mstage[slot + i] = top[:, i * W:(i + 1) * W]
            sstage[slot + i] = total[:, i * W:(i + 1) * W]
        yield

    def together(*steps):
        for _ in zip(*steps):
            pass

    x_copies, z_copies = {}, {}

    tiles = [(q, slot) for q in range(Q) for slot in range(0, Z, 2)]

    def column_chunk(q):
        for n, (tile_q, slot) in enumerate(tiles):
            if tile_q == q:
                here, there = ((col_a, top_a), (col_b, top_b)) if n % 2 == 0 else ((col_b, top_b), (col_a, top_a))
                steps = [column(*here, slot, q * CH + slot * W)]
                if n + 1 < len(tiles):
                    steps.insert(0, scores(*there, *tiles[n + 1]))
                together(*steps)

        mcol[q] = jnp.concatenate([mstage[r, 0:1, :] for r in range(Z)], axis=0)
        total = jnp.concatenate([sstage[r, 0:1, :] for r in range(Z)], axis=0)
        lcol[q] = mcol[q] + jnp.log2(total) * (1.0 / SCALE)
        for d in range(1, X):
            k = q * (X - 1) + d - 1
            x_copies[q, d] = remote(lcol.at[q], xbuf.at[k], x_send.at[k], x_recv.at[k], dev((x + d) % X, y, z, c))

    def across_z(q):
        for d in range(1, X):
            x_copies[q, d].wait_recv()
        zsend[q] = lse([lcol[q]] + [xbuf[q * (X - 1) + d - 1] for d in range(1, X)])
        for d in range(1, Z):
            k = q * (Z - 1) + d - 1
            z_copies[q, d] = remote(zsend.at[q], zbuf.at[k], z_send.at[k], z_recv.at[k], dev(x, y, (z + d) % Z, c))

    def weights(q):
        terms = [zsend[q]]
        for d in range(1, Z):
            z_copies[q, d].wait_recv()
            got = zbuf[q * (Z - 1) + d - 1]
            terms.append(jnp.concatenate([got[d:Z, :], got[0:d, :]], axis=0))
        l2 = lse(terms)
        g_out[0:1, q * W:(q + 1) * W] = pbuf[0:1, q * W:(q + 1) * W] - l2[0:1, :] * (1.0 / D) + EPS * (
            math.log(all_s) - math.log(all_t))
        w = jnp.exp2((mcol[q] - l2) * SCALE)
        for r in range(Z):
            wrep[q, :, r * W:(r + 1) * W] = jnp.broadcast_to(w[r:r + 1, :], (16, W)).astype(BF16)

    pair = C * ns

    def weigh(q, rows):
        for i in range(0, rows.size, 64):
            part = pl.ds(rows.start + i, 64)
            plan[part, :] = (e2[part, q * CH:(q + 1) * CH].reshape(4, 16, CH) * wrep[q][None]).reshape(64, CH)

    def weighted(q, rows):
        got = jnp.dot(plan[rows, :], ta[q * CH:(q + 1) * CH, :], preferred_element_type=F32)
        acc[rows, :] = got if q == 0 else acc[rows, :] + got

    def add_chunk(q):
        weights(q)
        weigh(q, pl.ds(0, G * ns))
        for i in range(2):
            weighted(q, pl.ds(i * (G * ns // 2), G * ns // 2))

    together(scores(col_a, top_a, 0, 0))
    for q in range(Q):
        column_chunk(q)
    for q in range(Q):
        across_z(q)
    for q in range(Q - 1):
        add_chunk(q)
    weights(Q - 1)

    eye = lax.broadcasted_iota(jnp.int32, (ns, W), 0) == lax.broadcasted_iota(jnp.int32, (ns, W), 1)
    n_copies = {}
    own = None
    for dy in sorted(range(1, Y), key=lambda d: -min(d, Y - d)) + [0]:
        start = pl.multiple_of(((y + dy) % Y) * pair, pair)
        rows = pl.ds(start, pair)
        weigh(Q - 1, rows)
        weighted(Q - 1, rows)
        for dc in reversed(range(C)):
            rows = pl.ds(pl.multiple_of(start + ((c + dc) % C) * ns, ns), ns)
            num, den = acc[rows, 0:D], acc[rows, D:2 * D]
            den = jnp.sum(jnp.where(eye, den, 0.0), axis=0, keepdims=True)
            if (dy, dc) == (0, 0):
                own = (num, den)
                continue
            i = group.index((dy, dc))
            hi, lo = split2(den)
            nsend[i, 0:ns, :] = num.astype(BF16)
            nsend[i, ns:ns + 16, :] = jnp.concatenate(
                [hi.astype(F32), lo.astype(F32), jnp.zeros((14, W), F32)], axis=0).astype(BF16)
            n_copies[i] = remote(nsend.at[i], nrecv.at[i], n_send.at[i], n_recv.at[i], group_dev(dy, dc))
    for cps in (s_copies, a_copies, t_copies.values(), r_copies, x_copies.values(), z_copies.values()):
        for cp in cps:
            cp.wait_send()
    num, den = own
    for i in n_copies:
        n_copies[i].wait_recv()
        got = nrecv[i].astype(F32)
        num = num + got[0:ns, :]
        den = den + got[ns:ns + 1, :] + got[ns + 1:ns + 2, :]
    den = jnp.broadcast_to(den, (ns, W)).T
    map_out[...] = (num / den).astype(BF16)
    for cp in n_copies.values():
        cp.wait_send()


def write_out(f, g, mapped, f_out, g_out, map_out, f_mid, g_mid, map_mid, sem):
    arrays = ((f, f_mid, f_out), (g, g_mid, g_out), (mapped, map_mid, map_out))
    into = [pltpu.make_async_copy(a, b, sem.at[i]) for i, (a, b, _) in enumerate(arrays)]
    out = [pltpu.make_async_copy(b, c, sem.at[3 + i]) for i, (_, b, c) in enumerate(arrays)]
    for cp in into:
        cp.start()
    for i in (2, 1, 0):
        into[i].wait()
        out[i].start()
    for cp in out:
        cp.wait()


def local(dims, source, target, potential):
    X, Y, Z, C, ns, nt, D, all_s, all_t = dims
    G = Y * C
    Q = nt // W
    vm = pltpu.VMEM
    dma = pltpu.SemaphoreType.DMA
    f, g, mapped = pl.pallas_call(
        functools.partial(kernel, dims),
        out_shape=(
            jax.ShapeDtypeStruct((1, ns), F32),
            jax.ShapeDtypeStruct((1, nt), F32),
            jax.ShapeDtypeStruct((ns, D), BF16),
        ),
        in_specs=[pl.BlockSpec(memory_space=pl.ANY)] * 3,
        out_specs=(pl.BlockSpec(memory_space=pltpu.VMEM),) * 3,
        scratch_shapes=[
            vm((Z, nt, D), BF16),
            vm((Z, EXTRA, W), BF16),
            vm((G, ns, D), BF16),
            vm((1, nt), F32),
            vm((G * ns, 2 * D), BF16),
            vm((2 * D, Z * nt), BF16),
            vm((Z * nt, 2 * D), BF16),
            vm((G * ns, Z * nt), F32),
            vm((G * ns, W), F32),
            vm((G * ns, 2 * W), F32),
            vm((G * ns, 2 * W), F32),
            vm((8, 2 * W), F32),
            vm((8, 2 * W), F32),
            vm((G * ns, 128), F32),
            vm((G * ns, 128), F32),
            vm((G, G, ns), F32),
            vm((8, ns), F32),
            vm((Z, 8, W), F32),
            vm((Z, 8, W), F32),
            vm((Q, Z, W), F32),
            vm((Q, Z, W), F32),
            vm((Q * (X - 1), Z, W), F32),
            vm((Q, Z, W), F32),
            vm((Q * (Z - 1), Z, W), F32),
            vm((Q, 16, Z * W), BF16),
            vm((G * ns, Z * nt), BF16),
            vm((G * ns, 2 * D), F32),
            vm((G * ns, Z * W), BF16),
            vm((G - 1, ns + 16, D), BF16),
            vm((G - 1, ns + 16, D), BF16),
            dma((Q + 2,)),
            dma((Z - 1,)), dma((Z - 1,)),
            dma((Z * Q,)), dma((Z * Q,)),
            dma((G - 1,)), dma((G - 1,)),
            dma((G - 1,)), dma((G - 1,)),
            dma((Q * (X - 1),)), dma((Q * (X - 1),)),
            dma((Q * (Z - 1),)), dma((Q * (Z - 1),)),
            dma((G - 1,)), dma((G - 1,)),
        ],
        compiler_params=pltpu.CompilerParams(
            collective_id=0, has_side_effects=True, vmem_limit_bytes=VMEM),
        cost_estimate=pl.CostEstimate(flops=6 * 10**9, bytes_accessed=10**6, transcendentals=10**7),
    )(source, target, potential.reshape(1, nt))
    f, g, mapped = pl.pallas_call(
        write_out,
        out_shape=(
            jax.ShapeDtypeStruct((1, ns), F32),
            jax.ShapeDtypeStruct((1, nt), F32),
            jax.ShapeDtypeStruct((ns, D), BF16),
        ),
        in_specs=[pl.BlockSpec(memory_space=pl.ANY)] * 3,
        out_specs=(pl.BlockSpec(memory_space=pl.ANY),) * 3,
        scratch_shapes=[vm((1, ns), F32), vm((1, nt), F32), vm((ns, D), BF16), dma((6,))],
        compiler_params=pltpu.CompilerParams(vmem_limit_bytes=VMEM),
    )(f, g, mapped)
    return f.reshape(ns), g.reshape(nt), mapped


def solution(mesh, shape=(Y, Z, C)):
    placed = (P(("row", "col"), None), P("col", None), P("col"))

    def whole(source, target, potential):
        rows, cols = mesh.shape["row"], mesh.shape["col"]
        dims = (rows, *shape, source.shape[0] // (rows * cols), target.shape[0] // cols, source.shape[1],
                source.shape[0], target.shape[0])
        return jax.shard_map(
            functools.partial(local, dims),
            mesh=mesh,
            in_specs=placed,
            out_specs=(P(("row", "col")), P("col"), P(("row", "col"), None)),
            check_vma=False,
        )(source, target, potential)

    return whole
```

```python
import functools
import math

import jax
import jax.numpy as jnp
from jax import lax
from jax.experimental import pallas as pl
from jax.experimental.pallas import tpu as pltpu
from jax.sharding import PartitionSpec as P

MESH = pl.DeviceIdType.MESH
EPS = 0.02
LOG2E = 1.0 / math.log(2.0)
F32 = jnp.float32
BF16 = jnp.bfloat16

Y, Z, C = 4, 8, 2
LOW = -1e30
VMEM = 63532032
W, EXTRA = 128, 16


def split2(x):
    hi = x.astype(BF16)
    return hi, (x - hi.astype(F32)).astype(BF16)


def split3(x):
    hi = x.astype(BF16).astype(F32)
    mid = (x - hi).astype(BF16).astype(F32)
    return hi, mid, x - hi - mid


def nt_dot(a, b):
    return lax.dot_general(a, b, (((1,), (1,)), ((), ())), preferred_element_type=F32)


def squares(rows):
    both = jnp.concatenate(split2(jnp.square(rows.astype(F32))), axis=1)
    ones = jnp.ones((8, both.shape[1]), BF16)
    return nt_dot(ones, both)[0:1, :]


def kernel(dims, src, tgt, pot, f_out, g_out, map_out, tbuf, abuf, sbuf, pbuf, ta, uall, lbc, col_a, col_b, top_a, top_b, macc, sacc, lrow, lfin,
           mstage, sstage, mcol, lcol, xbuf, zsend, zbuf, wrep, e2, acc, plan, nsend, nrecv, i_sem, a_send, a_recv, t_send, t_recv, s_send, s_recv,
           r_send, r_recv, x_send, x_recv, z_send, z_recv, n_send, n_recv):
    X, Y, Z, C, ns, nt, D, all_s, all_t = dims
    G = Y * C
    Q = nt // W
    CH = Z * W
    SCALE = LOG2E / (D * EPS)
    x = lax.axis_index("row")
    col = lax.axis_index("col")
    y = col // (Z * C)
    z = (col // C) % Z
    c = col % C

    def dev(xx, yy, zz, cc):
        return {"row": xx, "col": (yy * Z + zz) * C + cc}

    def remote(a, b, send, recv, to):
        cp = pltpu.make_async_remote_copy(
            src_ref=a, dst_ref=b, send_sem=send, recv_sem=recv, device_id=to, device_id_type=MESH)
        cp.start()
        return cp

    def lse(items):
        top = functools.reduce(jnp.maximum, items)
        total = functools.reduce(jnp.add, [jnp.exp2((i - top) * SCALE) for i in items])
        return top + jnp.log2(total) * (1.0 / SCALE)

    group = [(dy, dc) for dy in range(Y) for dc in range(C) if (dy, dc) != (0, 0)]

    def group_dev(dy, dc):
        return dev(x, (y + dy) % Y, z, (c + dc) % C)

    place = y * C + c

    barrier = pltpu.get_barrier_semaphore()
    peers = [group_dev(*g) for g in group]
    peers += [dev((x + d) % X, y, z, c) for d in range(1, X)]
    peers += [dev(x, y, (z + d) % Z, c) for d in range(1, Z)]
    for peer in peers:
        pl.semaphore_signal(barrier, inc=1, device_id=peer, device_id_type=MESH)
    fetch = [pltpu.make_async_copy(tgt.at[pl.ds(q * W, W), :], tbuf.at[0, pl.ds(q * W, W), :], i_sem.at[q]) for q in range(Q)]
    fetch.append(pltpu.make_async_copy(pot, pbuf, i_sem.at[Q]))
    fetch.append(pltpu.make_async_copy(src, sbuf.at[place], i_sem.at[Q + 1]))
    for cp in fetch:
        cp.start()
    macc[...] = jnp.full(macc.shape, LOW, F32)
    sacc[...] = jnp.zeros(sacc.shape, F32)
    ta[:, D:2 * D] = jnp.ones((Z * nt, D), BF16)
    pl.semaphore_wait(barrier, len(peers))

    s_copies = [remote(src, sbuf.at[place], s_send.at[i], s_recv.at[i], group_dev(*g)) for i, g in enumerate(group)]

    H = Z // 2
    half = nt // 2
    t_copies = {}

    def side(d):
        return dev(x, y, (z + d) % Z, c)

    own_piece = pl.ds(pl.multiple_of(x * W, W), W)

    def to_z(r, k, a, b):
        t_copies[r, k] = remote(a, b, t_send.at[r * Q + k], t_recv.at[r * Q + k], side(Z - r))

    for r in (3, Z - 3):
        to_z(r, 0, tgt.at[own_piece, :], tbuf.at[r, own_piece, :])
    for h in range(2):
        rows = pl.ds(h * half, half)
        for r in (1, Z - 1):
            to_z(r, h, tgt.at[rows, :], tbuf.at[r, rows, :])

    def pass_on(r, h):
        t_copies[r, h].wait_recv()
        rows = pl.ds(h * half, half)
        there = 2 if r == 1 else Z - 2
        t_copies[there, h] = remote(
            tbuf.at[r, rows, :], tbuf.at[there, rows, :], t_send.at[there * Q + h], t_recv.at[there * Q + h],
            side(Z - 1 if r == 1 else 1))

    def half_way():
        have = jnp.where(c == 0, Z - 3, 3)
        to = jnp.where(c == 0, (z + 1) % Z, (z + Z - 1) % Z)
        t_copies[H, 0] = remote(
            tbuf.at[have, own_piece, :], tbuf.at[H, own_piece, :], t_send.at[H * Q], t_recv.at[H * Q], dev(x, y, to, c))

    def spread(r):
        t_copies[r, 0].wait_recv()
        for d in range(1, X):
            k = r * Q + d
            t_copies[r, d] = remote(
                tbuf.at[r, own_piece, :], tbuf.at[r, own_piece, :], t_send.at[k], t_recv.at[k], dev((x + d) % X, y, z, c))

    for cp in fetch:
        cp.wait()
    own_sq = [squares(tbuf[0, q * W:(q + 1) * W, :]) for q in range(Q)]
    offset = jnp.concatenate([pbuf[0:1, q * W:(q + 1) * W] * float(D) - 0.5 * own_sq[q] for q in range(Q)], axis=0)
    abuf[0] = jnp.concatenate(list(split3(offset)) + [jnp.zeros((EXTRA - 3 * Q, W), F32)], axis=0).astype(BF16)
    a_copies = [
        remote(abuf.at[0], abuf.at[r], a_send.at[r - 1], a_recv.at[r - 1], dev(x, y, (z + Z - r) % Z, c)) for r in range(1, Z)]

    spread(3)
    spread(Z - 3)
    half_way()

    for cp in s_copies:
        cp.wait_recv()

    def take(slot):
        for q in range(Q):
            at = q * CH + slot * W
            ta[at:at + W, 0:D] = tbuf[slot, q * W:(q + 1) * W, :]

    RC = 32
    RP = G // 2

    def fold(rows, slots, offsets):
        pieces = [
            uall[rows, slot * nt + q * W:slot * nt + (q + 1) * W] + offset[q:q + 1, :]
            for slot, offset in zip(slots, offsets) for q in range(Q)]
        old = macc[rows, :]
        top = functools.reduce(jnp.maximum, pieces, old)
        total = sacc[rows, :] * jnp.exp2((old - top) * SCALE)
        for piece in pieces:
            total = total + jnp.exp2((piece - top) * SCALE)
        macc[rows, :] = top
        sacc[rows, :] = total

    def row_pass(*slots):
        offsets = []
        for slot in slots:
            parts = abuf[slot].astype(F32)
            offsets.append(parts[0:Q, :] + parts[Q:2 * Q, :] + parts[2 * Q:3 * Q, :])
        for p in range(0, G + RP, RP):
            if p < G:
                for slot in slots:
                    uall[p * ns:(p + RP) * ns, slot * nt:(slot + 1) * nt] = nt_dot(
                        sbuf[p:p + RP].reshape(RP * ns, D), tbuf[slot])
            if p > 0:
                for j in range((p - RP) * ns, p * ns, RC):
                    fold(slice(j, j + RC), slots, offsets)

    waited = {(1, 0), (1, 1), (Z - 1, 0), (Z - 1, 1), (3, 0), (Z - 3, 0), (H, 0)}

    def arrive(*slots):
        for slot in slots:
            a_copies[slot - 1].wait_recv()
            for (r, k), cp in t_copies.items():
                if r == slot and (r, k) not in waited:
                    cp.wait_recv()
        for slot in slots:
            take(slot)
        row_pass(*slots)

    take(0)
    pass_on(1, 0)
    pass_on(Z - 1, 0)
    row_pass(0)
    spread(H)
    pass_on(1, 1)
    pass_on(Z - 1, 1)
    arrive(1, Z - 1)
    arrive(3, Z - 3)
    arrive(2, Z - 2)
    arrive(H)

    for p in range(G):
        rows = slice(p * ns, (p + 1) * ns)
        part = (macc[rows, :] + jnp.log2(sacc[rows, :]) * (1.0 / SCALE)).T
        top = jnp.max(part, axis=0, keepdims=True)
        total = jnp.sum(jnp.exp2((part - top) * SCALE), axis=0, keepdims=True)
        lrow[0, p:p + 1, :] = top + jnp.log2(total) * (1.0 / SCALE)
    r_copies = [
        remote(lrow.at[0], lrow.at[i + 1], r_send.at[i], r_recv.at[i], group_dev(*g)) for i, g in enumerate(group)]
    src_sq = squares(sbuf[place])
    for cp in r_copies:
        cp.wait_recv()
    l1 = lse([lrow[i] for i in range(G)])
    lfin[0:G, :] = l1
    for p in range(G):
        lbc[p * ns:(p + 1) * ns, :] = jnp.broadcast_to(l1[p:p + 1, :], (ns, W)).T
    f_out[...] = (0.5 * src_sq - lfin[pl.ds(place, 1), :]) * (1.0 / D) - EPS * math.log(all_s)

    MC = 128
    chunks = G * ns // MC

    def scores(buf, tops, q, slot):
        cols = [slice((slot + i) * nt + q * W, (slot + i) * nt + (q + 1) * W) for i in range(2)]
        top = None
        for i in range(chunks):
            for j in range(0, MC, 32):
                rows = slice(i * MC + j, i * MC + j + 32)
                less = lbc[rows, :]
                u = jnp.concatenate([uall[rows, col] - less for col in cols], axis=1)
                buf[rows, :] = u
                part = jnp.max(u.reshape(4, 8, 2 * W), axis=0)
                top = part if top is None else jnp.maximum(top, part)
            yield
        tops[...] = jnp.broadcast_to(jnp.max(top, axis=0, keepdims=True), (8, 2 * W))
        yield

    def column(buf, tops, slot, at):
        top = tops[...]
        total = jnp.zeros((8, 2 * W), F32)
        for i in range(chunks):
            for j in range(0, MC, 32):
                rows = slice(i * MC + j, i * MC + j + 32)
                e = jnp.exp2((buf[rows, :].reshape(4, 8, 2 * W) - top[None]) * SCALE)
                total = total + jnp.sum(e, axis=0)
                e2[rows, at:at + 2 * W] = e.reshape(32, 2 * W).astype(BF16)
            yield
        total = jnp.broadcast_to(jnp.sum(total, axis=0, keepdims=True), (8, 2 * W))
        for i in range(2):
            mstage[slot + i] = top[:, i * W:(i + 1) * W]
            sstage[slot + i] = total[:, i * W:(i + 1) * W]
        yield

    def together(*steps):
        for _ in zip(*steps):
            pass

    x_copies, z_copies = {}, {}

    tiles = [(q, slot) for q in range(Q) for slot in range(0, Z, 2)]

    def column_chunk(q):
        for n, (tile_q, slot) in enumerate(tiles):
            if tile_q == q:
                here, there = ((col_a, top_a), (col_b, top_b)) if n % 2 == 0 else ((col_b, top_b), (col_a, top_a))
                steps = [column(*here, slot, q * CH + slot * W)]
                if n + 1 < len(tiles):
                    steps.insert(0, scores(*there, *tiles[n + 1]))
                together(*steps)

        mcol[q] = jnp.concatenate([mstage[r, 0:1, :] for r in range(Z)], axis=0)
        total = jnp.concatenate([sstage[r, 0:1, :] for r in range(Z)], axis=0)
        lcol[q] = mcol[q] + jnp.log2(total) * (1.0 / SCALE)
        for d in range(1, X):
            k = q * (X - 1) + d - 1
            x_copies[q, d] = remote(lcol.at[q], xbuf.at[k], x_send.at[k], x_recv.at[k], dev((x + d) % X, y, z, c))

    def across_z(q):
        for d in range(1, X):
            x_copies[q, d].wait_recv()
        zsend[q] = lse([lcol[q]] + [xbuf[q * (X - 1) + d - 1] for d in range(1, X)])
        for d in range(1, Z):
            k = q * (Z - 1) + d - 1
            z_copies[q, d] = remote(zsend.at[q], zbuf.at[k], z_send.at[k], z_recv.at[k], dev(x, y, (z + d) % Z, c))

    def weights(q):
        terms = [zsend[q]]
        for d in range(1, Z):
            z_copies[q, d].wait_recv()
            got = zbuf[q * (Z - 1) + d - 1]
            terms.append(jnp.concatenate([got[d:Z, :], got[0:d, :]], axis=0))
        l2 = lse(terms)
        g_out[0:1, q * W:(q + 1) * W] = (0.5 * own_sq[q] - l2[0:1, :]) * (1.0 / D) + EPS * (math.log(all_s) - math.log(all_t))
        w = jnp.exp2((mcol[q] - l2) * SCALE)
        for r in range(Z):
            wrep[q, :, r * W:(r + 1) * W] = jnp.broadcast_to(w[r:r + 1, :], (16, W)).astype(BF16)

    pair = C * ns

    def weigh(q, rows):
        for i in range(0, rows.size, 64):
            part = pl.ds(rows.start + i, 64)
            plan[part, :] = (e2[part, q * CH:(q + 1) * CH].reshape(4, 16, CH) * wrep[q][None]).reshape(64, CH)

    def weighted(q, rows):
        got = jnp.dot(plan[rows, :], ta[q * CH:(q + 1) * CH, :], preferred_element_type=F32)
        acc[rows, :] = got if q == 0 else acc[rows, :] + got

    def add_chunk(q):
        weights(q)
        weigh(q, pl.ds(0, G * ns))
        for i in range(2):
            weighted(q, pl.ds(i * (G * ns // 2), G * ns // 2))

    together(scores(col_a, top_a, 0, 0))
    for q in range(Q):
        column_chunk(q)
    for q in range(Q):
        across_z(q)
    for q in range(Q - 1):
        add_chunk(q)
    weights(Q - 1)

    eye = lax.broadcasted_iota(jnp.int32, (ns, W), 0) == lax.broadcasted_iota(jnp.int32, (ns, W), 1)
    n_copies = {}
    own = None
    for dy in sorted(range(1, Y), key=lambda d: -min(d, Y - d)) + [0]:
        start = pl.multiple_of(((y + dy) % Y) * pair, pair)
        rows = pl.ds(start, pair)
        weigh(Q - 1, rows)
        weighted(Q - 1, rows)
        for dc in reversed(range(C)):
            rows = pl.ds(pl.multiple_of(start + ((c + dc) % C) * ns, ns), ns)
            num, den = acc[rows, 0:D], acc[rows, D:2 * D]
            den = jnp.sum(jnp.where(eye, den, 0.0), axis=0, keepdims=True)
            if (dy, dc) == (0, 0):
                own = (num, den)
                continue
            i = group.index((dy, dc))
            hi, lo = split2(den)
            nsend[i, 0:ns, :] = num.astype(BF16)
            nsend[i, ns:ns + 16, :] = jnp.concatenate(
                [hi.astype(F32), lo.astype(F32), jnp.zeros((14, W), F32)], axis=0).astype(BF16)
            n_copies[i] = remote(nsend.at[i], nrecv.at[i], n_send.at[i], n_recv.at[i], group_dev(dy, dc))
    for cps in (s_copies, a_copies, t_copies.values(), r_copies, x_copies.values(), z_copies.values()):
        for cp in cps:
            cp.wait_send()
    num, den = own
    for i in n_copies:
        n_copies[i].wait_recv()
        got = nrecv[i].astype(F32)
        num = num + got[0:ns, :]
        den = den + got[ns:ns + 1, :] + got[ns + 1:ns + 2, :]
    den = jnp.broadcast_to(den, (ns, W)).T
    map_out[...] = (num / den).astype(BF16)
    for cp in n_copies.values():
        cp.wait_send()


def write_out(f, g, mapped, f_out, g_out, map_out, f_mid, g_mid, map_mid, sem):
    arrays = ((f, f_mid, f_out), (g, g_mid, g_out), (mapped, map_mid, map_out))
    into = [pltpu.make_async_copy(a, b, sem.at[i]) for i, (a, b, _) in enumerate(arrays)]
    out = [pltpu.make_async_copy(b, c, sem.at[3 + i]) for i, (_, b, c) in enumerate(arrays)]
    for cp in into:
        cp.start()
    for i in (2, 1, 0):
        into[i].wait()
        out[i].start()
    for cp in out:
        cp.wait()


def local(dims, source, target, potential):
    X, Y, Z, C, ns, nt, D, all_s, all_t = dims
    G = Y * C
    Q = nt // W
    vm = pltpu.VMEM
    dma = pltpu.SemaphoreType.DMA
    f, g, mapped = pl.pallas_call(
        functools.partial(kernel, dims),
        out_shape=(
            jax.ShapeDtypeStruct((1, ns), F32),
            jax.ShapeDtypeStruct((1, nt), F32),
            jax.ShapeDtypeStruct((ns, D), BF16),
        ),
        in_specs=[pl.BlockSpec(memory_space=pl.ANY)] * 3,
        out_specs=(pl.BlockSpec(memory_space=pltpu.VMEM),) * 3,
        scratch_shapes=[
            vm((Z, nt, D), BF16),
            vm((Z, EXTRA, W), BF16),
            vm((G, ns, D), BF16),
            vm((1, nt), F32),
            vm((Z * nt, 2 * D), BF16),
            vm((G * ns, Z * nt), F32),
            vm((G * ns, W), F32),
            vm((G * ns, 2 * W), F32),
            vm((G * ns, 2 * W), F32),
            vm((8, 2 * W), F32),
            vm((8, 2 * W), F32),
            vm((G * ns, 128), F32),
            vm((G * ns, 128), F32),
            vm((G, G, ns), F32),
            vm((8, ns), F32),
            vm((Z, 8, W), F32),
            vm((Z, 8, W), F32),
            vm((Q, Z, W), F32),
            vm((Q, Z, W), F32),
            vm((Q * (X - 1), Z, W), F32),
            vm((Q, Z, W), F32),
            vm((Q * (Z - 1), Z, W), F32),
            vm((Q, 16, Z * W), BF16),
            vm((G * ns, Z * nt), BF16),
            vm((G * ns, 2 * D), F32),
            vm((G * ns, Z * W), BF16),
            vm((G - 1, ns + 16, D), BF16),
            vm((G - 1, ns + 16, D), BF16),
            dma((Q + 2,)),
            dma((Z - 1,)), dma((Z - 1,)),
            dma((Z * Q,)), dma((Z * Q,)),
            dma((G - 1,)), dma((G - 1,)),
            dma((G - 1,)), dma((G - 1,)),
            dma((Q * (X - 1),)), dma((Q * (X - 1),)),
            dma((Q * (Z - 1),)), dma((Q * (Z - 1),)),
            dma((G - 1,)), dma((G - 1,)),
        ],
        compiler_params=pltpu.CompilerParams(
            collective_id=0, has_side_effects=True, vmem_limit_bytes=VMEM),
        cost_estimate=pl.CostEstimate(flops=6 * 10**9, bytes_accessed=10**6, transcendentals=10**7),
    )(source, target, potential.reshape(1, nt))
    f, g, mapped = pl.pallas_call(
        write_out,
        out_shape=(
            jax.ShapeDtypeStruct((1, ns), F32),
            jax.ShapeDtypeStruct((1, nt), F32),
            jax.ShapeDtypeStruct((ns, D), BF16),
        ),
        in_specs=[pl.BlockSpec(memory_space=pl.ANY)] * 3,
        out_specs=(pl.BlockSpec(memory_space=pl.ANY),) * 3,
        scratch_shapes=[vm((1, ns), F32), vm((1, nt), F32), vm((ns, D), BF16), dma((6,))],
        compiler_params=pltpu.CompilerParams(vmem_limit_bytes=VMEM),
    )(f, g, mapped)
    return f.reshape(ns), g.reshape(nt), mapped


def solution(mesh, shape=(Y, Z, C)):
    placed = (P(("row", "col"), None), P("col", None), P("col"))

    def whole(source, target, potential):
        rows, cols = mesh.shape["row"], mesh.shape["col"]
        dims = (rows, *shape, source.shape[0] // (rows * cols), target.shape[0] // cols, source.shape[1],
                source.shape[0], target.shape[0])
        return jax.shard_map(
            functools.partial(local, dims),
            mesh=mesh,
            in_specs=placed,
            out_specs=(P(("row", "col")), P("col"), P(("row", "col"), None)),
            check_vma=False,
        )(source, target, potential)

    return whole
```

```python
import functools
import math

import jax
import jax.numpy as jnp
from jax import lax
from jax.experimental import pallas as pl
from jax.experimental.pallas import tpu as pltpu
from jax.sharding import PartitionSpec as P

MESH = pl.DeviceIdType.MESH
EPS = 0.02
LOG2E = 1.0 / math.log(2.0)
F32 = jnp.float32
BF16 = jnp.bfloat16

Y, Z, C = 4, 8, 2
LOW = -1e30
VMEM = 48 * 1024 * 1024
W, EXTRA = 128, 16


def split2(x):
    hi = x.astype(BF16)
    return hi, (x - hi.astype(F32)).astype(BF16)


def split3(x):
    hi = x.astype(BF16).astype(F32)
    mid = (x - hi).astype(BF16).astype(F32)
    return hi, mid, x - hi - mid


def nt_dot(a, b):
    return lax.dot_general(a, b, (((1,), (1,)), ((), ())), preferred_element_type=F32)


def squares(rows):
    both = jnp.concatenate(split2(jnp.square(rows.astype(F32))), axis=1)
    ones = jnp.ones((8, both.shape[1]), BF16)
    return nt_dot(ones, both)[0:1, :]


def kernel(dims, src, tgt, pot, f_out, g_out, map_out, tbuf, abuf, sbuf, pbuf, ta, uall, lbc, col_a, col_b, top_a, top_b, macc, sacc, lrow, lfin,
           mstage, sstage, mcol, lcol, xbuf, zsend, zbuf, wrep, e2, acc, plan, nsend, nrecv, i_sem, a_send, a_recv, t_send, t_recv, s_send, s_recv,
           r_send, r_recv, x_send, x_recv, z_send, z_recv, n_send, n_recv):
    X, Y, Z, C, ns, nt, D, all_s, all_t = dims
    G = Y * C
    Q = nt // W
    CH = Z * W
    SCALE = LOG2E / (D * EPS)
    x = lax.axis_index("row")
    col = lax.axis_index("col")
    y = col // (Z * C)
    z = (col // C) % Z
    c = col % C

    def dev(xx, yy, zz, cc):
        return {"row": xx, "col": (yy * Z + zz) * C + cc}

    def remote(a, b, send, recv, to):
        cp = pltpu.make_async_remote_copy(
            src_ref=a, dst_ref=b, send_sem=send, recv_sem=recv, device_id=to, device_id_type=MESH)
        cp.start()
        return cp

    def lse(items):
        top = functools.reduce(jnp.maximum, items)
        total = functools.reduce(jnp.add, [jnp.exp2((i - top) * SCALE) for i in items])
        return top + jnp.log2(total) * (1.0 / SCALE)

    group = [(dy, dc) for dy in range(Y) for dc in range(C) if (dy, dc) != (0, 0)]

    def group_dev(dy, dc):
        return dev(x, (y + dy) % Y, z, (c + dc) % C)

    place = y * C + c

    barrier = pltpu.get_barrier_semaphore()
    peers = [group_dev(*g) for g in group]
    peers += [dev((x + d) % X, y, z, c) for d in range(1, X)]
    peers += [dev(x, y, (z + d) % Z, c) for d in range(1, Z)]
    for peer in peers:
        pl.semaphore_signal(barrier, inc=1, device_id=peer, device_id_type=MESH)
    fetch = [pltpu.make_async_copy(tgt.at[pl.ds(q * W, W), :], tbuf.at[0, pl.ds(q * W, W), :], i_sem.at[q]) for q in range(Q)]
    fetch.append(pltpu.make_async_copy(pot, pbuf, i_sem.at[Q]))
    fetch.append(pltpu.make_async_copy(src, sbuf.at[place], i_sem.at[Q + 1]))
    for cp in fetch:
        cp.start()
    macc[...] = jnp.full(macc.shape, LOW, F32)
    sacc[...] = jnp.zeros(sacc.shape, F32)
    ta[:, D:2 * D] = jnp.ones((Z * nt, D), BF16)
    pl.semaphore_wait(barrier, len(peers))

    s_copies = [remote(src, sbuf.at[place], s_send.at[i], s_recv.at[i], group_dev(*g)) for i, g in enumerate(group)]

    H = Z // 2
    half = nt // 2
    t_copies = {}

    def side(d):
        return dev(x, y, (z + d) % Z, c)

    own_piece = pl.ds(pl.multiple_of(x * W, W), W)

    def to_z(r, k, a, b):
        t_copies[r, k] = remote(a, b, t_send.at[r * Q + k], t_recv.at[r * Q + k], side(Z - r))

    for r in (3, Z - 3):
        to_z(r, 0, tgt.at[own_piece, :], tbuf.at[r, own_piece, :])
    for h in range(2):
        rows = pl.ds(h * half, half)
        for r in (1, Z - 1):
            to_z(r, h, tgt.at[rows, :], tbuf.at[r, rows, :])

    def pass_on(r, h):
        t_copies[r, h].wait_recv()
        rows = pl.ds(h * half, half)
        there = 2 if r == 1 else Z - 2
        t_copies[there, h] = remote(
            tbuf.at[r, rows, :], tbuf.at[there, rows, :], t_send.at[there * Q + h], t_recv.at[there * Q + h],
            side(Z - 1 if r == 1 else 1))

    def half_way():
        have = jnp.where(c == 0, Z - 3, 3)
        to = jnp.where(c == 0, (z + 1) % Z, (z + Z - 1) % Z)
        t_copies[H, 0] = remote(
            tbuf.at[have, own_piece, :], tbuf.at[H, own_piece, :], t_send.at[H * Q], t_recv.at[H * Q], dev(x, y, to, c))

    def spread(r):
        t_copies[r, 0].wait_recv()
        for d in range(1, X):
            k = r * Q + d
            t_copies[r, d] = remote(
                tbuf.at[r, own_piece, :], tbuf.at[r, own_piece, :], t_send.at[k], t_recv.at[k], dev((x + d) % X, y, z, c))

    for cp in fetch:
        cp.wait()
    own_sq = [squares(tbuf[0, q * W:(q + 1) * W, :]) for q in range(Q)]
    offset = jnp.concatenate([pbuf[0:1, q * W:(q + 1) * W] * float(D) - 0.5 * own_sq[q] for q in range(Q)], axis=0)
    abuf[0] = jnp.concatenate(list(split3(offset)) + [jnp.zeros((EXTRA - 3 * Q, W), F32)], axis=0).astype(BF16)
    a_copies = [
        remote(abuf.at[0], abuf.at[r], a_send.at[r - 1], a_recv.at[r - 1], dev(x, y, (z + Z - r) % Z, c)) for r in range(1, Z)]

    spread(3)
    spread(Z - 3)
    half_way()

    for cp in s_copies:
        cp.wait_recv()

    RC = 32
    RP = G // 2

    def fold(rows, pieces):
        pieces = [uall[rows, slot * nt + q * W:slot * nt + (q + 1) * W] + offset for slot, q, offset in pieces]
        old = macc[rows, :]
        top = functools.reduce(jnp.maximum, pieces, old)
        total = sacc[rows, :] * jnp.exp2((old - top) * SCALE)
        for piece in pieces:
            total = total + jnp.exp2((piece - top) * SCALE)
        macc[rows, :] = top
        sacc[rows, :] = total

    def row_pass(slots, first=0, last=Q):
        pieces = []
        for slot in slots:
            parts = abuf[slot].astype(F32)
            offsets = parts[0:Q, :] + parts[Q:2 * Q, :] + parts[2 * Q:3 * Q, :]
            for q in range(first, last):
                at = q * CH + slot * W
                ta[at:at + W, 0:D] = tbuf[slot, q * W:(q + 1) * W, :]
                pieces.append((slot, q, offsets[q:q + 1, :]))
        for p in range(0, G + RP, RP):
            if p < G:
                for slot in slots:
                    uall[p * ns:(p + RP) * ns, slot * nt + first * W:slot * nt + last * W] = nt_dot(
                        sbuf[p:p + RP].reshape(RP * ns, D), tbuf[slot, first * W:last * W, :])
            if p > 0:
                for j in range((p - RP) * ns, p * ns, RC):
                    fold(slice(j, j + RC), pieces)

    def arrived(slot, k):
        if (slot, k) in t_copies:
            t_copies[slot, k].wait_recv()

    pass_on(1, 0)
    pass_on(Z - 1, 0)
    row_pass([0])
    spread(H)
    pass_on(1, 1)
    pass_on(Z - 1, 1)
    for cp in a_copies:
        cp.wait_recv()
    row_pass([1, Z - 1])
    for slot in (3, Z - 3):
        for d in range(1, X):
            arrived(slot, d)
    row_pass([3, Z - 3])
    for h in range(2):
        arrived(2, h)
        arrived(Z - 2, h)
        row_pass([2, Z - 2], h * Q // 2, (h + 1) * Q // 2)
    for d in range(1, X):
        arrived(H, d)
    row_pass([H])

    for p in range(G):
        rows = slice(p * ns, (p + 1) * ns)
        part = (macc[rows, :] + jnp.log2(sacc[rows, :]) * (1.0 / SCALE)).T
        top = jnp.max(part, axis=0, keepdims=True)
        total = jnp.sum(jnp.exp2((part - top) * SCALE), axis=0, keepdims=True)
        lrow[0, p:p + 1, :] = top + jnp.log2(total) * (1.0 / SCALE)
    r_copies = [
        remote(lrow.at[0], lrow.at[i + 1], r_send.at[i], r_recv.at[i], group_dev(*g)) for i, g in enumerate(group)]
    src_sq = squares(sbuf[place])
    for cp in r_copies:
        cp.wait_recv()
    l1 = lse([lrow[i] for i in range(G)])
    lfin[0:G, :] = l1
    for p in range(G):
        lbc[p * ns:(p + 1) * ns, :] = jnp.broadcast_to(l1[p:p + 1, :], (ns, W)).T
    f_out[...] = (0.5 * src_sq - lfin[pl.ds(place, 1), :]) * (1.0 / D) - EPS * math.log(all_s)

    MC = 128
    chunks = G * ns // MC

    def scores(buf, tops, q, slot):
        cols = [slice((slot + i) * nt + q * W, (slot + i) * nt + (q + 1) * W) for i in range(2)]
        top = None
        for i in range(chunks):
            for j in range(0, MC, 32):
                rows = slice(i * MC + j, i * MC + j + 32)
                less = lbc[rows, :]
                u = jnp.concatenate([uall[rows, col] - less for col in cols], axis=1)
                buf[rows, :] = u
                part = jnp.max(u.reshape(4, 8, 2 * W), axis=0)
                top = part if top is None else jnp.maximum(top, part)
            yield
        tops[...] = jnp.broadcast_to(jnp.max(top, axis=0, keepdims=True), (8, 2 * W))
        yield

    def column(buf, tops, slot, at):
        top = tops[...]
        total = jnp.zeros((8, 2 * W), F32)
        for i in range(chunks):
            for j in range(0, MC, 32):
                rows = slice(i * MC + j, i * MC + j + 32)
                e = jnp.exp2((buf[rows, :].reshape(4, 8, 2 * W) - top[None]) * SCALE)
                total = total + jnp.sum(e, axis=0)
                e2[rows, at:at + 2 * W] = e.reshape(32, 2 * W).astype(BF16)
            yield
        total = jnp.broadcast_to(jnp.sum(total, axis=0, keepdims=True), (8, 2 * W))
        for i in range(2):
            mstage[slot + i] = top[:, i * W:(i + 1) * W]
            sstage[slot + i] = total[:, i * W:(i + 1) * W]
        yield

    def together(*steps):
        for _ in zip(*steps):
            pass

    x_copies, z_copies = {}, {}

    tiles = [(q, slot) for q in range(Q) for slot in range(0, Z, 2)]

    def column_chunk(q):
        for n, (tile_q, slot) in enumerate(tiles):
            if tile_q == q:
                here, there = ((col_a, top_a), (col_b, top_b)) if n % 2 == 0 else ((col_b, top_b), (col_a, top_a))
                steps = [column(*here, slot, q * CH + slot * W)]
                if n + 1 < len(tiles):
                    steps.insert(0, scores(*there, *tiles[n + 1]))
                together(*steps)

        mcol[q] = jnp.concatenate([mstage[r, 0:1, :] for r in range(Z)], axis=0)
        total = jnp.concatenate([sstage[r, 0:1, :] for r in range(Z)], axis=0)
        lcol[q] = mcol[q] + jnp.log2(total) * (1.0 / SCALE)
        for d in range(1, X):
            k = q * (X - 1) + d - 1
            x_copies[q, d] = remote(lcol.at[q], xbuf.at[k], x_send.at[k], x_recv.at[k], dev((x + d) % X, y, z, c))

    def across_z(q):
        for d in range(1, X):
            x_copies[q, d].wait_recv()
        zsend[q] = lse([lcol[q]] + [xbuf[q * (X - 1) + d - 1] for d in range(1, X)])
        for d in range(1, Z):
            k = q * (Z - 1) + d - 1
            z_copies[q, d] = remote(zsend.at[q], zbuf.at[k], z_send.at[k], z_recv.at[k], dev(x, y, (z + d) % Z, c))

    def weights(q):
        terms = [zsend[q]]
        for d in range(1, Z):
            z_copies[q, d].wait_recv()
            got = zbuf[q * (Z - 1) + d - 1]
            terms.append(jnp.concatenate([got[d:Z, :], got[0:d, :]], axis=0))
        l2 = lse(terms)
        g_out[0:1, q * W:(q + 1) * W] = (0.5 * own_sq[q] - l2[0:1, :]) * (1.0 / D) + EPS * (math.log(all_s) - math.log(all_t))
        w = jnp.exp2((mcol[q] - l2) * SCALE)
        for r in range(Z):
            wrep[q, :, r * W:(r + 1) * W] = jnp.broadcast_to(w[r:r + 1, :], (16, W)).astype(BF16)

    pair = C * ns

    def weigh(q, rows):
        for i in range(0, rows.size, 64):
            part = pl.ds(rows.start + i, 64)
            plan[part, :] = (e2[part, q * CH:(q + 1) * CH].reshape(4, 16, CH) * wrep[q][None]).reshape(64, CH)

    def weighted(q, rows):
        got = jnp.dot(plan[rows, :], ta[q * CH:(q + 1) * CH, :], preferred_element_type=F32)
        acc[rows, :] = got if q == 0 else acc[rows, :] + got

    def add_chunk(q):
        weights(q)
        weigh(q, pl.ds(0, G * ns))
        for i in range(2):
            weighted(q, pl.ds(i * (G * ns // 2), G * ns // 2))

    together(scores(col_a, top_a, 0, 0))
    for q in range(Q):
        column_chunk(q)
    for q in range(Q):
        across_z(q)
    for q in range(Q - 1):
        add_chunk(q)
    weights(Q - 1)

    eye = lax.broadcasted_iota(jnp.int32, (ns, W), 0) == lax.broadcasted_iota(jnp.int32, (ns, W), 1)
    n_copies = {}
    own = None
    for dy in sorted(range(1, Y), key=lambda d: -min(d, Y - d)) + [0]:
        start = pl.multiple_of(((y + dy) % Y) * pair, pair)
        rows = pl.ds(start, pair)
        weigh(Q - 1, rows)
        weighted(Q - 1, rows)
        for dc in reversed(range(C)):
            rows = pl.ds(pl.multiple_of(start + ((c + dc) % C) * ns, ns), ns)
            num, den = acc[rows, 0:D], acc[rows, D:2 * D]
            den = jnp.sum(jnp.where(eye, den, 0.0), axis=0, keepdims=True)
            if (dy, dc) == (0, 0):
                own = (num, den)
                continue
            i = group.index((dy, dc))
            hi, lo = split2(den)
            nsend[i, 0:ns, :] = num.astype(BF16)
            nsend[i, ns:ns + 16, :] = jnp.concatenate(
                [hi.astype(F32), lo.astype(F32), jnp.zeros((14, W), F32)], axis=0).astype(BF16)
            n_copies[i] = remote(nsend.at[i], nrecv.at[i], n_send.at[i], n_recv.at[i], group_dev(dy, dc))
    for cps in (s_copies, a_copies, t_copies.values(), r_copies, x_copies.values(), z_copies.values()):
        for cp in cps:
            cp.wait_send()
    num, den = own
    for i in n_copies:
        n_copies[i].wait_recv()
        got = nrecv[i].astype(F32)
        num = num + got[0:ns, :]
        den = den + got[ns:ns + 1, :] + got[ns + 1:ns + 2, :]
    den = jnp.broadcast_to(den, (ns, W)).T
    map_out[...] = (num / den).astype(BF16)
    for cp in n_copies.values():
        cp.wait_send()


def write_out(f, g, mapped, f_out, g_out, map_out, sem):
    copies = [
        pltpu.make_async_copy(a, b, sem.at[i]) for i, (a, b) in enumerate(((mapped, map_out), (g, g_out), (f, f_out)))]
    for cp in copies:
        cp.start()
    for cp in copies:
        cp.wait()


def local(dims, source, target, potential):
    X, Y, Z, C, ns, nt, D, all_s, all_t = dims
    G = Y * C
    Q = nt // W
    vm = pltpu.VMEM
    dma = pltpu.SemaphoreType.DMA
    f, g, mapped = pl.pallas_call(
        functools.partial(kernel, dims),
        out_shape=(
            jax.ShapeDtypeStruct((1, ns), F32),
            jax.ShapeDtypeStruct((1, nt), F32),
            jax.ShapeDtypeStruct((ns, D), BF16),
        ),
        in_specs=[pl.BlockSpec(memory_space=pl.ANY)] * 3,
        out_specs=(pl.BlockSpec(memory_space=pltpu.VMEM),) * 3,
        scratch_shapes=[
            vm((Z, nt, D), BF16),
            vm((Z, EXTRA, W), BF16),
            vm((G, ns, D), BF16),
            vm((1, nt), F32),
            vm((Z * nt, 2 * D), BF16),
            vm((G * ns, Z * nt), F32),
            vm((G * ns, W), F32),
            vm((G * ns, 2 * W), F32),
            vm((G * ns, 2 * W), F32),
            vm((8, 2 * W), F32),
            vm((8, 2 * W), F32),
            vm((G * ns, 128), F32),
            vm((G * ns, 128), F32),
            vm((G, G, ns), F32),
            vm((8, ns), F32),
            vm((Z, 8, W), F32),
            vm((Z, 8, W), F32),
            vm((Q, Z, W), F32),
            vm((Q, Z, W), F32),
            vm((Q * (X - 1), Z, W), F32),
            vm((Q, Z, W), F32),
            vm((Q * (Z - 1), Z, W), F32),
            vm((Q, 16, Z * W), BF16),
            vm((G * ns, Z * nt), BF16),
            vm((G * ns, 2 * D), F32),
            vm((G * ns, Z * W), BF16),
            vm((G - 1, ns + 16, D), BF16),
            vm((G - 1, ns + 16, D), BF16),
            dma((Q + 2,)),
            dma((Z - 1,)), dma((Z - 1,)),
            dma((Z * Q,)), dma((Z * Q,)),
            dma((G - 1,)), dma((G - 1,)),
            dma((G - 1,)), dma((G - 1,)),
            dma((Q * (X - 1),)), dma((Q * (X - 1),)),
            dma((Q * (Z - 1),)), dma((Q * (Z - 1),)),
            dma((G - 1,)), dma((G - 1,)),
        ],
        compiler_params=pltpu.CompilerParams(
            collective_id=0, has_side_effects=True, vmem_limit_bytes=VMEM),
        cost_estimate=pl.CostEstimate(flops=6 * 10**9, bytes_accessed=10**6, transcendentals=10**7),
    )(*[pltpu.with_memory_space_constraint(a, pltpu.HBM) for a in (source, target, potential.reshape(1, nt))])
    f, g, mapped = pl.pallas_call(
        write_out,
        out_shape=(
            jax.ShapeDtypeStruct((1, ns), F32),
            jax.ShapeDtypeStruct((1, nt), F32),
            jax.ShapeDtypeStruct((ns, D), BF16),
        ),
        in_specs=[pl.BlockSpec(memory_space=pltpu.VMEM)] * 3,
        out_specs=(pl.BlockSpec(memory_space=pl.ANY),) * 3,
        scratch_shapes=[dma((3,))],
    )(f, g, mapped)
    return f.reshape(ns), g.reshape(nt), mapped


def solution(mesh, shape=(Y, Z, C)):
    placed = (P(("row", "col"), None), P("col", None), P("col"))

    def whole(source, target, potential):
        rows, cols = mesh.shape["row"], mesh.shape["col"]
        dims = (rows, *shape, source.shape[0] // (rows * cols), target.shape[0] // cols, source.shape[1],
                source.shape[0], target.shape[0])
        return jax.shard_map(
            functools.partial(local, dims),
            mesh=mesh,
            in_specs=placed,
            out_specs=(P(("row", "col")), P("col"), P(("row", "col"), None)),
            check_vma=False,
        )(source, target, potential)

    return whole
```

```python
import functools
import math

import jax
import jax.numpy as jnp
from jax import lax
from jax.experimental import pallas as pl
from jax.experimental.pallas import tpu as pltpu
from jax.sharding import PartitionSpec as P

MESH = pl.DeviceIdType.MESH
EPS = 0.02
LOG2E = 1.0 / math.log(2.0)
F32 = jnp.float32
BF16 = jnp.bfloat16

Y, Z, C = 4, 8, 2
LOW = -1e30
VMEM = 48 * 1024 * 1024
W, EXTRA = 128, 16


def split2(x):
    hi = x.astype(BF16)
    return hi, (x - hi.astype(F32)).astype(BF16)


def split3(x):
    hi = x.astype(BF16).astype(F32)
    mid = (x - hi).astype(BF16).astype(F32)
    return hi, mid, x - hi - mid


def nt_dot(a, b):
    return lax.dot_general(a, b, (((1,), (1,)), ((), ())), preferred_element_type=F32)


def squares(rows):
    both = jnp.concatenate(split2(jnp.square(rows.astype(F32))), axis=1)
    ones = jnp.ones((8, both.shape[1]), BF16)
    return nt_dot(ones, both)[0:1, :]


def kernel(dims, src, tgt, pot, f_out, g_out, map_out, tbuf, abuf, sbuf, pbuf, ta, uall, lbc, col_a, col_b, top_a, top_b, macc, sacc, lrow, lfin,
           mstage, sstage, mcol, lcol, xbuf, zsend, zbuf, wrep, e2, acc, plan, nsend, nrecv, i_sem, a_send, a_recv, t_send, t_recv, s_send, s_recv,
           r_send, r_recv, x_send, x_recv, z_send, z_recv, n_send, n_recv):
    X, Y, Z, C, ns, nt, D, all_s, all_t = dims
    G = Y * C
    Q = nt // W
    CH = Z * W
    SCALE = LOG2E / (D * EPS)
    x = lax.axis_index("row")
    col = lax.axis_index("col")
    y = col // (Z * C)
    z = (col // C) % Z
    c = col % C

    def dev(xx, yy, zz, cc):
        return {"row": xx, "col": (yy * Z + zz) * C + cc}

    def remote(a, b, send, recv, to):
        cp = pltpu.make_async_remote_copy(
            src_ref=a, dst_ref=b, send_sem=send, recv_sem=recv, device_id=to, device_id_type=MESH)
        cp.start()
        return cp

    def lse(items):
        top = functools.reduce(jnp.maximum, items)
        total = functools.reduce(jnp.add, [jnp.exp2((i - top) * SCALE) for i in items])
        return top + jnp.log2(total) * (1.0 / SCALE)

    group = [(dy, dc) for dy in range(Y) for dc in range(C) if (dy, dc) != (0, 0)]

    def group_dev(dy, dc):
        return dev(x, (y + dy) % Y, z, (c + dc) % C)

    place = y * C + c

    barrier = pltpu.get_barrier_semaphore()
    peers = [group_dev(*g) for g in group]
    peers += [dev((x + d) % X, y, z, c) for d in range(1, X)]
    peers += [dev(x, y, (z + d) % Z, c) for d in range(1, Z)]
    for peer in peers:
        pl.semaphore_signal(barrier, inc=1, device_id=peer, device_id_type=MESH)
    fetch = [pltpu.make_async_copy(tgt.at[pl.ds(q * W, W), :], tbuf.at[0, pl.ds(q * W, W), :], i_sem.at[q]) for q in range(Q)]
    fetch.append(pltpu.make_async_copy(pot, pbuf, i_sem.at[Q]))
    fetch.append(pltpu.make_async_copy(src, sbuf.at[place], i_sem.at[Q + 1]))
    for cp in fetch:
        cp.start()
    macc[...] = jnp.full(macc.shape, LOW, F32)
    sacc[...] = jnp.zeros(sacc.shape, F32)
    ta[:, D:2 * D] = jnp.ones((Z * nt, D), BF16)
    pl.semaphore_wait(barrier, len(peers))

    s_copies = [remote(src, sbuf.at[place], s_send.at[i], s_recv.at[i], group_dev(*g)) for i, g in enumerate(group)]

    H = Z // 2
    half = nt // 2
    t_copies = {}

    def side(d):
        return dev(x, y, (z + d) % Z, c)

    own_piece = pl.ds(pl.multiple_of(x * W, W), W)

    def to_z(r, k, a, b):
        t_copies[r, k] = remote(a, b, t_send.at[r * Q + k], t_recv.at[r * Q + k], side(Z - r))

    for r in (3, Z - 3):
        to_z(r, 0, tgt.at[own_piece, :], tbuf.at[r, own_piece, :])
    for h in range(2):
        rows = pl.ds(h * half, half)
        for r in (1, Z - 1):
            to_z(r, h, tgt.at[rows, :], tbuf.at[r, rows, :])

    def pass_on(r, h):
        t_copies[r, h].wait_recv()
        rows = pl.ds(h * half, half)
        there = 2 if r == 1 else Z - 2
        t_copies[there, h] = remote(
            tbuf.at[r, rows, :], tbuf.at[there, rows, :], t_send.at[there * Q + h], t_recv.at[there * Q + h],
            side(Z - 1 if r == 1 else 1))

    def half_way():
        have = jnp.where(c == 0, Z - 3, 3)
        to = jnp.where(c == 0, (z + 1) % Z, (z + Z - 1) % Z)
        t_copies[H, 0] = remote(
            tbuf.at[have, own_piece, :], tbuf.at[H, own_piece, :], t_send.at[H * Q], t_recv.at[H * Q], dev(x, y, to, c))

    def spread(r):
        t_copies[r, 0].wait_recv()
        for d in range(1, X):
            k = r * Q + d
            t_copies[r, d] = remote(
                tbuf.at[r, own_piece, :], tbuf.at[r, own_piece, :], t_send.at[k], t_recv.at[k], dev((x + d) % X, y, z, c))

    for cp in fetch:
        cp.wait()
    own_sq = [squares(tbuf[0, q * W:(q + 1) * W, :]) for q in range(Q)]
    offset = jnp.concatenate([pbuf[0:1, q * W:(q + 1) * W] * float(D) - 0.5 * own_sq[q] for q in range(Q)], axis=0)
    abuf[0] = jnp.concatenate(list(split3(offset)) + [jnp.zeros((EXTRA - 3 * Q, W), F32)], axis=0).astype(BF16)
    a_copies = [
        remote(abuf.at[0], abuf.at[r], a_send.at[r - 1], a_recv.at[r - 1], dev(x, y, (z + Z - r) % Z, c)) for r in range(1, Z)]

    spread(3)
    spread(Z - 3)
    half_way()

    for cp in s_copies:
        cp.wait_recv()

    RC = 32
    RP = G // 2

    def fold(rows, pieces):
        pieces = [uall[rows, slot * nt + q * W:slot * nt + (q + 1) * W] + offset for slot, q, offset in pieces]
        old = macc[rows, :]
        top = functools.reduce(jnp.maximum, pieces, old)
        total = sacc[rows, :] * jnp.exp2((old - top) * SCALE)
        for piece in pieces:
            total = total + jnp.exp2((piece - top) * SCALE)
        macc[rows, :] = top
        sacc[rows, :] = total

    def row_pass(slots, first=0, last=Q):
        pieces = []
        for slot in slots:
            parts = abuf[slot].astype(F32)
            offsets = parts[0:Q, :] + parts[Q:2 * Q, :] + parts[2 * Q:3 * Q, :]
            for q in range(first, last):
                at = q * CH + slot * W
                ta[at:at + W, 0:D] = tbuf[slot, q * W:(q + 1) * W, :]
                pieces.append((slot, q, offsets[q:q + 1, :]))
        for p in range(0, G + RP, RP):
            if p < G:
                for slot in slots:
                    uall[p * ns:(p + RP) * ns, slot * nt + first * W:slot * nt + last * W] = nt_dot(
                        sbuf[p:p + RP].reshape(RP * ns, D), tbuf[slot, first * W:last * W, :])
            if p > 0:
                for j in range((p - RP) * ns, p * ns, RC):
                    fold(slice(j, j + RC), pieces)

    def arrived(slot, k):
        if (slot, k) in t_copies:
            t_copies[slot, k].wait_recv()

    pass_on(1, 0)
    pass_on(Z - 1, 0)
    row_pass([0])
    spread(H)
    pass_on(1, 1)
    pass_on(Z - 1, 1)
    for cp in a_copies:
        cp.wait_recv()
    row_pass([1, Z - 1])
    for slot in (3, Z - 3):
        for d in range(1, X):
            arrived(slot, d)
    row_pass([3, Z - 3])
    for h in range(2):
        arrived(2, h)
        arrived(Z - 2, h)
        row_pass([2, Z - 2], h * Q // 2, (h + 1) * Q // 2)
    for d in range(1, X):
        arrived(H, d)
    row_pass([H])

    for p in range(G):
        rows = slice(p * ns, (p + 1) * ns)
        part = (macc[rows, :] + jnp.log2(sacc[rows, :]) * (1.0 / SCALE)).T
        top = jnp.max(part, axis=0, keepdims=True)
        total = jnp.sum(jnp.exp2((part - top) * SCALE), axis=0, keepdims=True)
        lrow[0, p:p + 1, :] = top + jnp.log2(total) * (1.0 / SCALE)
    r_copies = [
        remote(lrow.at[0], lrow.at[i + 1], r_send.at[i], r_recv.at[i], group_dev(*g)) for i, g in enumerate(group)]
    src_sq = squares(sbuf[place])
    for cp in r_copies:
        cp.wait_recv()
    l1 = lse([lrow[i] for i in range(G)])
    lfin[0:G, :] = l1
    for p in range(G):
        lbc[p * ns:(p + 1) * ns, :] = jnp.broadcast_to(l1[p:p + 1, :], (ns, W)).T
    f_out[...] = (0.5 * src_sq - lfin[pl.ds(place, 1), :]) * (1.0 / D) - EPS * math.log(all_s)

    MC = 128
    chunks = G * ns // MC

    def scores(buf, tops, q, slot):
        cols = [slice((slot + i) * nt + q * W, (slot + i) * nt + (q + 1) * W) for i in range(2)]
        top = None
        for i in range(chunks):
            for j in range(0, MC, 32):
                rows = slice(i * MC + j, i * MC + j + 32)
                less = lbc[rows, :]
                u = jnp.concatenate([uall[rows, col] - less for col in cols], axis=1)
                buf[rows, :] = u
                part = jnp.max(u.reshape(4, 8, 2 * W), axis=0)
                top = part if top is None else jnp.maximum(top, part)
            yield
        tops[...] = jnp.broadcast_to(jnp.max(top, axis=0, keepdims=True), (8, 2 * W))
        yield

    def column(buf, tops, slot, at):
        top = tops[...]
        total = jnp.zeros((8, 2 * W), F32)
        for i in range(chunks):
            for j in range(0, MC, 32):
                rows = slice(i * MC + j, i * MC + j + 32)
                e = jnp.exp2((buf[rows, :].reshape(4, 8, 2 * W) - top[None]) * SCALE)
                total = total + jnp.sum(e, axis=0)
                e2[rows, at:at + 2 * W] = e.reshape(32, 2 * W).astype(BF16)
            yield
        total = jnp.broadcast_to(jnp.sum(total, axis=0, keepdims=True), (8, 2 * W))
        for i in range(2):
            mstage[slot + i] = top[:, i * W:(i + 1) * W]
            sstage[slot + i] = total[:, i * W:(i + 1) * W]
        yield

    def together(*steps):
        for _ in zip(*steps):
            pass

    x_copies, z_copies = {}, {}

    tiles = [(q, slot) for q in range(Q) for slot in range(0, Z, 2)]

    def column_chunk(q):
        for n, (tile_q, slot) in enumerate(tiles):
            if tile_q == q:
                here, there = ((col_a, top_a), (col_b, top_b)) if n % 2 == 0 else ((col_b, top_b), (col_a, top_a))
                steps = [column(*here, slot, q * CH + slot * W)]
                if n + 1 < len(tiles):
                    steps.insert(0, scores(*there, *tiles[n + 1]))
                together(*steps)

        mcol[q] = jnp.concatenate([mstage[r, 0:1, :] for r in range(Z)], axis=0)
        total = jnp.concatenate([sstage[r, 0:1, :] for r in range(Z)], axis=0)
        lcol[q] = mcol[q] + jnp.log2(total) * (1.0 / SCALE)
        for d in range(1, X):
            k = q * (X - 1) + d - 1
            x_copies[q, d] = remote(lcol.at[q], xbuf.at[k], x_send.at[k], x_recv.at[k], dev((x + d) % X, y, z, c))

    def across_z(q):
        for d in range(1, X):
            x_copies[q, d].wait_recv()
        zsend[q] = lse([lcol[q]] + [xbuf[q * (X - 1) + d - 1] for d in range(1, X)])
        for d in range(1, Z):
            k = q * (Z - 1) + d - 1
            z_copies[q, d] = remote(zsend.at[q], zbuf.at[k], z_send.at[k], z_recv.at[k], dev(x, y, (z + d) % Z, c))

    def weights(q):
        terms = [zsend[q]]
        for d in range(1, Z):
            z_copies[q, d].wait_recv()
            got = zbuf[q * (Z - 1) + d - 1]
            terms.append(jnp.concatenate([got[d:Z, :], got[0:d, :]], axis=0))
        l2 = lse(terms)
        g_out[0:1, q * W:(q + 1) * W] = (0.5 * own_sq[q] - l2[0:1, :]) * (1.0 / D) + EPS * (math.log(all_s) - math.log(all_t))
        w = jnp.exp2((mcol[q] - l2) * SCALE)
        for r in range(Z):
            wrep[q, :, r * W:(r + 1) * W] = jnp.broadcast_to(w[r:r + 1, :], (16, W)).astype(BF16)

    pair = C * ns

    def weigh(q, rows):
        for i in range(0, rows.size, 64):
            part = pl.ds(rows.start + i, 64)
            plan[part, :] = (e2[part, q * CH:(q + 1) * CH].reshape(4, 16, CH) * wrep[q][None]).reshape(64, CH)

    def weighted(q, rows):
        got = jnp.dot(plan[rows, :], ta[q * CH:(q + 1) * CH, :], preferred_element_type=F32)
        acc[rows, :] = got if q == 0 else acc[rows, :] + got

    def add_chunk(q):
        weights(q)
        weigh(q, pl.ds(0, G * ns))
        for i in range(2):
            weighted(q, pl.ds(i * (G * ns // 2), G * ns // 2))

    together(scores(col_a, top_a, 0, 0))
    for q in range(Q):
        column_chunk(q)
    for q in range(Q):
        across_z(q)
    for q in range(Q - 1):
        add_chunk(q)
    weights(Q - 1)

    eye = lax.broadcasted_iota(jnp.int32, (ns, W), 0) == lax.broadcasted_iota(jnp.int32, (ns, W), 1)
    n_copies = {}
    own = None
    for dy in sorted(range(1, Y), key=lambda d: -min(d, Y - d)) + [0]:
        start = pl.multiple_of(((y + dy) % Y) * pair, pair)
        rows = pl.ds(start, pair)
        weigh(Q - 1, rows)
        weighted(Q - 1, rows)
        for dc in reversed(range(C)):
            rows = pl.ds(pl.multiple_of(start + ((c + dc) % C) * ns, ns), ns)
            num, den = acc[rows, 0:D], acc[rows, D:2 * D]
            den = jnp.sum(jnp.where(eye, den, 0.0), axis=0, keepdims=True)
            if (dy, dc) == (0, 0):
                own = (num, den)
                continue
            i = group.index((dy, dc))
            hi, lo = split2(den)
            nsend[i, 0:ns, :] = num.astype(BF16)
            nsend[i, ns:ns + 16, :] = jnp.concatenate(
                [hi.astype(F32), lo.astype(F32), jnp.zeros((14, W), F32)], axis=0).astype(BF16)
            n_copies[i] = remote(nsend.at[i], nrecv.at[i], n_send.at[i], n_recv.at[i], group_dev(dy, dc))
    for cps in (s_copies, a_copies, t_copies.values(), r_copies, x_copies.values(), z_copies.values()):
        for cp in cps:
            cp.wait_send()
    num, den = own
    for i in n_copies:
        n_copies[i].wait_recv()
        got = nrecv[i].astype(F32)
        num = num + got[0:ns, :]
        den = den + got[ns:ns + 1, :] + got[ns + 1:ns + 2, :]
    den = jnp.broadcast_to(den, (ns, W)).T
    map_out[...] = (num / den).astype(BF16)
    for cp in n_copies.values():
        cp.wait_send()


def write_out(f, g, mapped, f_out, g_out, map_out, sem):
    copies = [
        pltpu.make_async_copy(a, b, sem.at[i]) for i, (a, b) in enumerate(((mapped, map_out), (g, g_out), (f, f_out)))]
    for cp in copies:
        cp.start()
    for cp in copies:
        cp.wait()


def local(dims, source, target, potential):
    X, Y, Z, C, ns, nt, D, all_s, all_t = dims
    G = Y * C
    Q = nt // W
    vm = pltpu.VMEM
    dma = pltpu.SemaphoreType.DMA
    f, g, mapped = pl.pallas_call(
        functools.partial(kernel, dims),
        out_shape=(
            jax.ShapeDtypeStruct((1, ns), F32),
            jax.ShapeDtypeStruct((1, nt), F32),
            jax.ShapeDtypeStruct((ns, D), BF16),
        ),
        in_specs=[pl.BlockSpec(memory_space=pl.ANY)] * 3,
        out_specs=(pl.BlockSpec(memory_space=pltpu.VMEM),) * 3,
        scratch_shapes=[
            vm((Z, nt, D), BF16),
            vm((Z, EXTRA, W), BF16),
            vm((G, ns, D), BF16),
            vm((1, nt), F32),
            vm((Z * nt, 2 * D), BF16),
            vm((G * ns, Z * nt), F32),
            vm((G * ns, W), F32),
            vm((G * ns, 2 * W), F32),
            vm((G * ns, 2 * W), F32),
            vm((8, 2 * W), F32),
            vm((8, 2 * W), F32),
            vm((G * ns, 128), F32),
            vm((G * ns, 128), F32),
            vm((G, G, ns), F32),
            vm((8, ns), F32),
            vm((Z, 8, W), F32),
            vm((Z, 8, W), F32),
            vm((Q, Z, W), F32),
            vm((Q, Z, W), F32),
            vm((Q * (X - 1), Z, W), F32),
            vm((Q, Z, W), F32),
            vm((Q * (Z - 1), Z, W), F32),
            vm((Q, 16, Z * W), BF16),
            vm((G * ns, Z * nt), BF16),
            vm((G * ns, 2 * D), F32),
            vm((G * ns, Z * W), BF16),
            vm((G - 1, ns + 16, D), BF16),
            vm((G - 1, ns + 16, D), BF16),
            dma((Q + 2,)),
            dma((Z - 1,)), dma((Z - 1,)),
            dma((Z * Q,)), dma((Z * Q,)),
            dma((G - 1,)), dma((G - 1,)),
            dma((G - 1,)), dma((G - 1,)),
            dma((Q * (X - 1),)), dma((Q * (X - 1),)),
            dma((Q * (Z - 1),)), dma((Q * (Z - 1),)),
            dma((G - 1,)), dma((G - 1,)),
        ],
        compiler_params=pltpu.CompilerParams(
            collective_id=0, has_side_effects=True, vmem_limit_bytes=VMEM),
        cost_estimate=pl.CostEstimate(flops=6 * 10**9, bytes_accessed=10**6, transcendentals=10**7),
    )(*[pltpu.with_memory_space_constraint(a, pltpu.HBM) for a in (source, target, potential.reshape(1, nt))])
    f, g, mapped = pl.pallas_call(
        write_out,
        out_shape=(
            jax.ShapeDtypeStruct((1, ns), F32),
            jax.ShapeDtypeStruct((1, nt), F32),
            jax.ShapeDtypeStruct((ns, D), BF16),
        ),
        in_specs=[pl.BlockSpec(memory_space=pltpu.VMEM)] * 3,
        out_specs=(pl.BlockSpec(memory_space=pl.ANY),) * 3,
        scratch_shapes=[dma((3,))],
        compiler_params=pltpu.CompilerParams(vmem_limit_bytes=1024 * 1024),
    )(f, g, mapped)
    return f.reshape(ns), g.reshape(nt), mapped


def solution(mesh, shape=(Y, Z, C)):
    placed = (P(("row", "col"), None), P("col", None), P("col"))

    def whole(source, target, potential):
        rows, cols = mesh.shape["row"], mesh.shape["col"]
        dims = (rows, *shape, source.shape[0] // (rows * cols), target.shape[0] // cols, source.shape[1],
                source.shape[0], target.shape[0])
        return jax.shard_map(
            functools.partial(local, dims),
            mesh=mesh,
            in_specs=placed,
            out_specs=(P(("row", "col")), P("col"), P(("row", "col"), None)),
            check_vma=False,
        )(source, target, potential)

    return whole
```

```python
import functools
import math

import jax
import jax.numpy as jnp
from jax import lax
from jax.experimental import pallas as pl
from jax.experimental.pallas import tpu as pltpu
from jax.sharding import PartitionSpec as P

MESH = pl.DeviceIdType.MESH
EPS = 0.02
LOG2E = 1.0 / math.log(2.0)
F32 = jnp.float32
BF16 = jnp.bfloat16

Y, Z, C = 4, 8, 2
LOW = -1e30
VMEM = 48 * 1024 * 1024
W, EXTRA = 128, 16


def split2(x):
    hi = x.astype(BF16)
    return hi, (x - hi.astype(F32)).astype(BF16)


def split3(x):
    hi = x.astype(BF16).astype(F32)
    mid = (x - hi).astype(BF16).astype(F32)
    return hi, mid, x - hi - mid


def nt_dot(a, b):
    return lax.dot_general(a, b, (((1,), (1,)), ((), ())), preferred_element_type=F32)


def squares(rows):
    both = jnp.concatenate(split2(jnp.square(rows.astype(F32))), axis=1)
    ones = jnp.ones((8, both.shape[1]), BF16)
    return nt_dot(ones, both)[0:1, :]


def kernel(dims, src, tgt, pot, f_out, g_out, map_out, tbuf, abuf, sbuf, pbuf, ta, uall, lbc, col_a, col_b, top_a, top_b, macc, sacc, lrow, lfin,
           mstage, sstage, mcol, lcol, xbuf, zsend, zbuf, wrep, e2, acc, plan, nsend, nrecv, i_sem, a_send, a_recv, t_send, t_recv, s_send, s_recv,
           r_send, r_recv, x_send, x_recv, z_send, z_recv, n_send, n_recv):
    X, Y, Z, C, ns, nt, D, all_s, all_t = dims
    G = Y * C
    Q = nt // W
    CH = Z * W
    SCALE = LOG2E / (D * EPS)
    x = lax.axis_index("row")
    col = lax.axis_index("col")
    y = col // (Z * C)
    z = (col // C) % Z
    c = col % C

    def dev(xx, yy, zz, cc):
        return {"row": xx, "col": (yy * Z + zz) * C + cc}

    def remote(a, b, send, recv, to):
        cp = pltpu.make_async_remote_copy(
            src_ref=a, dst_ref=b, send_sem=send, recv_sem=recv, device_id=to, device_id_type=MESH)
        cp.start()
        return cp

    def lse(items):
        top = functools.reduce(jnp.maximum, items)
        total = functools.reduce(jnp.add, [jnp.exp2(i - top) for i in items])
        return top + jnp.log2(total)

    group = [(dy, dc) for dy in range(Y) for dc in range(C) if (dy, dc) != (0, 0)]

    def group_dev(dy, dc):
        return dev(x, (y + dy) % Y, z, (c + dc) % C)

    place = y * C + c

    barrier = pltpu.get_barrier_semaphore()
    peers = [group_dev(*g) for g in group]
    peers += [dev((x + d) % X, y, z, c) for d in range(1, X)]
    peers += [dev(x, y, (z + d) % Z, c) for d in range(1, Z)]
    for peer in peers:
        pl.semaphore_signal(barrier, inc=1, device_id=peer, device_id_type=MESH)
    fetch = [pltpu.make_async_copy(tgt.at[pl.ds(q * W, W), :], tbuf.at[0, pl.ds(q * W, W), :], i_sem.at[q]) for q in range(Q)]
    fetch.append(pltpu.make_async_copy(pot, pbuf, i_sem.at[Q]))
    fetch.append(pltpu.make_async_copy(src, sbuf.at[place], i_sem.at[Q + 1]))
    for cp in fetch:
        cp.start()
    macc[...] = jnp.full(macc.shape, LOW, F32)
    sacc[...] = jnp.zeros(sacc.shape, F32)
    ta[:, D:2 * D] = jnp.ones((Z * nt, D), BF16)
    pl.semaphore_wait(barrier, len(peers))

    s_copies = [remote(src, sbuf.at[place], s_send.at[i], s_recv.at[i], group_dev(*g)) for i, g in enumerate(group)]

    H = Z // 2
    half = nt // 2
    t_copies = {}

    def side(d):
        return dev(x, y, (z + d) % Z, c)

    own_piece = pl.ds(pl.multiple_of(x * W, W), W)

    def to_z(r, k, a, b):
        t_copies[r, k] = remote(a, b, t_send.at[r * Q + k], t_recv.at[r * Q + k], side(Z - r))

    for r in (3, Z - 3):
        to_z(r, 0, tgt.at[own_piece, :], tbuf.at[r, own_piece, :])
    for h in range(2):
        rows = pl.ds(h * half, half)
        for r in (1, Z - 1):
            to_z(r, h, tgt.at[rows, :], tbuf.at[r, rows, :])

    def pass_on(r, h):
        t_copies[r, h].wait_recv()
        rows = pl.ds(h * half, half)
        there = 2 if r == 1 else Z - 2
        t_copies[there, h] = remote(
            tbuf.at[r, rows, :], tbuf.at[there, rows, :], t_send.at[there * Q + h], t_recv.at[there * Q + h],
            side(Z - 1 if r == 1 else 1))

    def half_way():
        have = jnp.where(c == 0, Z - 3, 3)
        to = jnp.where(c == 0, (z + 1) % Z, (z + Z - 1) % Z)
        t_copies[H, 0] = remote(
            tbuf.at[have, own_piece, :], tbuf.at[H, own_piece, :], t_send.at[H * Q], t_recv.at[H * Q], dev(x, y, to, c))

    def spread(r):
        t_copies[r, 0].wait_recv()
        for d in range(1, X):
            k = r * Q + d
            t_copies[r, d] = remote(
                tbuf.at[r, own_piece, :], tbuf.at[r, own_piece, :], t_send.at[k], t_recv.at[k], dev((x + d) % X, y, z, c))

    for cp in fetch:
        cp.wait()
    own_sq = [squares(tbuf[0, q * W:(q + 1) * W, :]) for q in range(Q)]
    offset = jnp.concatenate([pbuf[0:1, q * W:(q + 1) * W] * float(D) - 0.5 * own_sq[q] for q in range(Q)], axis=0)
    abuf[0] = jnp.concatenate(list(split3(offset)) + [jnp.zeros((EXTRA - 3 * Q, W), F32)], axis=0).astype(BF16)
    a_copies = [
        remote(abuf.at[0], abuf.at[r], a_send.at[r - 1], a_recv.at[r - 1], dev(x, y, (z + Z - r) % Z, c)) for r in range(1, Z)]

    spread(3)
    spread(Z - 3)
    half_way()

    for cp in s_copies:
        cp.wait_recv()

    RC = 32
    RP = G // 2

    def fold(rows, pieces):
        kept = []
        for slot, q, offset in pieces:
            cols = slice(slot * nt + q * W, slot * nt + (q + 1) * W)
            u = uall[rows, cols] * SCALE
            uall[rows, cols] = u
            kept.append(u + offset)
        old = macc[rows, :]
        top = functools.reduce(jnp.maximum, kept, old)
        total = sacc[rows, :] * jnp.exp2(old - top)
        for piece in kept:
            total = total + jnp.exp2(piece - top)
        macc[rows, :] = top
        sacc[rows, :] = total

    def row_pass(slots, first=0, last=Q):
        pieces = []
        for slot in slots:
            parts = abuf[slot].astype(F32)
            offsets = (parts[0:Q, :] + parts[Q:2 * Q, :] + parts[2 * Q:3 * Q, :]) * SCALE
            for q in range(first, last):
                at = q * CH + slot * W
                ta[at:at + W, 0:D] = tbuf[slot, q * W:(q + 1) * W, :]
                pieces.append((slot, q, offsets[q:q + 1, :]))
        for p in range(0, G + RP, RP):
            if p < G:
                for slot in slots:
                    uall[p * ns:(p + RP) * ns, slot * nt + first * W:slot * nt + last * W] = nt_dot(
                        sbuf[p:p + RP].reshape(RP * ns, D), tbuf[slot, first * W:last * W, :])
            if p > 0:
                for j in range((p - RP) * ns, p * ns, RC):
                    fold(slice(j, j + RC), pieces)

    def arrived(slot, k):
        if (slot, k) in t_copies:
            t_copies[slot, k].wait_recv()

    pass_on(1, 0)
    pass_on(Z - 1, 0)
    row_pass([0])
    spread(H)
    pass_on(1, 1)
    pass_on(Z - 1, 1)
    for cp in a_copies:
        cp.wait_recv()
    row_pass([1, Z - 1])
    for slot in (3, Z - 3):
        for d in range(1, X):
            arrived(slot, d)
    row_pass([3, Z - 3])
    for h in range(2):
        arrived(2, h)
        arrived(Z - 2, h)
        row_pass([2, Z - 2], h * Q // 2, (h + 1) * Q // 2)
    for d in range(1, X):
        arrived(H, d)
    row_pass([H])

    for p in range(G):
        rows = slice(p * ns, (p + 1) * ns)
        part = (macc[rows, :] + jnp.log2(sacc[rows, :])).T
        top = jnp.max(part, axis=0, keepdims=True)
        total = jnp.sum(jnp.exp2(part - top), axis=0, keepdims=True)
        lrow[0, p:p + 1, :] = top + jnp.log2(total)
    r_copies = [
        remote(lrow.at[0], lrow.at[i + 1], r_send.at[i], r_recv.at[i], group_dev(*g)) for i, g in enumerate(group)]
    src_sq = squares(sbuf[place])
    for cp in r_copies:
        cp.wait_recv()
    l1 = lse([lrow[i] for i in range(G)])
    lfin[0:G, :] = l1
    for p in range(G):
        lbc[p * ns:(p + 1) * ns, :] = jnp.broadcast_to(l1[p:p + 1, :], (ns, W)).T
    f_out[...] = (0.5 * src_sq - lfin[pl.ds(place, 1), :] * (1.0 / SCALE)) * (1.0 / D) - EPS * math.log(all_s)

    MC = 128
    chunks = G * ns // MC

    def scores(buf, tops, q, slot):
        cols = [slice((slot + i) * nt + q * W, (slot + i) * nt + (q + 1) * W) for i in range(2)]
        top = None
        for i in range(chunks):
            for j in range(0, MC, 32):
                rows = slice(i * MC + j, i * MC + j + 32)
                less = lbc[rows, :]
                u = jnp.concatenate([uall[rows, col] - less for col in cols], axis=1)
                buf[rows, :] = u
                part = jnp.max(u.reshape(4, 8, 2 * W), axis=0)
                top = part if top is None else jnp.maximum(top, part)
            yield
        tops[...] = jnp.broadcast_to(jnp.max(top, axis=0, keepdims=True), (8, 2 * W))
        yield

    def column(buf, tops, slot, at):
        top = tops[...]
        total = jnp.zeros((8, 2 * W), F32)
        for i in range(chunks):
            for j in range(0, MC, 32):
                rows = slice(i * MC + j, i * MC + j + 32)
                e = jnp.exp2(buf[rows, :].reshape(4, 8, 2 * W) - top[None])
                total = total + jnp.sum(e, axis=0)
                e2[rows, at:at + 2 * W] = e.reshape(32, 2 * W).astype(BF16)
            yield
        total = jnp.broadcast_to(jnp.sum(total, axis=0, keepdims=True), (8, 2 * W))
        for i in range(2):
            mstage[slot + i] = top[:, i * W:(i + 1) * W]
            sstage[slot + i] = total[:, i * W:(i + 1) * W]
        yield

    def together(*steps):
        for _ in zip(*steps):
            pass

    x_copies, z_copies = {}, {}

    tiles = [(q, slot) for q in range(Q) for slot in range(0, Z, 2)]

    def column_chunk(q):
        for n, (tile_q, slot) in enumerate(tiles):
            if n == len(tiles) - 2 and tile_q == q:
                across_z(0)
            if tile_q == q:
                here, there = ((col_a, top_a), (col_b, top_b)) if n % 2 == 0 else ((col_b, top_b), (col_a, top_a))
                steps = [column(*here, slot, q * CH + slot * W)]
                if n + 1 < len(tiles):
                    steps.insert(0, scores(*there, *tiles[n + 1]))
                together(*steps)

        mcol[q] = jnp.concatenate([mstage[r, 0:1, :] for r in range(Z)], axis=0)
        total = jnp.concatenate([sstage[r, 0:1, :] for r in range(Z)], axis=0)
        lcol[q] = mcol[q] + jnp.log2(total)
        for d in range(1, X):
            k = q * (X - 1) + d - 1
            x_copies[q, d] = remote(lcol.at[q], xbuf.at[k], x_send.at[k], x_recv.at[k], dev((x + d) % X, y, z, c))

    def across_z(q):
        for d in range(1, X):
            x_copies[q, d].wait_recv()
        zsend[q] = lse([lcol[q]] + [xbuf[q * (X - 1) + d - 1] for d in range(1, X)])
        for d in range(1, Z):
            k = q * (Z - 1) + d - 1
            z_copies[q, d] = remote(zsend.at[q], zbuf.at[k], z_send.at[k], z_recv.at[k], dev(x, y, (z + d) % Z, c))

    def weights(q):
        terms = [zsend[q]]
        for d in range(1, Z):
            z_copies[q, d].wait_recv()
            got = zbuf[q * (Z - 1) + d - 1]
            terms.append(jnp.concatenate([got[d:Z, :], got[0:d, :]], axis=0))
        l2 = lse(terms)
        g_out[0:1, q * W:(q + 1) * W] = (0.5 * own_sq[q] - l2[0:1, :] * (1.0 / SCALE)) * (1.0 / D) + EPS * (
            math.log(all_s) - math.log(all_t))
        w = jnp.exp2(mcol[q] - l2)
        for r in range(Z):
            wrep[q, :, r * W:(r + 1) * W] = jnp.broadcast_to(w[r:r + 1, :], (16, W)).astype(BF16)

    pair = C * ns

    def weigh(q, rows):
        for i in range(0, rows.size, 64):
            part = pl.ds(rows.start + i, 64)
            plan[part, :] = (e2[part, q * CH:(q + 1) * CH].reshape(4, 16, CH) * wrep[q][None]).reshape(64, CH)

    def weighted(q, rows):
        got = jnp.dot(plan[rows, :], ta[q * CH:(q + 1) * CH, :], preferred_element_type=F32)
        acc[rows, :] = got if q == 0 else acc[rows, :] + got

    def add_chunk(q):
        weights(q)
        weigh(q, pl.ds(0, G * ns))
        for i in range(2):
            weighted(q, pl.ds(i * (G * ns // 2), G * ns // 2))

    together(scores(col_a, top_a, 0, 0))
    for q in range(Q):
        column_chunk(q)
    for q in range(1, Q):
        across_z(q)
    for q in range(Q - 1):
        add_chunk(q)
    weights(Q - 1)

    eye = lax.broadcasted_iota(jnp.int32, (ns, W), 0) == lax.broadcasted_iota(jnp.int32, (ns, W), 1)
    n_copies = {}
    own = None
    for dy in sorted(range(1, Y), key=lambda d: -min(d, Y - d)) + [0]:
        start = pl.multiple_of(((y + dy) % Y) * pair, pair)
        rows = pl.ds(start, pair)
        weigh(Q - 1, rows)
        weighted(Q - 1, rows)
        for dc in reversed(range(C)):
            rows = pl.ds(pl.multiple_of(start + ((c + dc) % C) * ns, ns), ns)
            num, den = acc[rows, 0:D], acc[rows, D:2 * D]
            den = jnp.sum(jnp.where(eye, den, 0.0), axis=0, keepdims=True)
            if (dy, dc) == (0, 0):
                own = (num, den)
                continue
            i = group.index((dy, dc))
            hi, lo = split2(den)
            nsend[i, 0:ns, :] = num.astype(BF16)
            nsend[i, ns:ns + 16, :] = jnp.concatenate(
                [hi.astype(F32), lo.astype(F32), jnp.zeros((14, W), F32)], axis=0).astype(BF16)
            n_copies[i] = remote(nsend.at[i], nrecv.at[i], n_send.at[i], n_recv.at[i], group_dev(dy, dc))
    for cps in (s_copies, a_copies, t_copies.values(), r_copies, x_copies.values(), z_copies.values()):
        for cp in cps:
            cp.wait_send()
    num, den = own
    for i in n_copies:
        n_copies[i].wait_recv()
        got = nrecv[i].astype(F32)
        num = num + got[0:ns, :]
        den = den + got[ns:ns + 1, :] + got[ns + 1:ns + 2, :]
    den = jnp.broadcast_to(den, (ns, W)).T
    map_out[...] = (num / den).astype(BF16)
    for cp in n_copies.values():
        cp.wait_send()


def write_out(f, g, mapped, f_out, g_out, map_out, sem):
    copies = [
        pltpu.make_async_copy(a, b, sem.at[i]) for i, (a, b) in enumerate(((mapped, map_out), (g, g_out), (f, f_out)))]
    for cp in copies:
        cp.start()
    for cp in copies:
        cp.wait()


def local(dims, source, target, potential):
    X, Y, Z, C, ns, nt, D, all_s, all_t = dims
    G = Y * C
    Q = nt // W
    vm = pltpu.VMEM
    dma = pltpu.SemaphoreType.DMA
    f, g, mapped = pl.pallas_call(
        functools.partial(kernel, dims),
        out_shape=(
            jax.ShapeDtypeStruct((1, ns), F32),
            jax.ShapeDtypeStruct((1, nt), F32),
            jax.ShapeDtypeStruct((ns, D), BF16),
        ),
        in_specs=[pl.BlockSpec(memory_space=pl.ANY)] * 3,
        out_specs=(pl.BlockSpec(memory_space=pltpu.VMEM),) * 3,
        scratch_shapes=[
            vm((Z, nt, D), BF16),
            vm((Z, EXTRA, W), BF16),
            vm((G, ns, D), BF16),
            vm((1, nt), F32),
            vm((Z * nt, 2 * D), BF16),
            vm((G * ns, Z * nt), F32),
            vm((G * ns, W), F32),
            vm((G * ns, 2 * W), F32),
            vm((G * ns, 2 * W), F32),
            vm((8, 2 * W), F32),
            vm((8, 2 * W), F32),
            vm((G * ns, 128), F32),
            vm((G * ns, 128), F32),
            vm((G, G, ns), F32),
            vm((8, ns), F32),
            vm((Z, 8, W), F32),
            vm((Z, 8, W), F32),
            vm((Q, Z, W), F32),
            vm((Q, Z, W), F32),
            vm((Q * (X - 1), Z, W), F32),
            vm((Q, Z, W), F32),
            vm((Q * (Z - 1), Z, W), F32),
            vm((Q, 16, Z * W), BF16),
            vm((G * ns, Z * nt), BF16),
            vm((G * ns, 2 * D), F32),
            vm((G * ns, Z * W), BF16),
            vm((G - 1, ns + 16, D), BF16),
            vm((G - 1, ns + 16, D), BF16),
            dma((Q + 2,)),
            dma((Z - 1,)), dma((Z - 1,)),
            dma((Z * Q,)), dma((Z * Q,)),
            dma((G - 1,)), dma((G - 1,)),
            dma((G - 1,)), dma((G - 1,)),
            dma((Q * (X - 1),)), dma((Q * (X - 1),)),
            dma((Q * (Z - 1),)), dma((Q * (Z - 1),)),
            dma((G - 1,)), dma((G - 1,)),
        ],
        compiler_params=pltpu.CompilerParams(
            collective_id=0, has_side_effects=True, vmem_limit_bytes=VMEM),
        cost_estimate=pl.CostEstimate(flops=6 * 10**9, bytes_accessed=10**6, transcendentals=10**7),
    )(*[pltpu.with_memory_space_constraint(a, pltpu.HBM) for a in (source, target, potential.reshape(1, nt))])
    f, g, mapped = pl.pallas_call(
        write_out,
        out_shape=(
            jax.ShapeDtypeStruct((1, ns), F32),
            jax.ShapeDtypeStruct((1, nt), F32),
            jax.ShapeDtypeStruct((ns, D), BF16),
        ),
        in_specs=[pl.BlockSpec(memory_space=pltpu.VMEM)] * 3,
        out_specs=(pl.BlockSpec(memory_space=pl.ANY),) * 3,
        scratch_shapes=[dma((3,))],
        compiler_params=pltpu.CompilerParams(vmem_limit_bytes=1024 * 1024),
    )(f, g, mapped)
    return f.reshape(ns), g.reshape(nt), mapped


def solution(mesh, shape=(Y, Z, C)):
    placed = (P(("row", "col"), None), P("col", None), P("col"))

    def whole(source, target, potential):
        rows, cols = mesh.shape["row"], mesh.shape["col"]
        dims = (rows, *shape, source.shape[0] // (rows * cols), target.shape[0] // cols, source.shape[1],
                source.shape[0], target.shape[0])
        return jax.shard_map(
            functools.partial(local, dims),
            mesh=mesh,
            in_specs=placed,
            out_specs=(P(("row", "col")), P("col"), P(("row", "col"), None)),
            check_vma=False,
        )(source, target, potential)

    return whole
```
